128 devices in a mesh: row: 8 (over x, core), col: 16 (over z, y).
Axes of the slice: x: 4, y: 4, z: 4, core: 2. Of those that a mesh axis runs over, the one named last changes fastest.
Arguments:
- depth_tiles: bfloat16 [8, 8192, 1024], P('row', 'col'), may hold values from -6 to 6
- conf_tiles: bfloat16 [8, 8192, 1024], P('row', 'col'), may hold values from 0.19921875 to 2
- tile_owner: int32 [8, 8192], P('row', 'col'), may hold values from 0 to 15, as said below
- tile_offset: int32 [8, 8192], P('row', 'col'), may hold values from 0 to 511
- tile_count: int32 [8, 16], P('row', 'col'), may hold values from 320 to 512, as said below
- prior: float32 [4096, 16384], P('row', 'col'), may hold values from -6 to 6
- edge_rows: float32 [4096, 16384], P('row', 'col'), may hold values from 0.25 to 4
- edge_cols: float32 [4096, 16384], P('row', 'col'), may hold values from 0.25 to 4
Outputs:
- height: float32 [4096, 16384], P('row', 'col')
- residual: float32 [4096, 16384], P('row', 'col')
The draws below stay inside these ranges and needn't reach their ends.
Inputs may be any that keep to these rules, and one draw needn't show every extreme that they name: `tile_owner`: the 512 tiles of a keyframe come in 8 consecutive runs of 64; each run goes to one owner, the runs of a keyframe to distinct owners; the first run of every keyframe of one grid row block goes to the same owner. The live tiles of a keyframe are its first tile_count tiles.
All inputs are finite; a program needn't handle non-finite values.
Results may differ from the reference program's by a relative error of at most 0.0003.
Values may be sent and summed in bfloat16 or wider, within the bound.
No kernel may reach another device: no remote copies, remote signals or barrier semaphores. Data moves between devices by JAX's collectives and lax.ppermute only.
A program may use at most 128 MiB of HBM per device.

```python
import math
import jax
import jax.numpy as jnp

CR = 512
CC = 1024
TS = 32
TILE = 1024
TPB = 512
K = 512
GROUPS = 8
ITERS = 2
NR = 4096
NC = 16384
N_ROW = 8
N_COL = 16


def draw_tile_owner(key, part):
    key = jax.random.fold_in(key, 7)
    first_key, second_key, third_key = jax.random.split(key, 3)
    favored = jax.random.randint(first_key, (N_ROW, 1, 1), 0, N_COL)
    liking = jax.random.randint(second_key, (N_ROW, 1, N_COL), 0, 4)
    jitter = jax.random.randint(third_key, (N_ROW, N_COL, N_COL), 0, 1024)
    candidate = jnp.arange(N_COL, dtype=jnp.int32)[None, None, :]
    scores = (liking * 1024 + jitter) * N_COL + candidate
    scores = scores + jnp.where(candidate == favored, 1 << 24, 0)
    ranking = jnp.argsort(-scores, axis=-1, stable=True)
    chosen = ranking[:, :, :GROUPS]
    owners = jnp.repeat(chosen, K // GROUPS, axis=-1)
    return owners.reshape(N_ROW, N_COL * K).astype(jnp.int32)


def draw_tile_count(key, part):
    key = jax.random.fold_in(key, 5)
    first_key, second_key, third_key = jax.random.split(key, 3)
    counts = jax.random.randint(first_key, (N_ROW * N_COL,), 5 * K // 8, K + 1)
    fullest = jax.random.randint(second_key, (), 0, N_ROW * N_COL)
    fewest = jax.random.randint(third_key, (), 0, N_ROW * N_COL - 1)
    fewest = jnp.where(fewest >= fullest, fewest + 1, fewest)
    places = jnp.arange(N_ROW * N_COL, dtype=jnp.int32)
    counts = jnp.where(places == fullest, K, jnp.where(places == fewest, 5 * K // 8, counts))
    return counts.reshape(N_ROW, N_COL).astype(jnp.int32)


def set_ends(array, own_key, low, high):
    index_at = [jax.random.randint(jax.random.fold_in(own_key, axis), (), 0, length) for axis, length in enumerate(array.shape)]
    widest = array.shape.index(max(array.shape))
    beside = index_at[:widest] + [(index_at[widest] + 1) % array.shape[widest]] + index_at[widest + 1:]
    return array.at[tuple(index_at)].set(low).at[tuple(beside)].set(high)


def block_scale(own_key, extent, cuts, low, top_value):
    gain = 1.0
    for axis_at, blocks in cuts:
        heights = jax.random.uniform(jax.random.fold_in(jax.random.fold_in(own_key, 6), axis_at), (blocks,), jnp.float32, low / len(cuts), top_value / len(cuts))
        gain = gain * jnp.repeat(jnp.exp(heights), extent[axis_at] // blocks).reshape((-1,) + (1,) * (len(extent) - 1 - axis_at))
    return gain


def noise(own_key, dims, scale, bound, pieces=(), kind=jnp.bfloat16):
    loudness = block_scale(own_key, dims, pieces, -0.22, 0.18) if pieces else 1.0
    result = jax.random.normal(own_key, dims, jnp.float32) * scale * loudness
    return jnp.minimum(jnp.maximum(result, -bound), bound).astype(kind)


def setup_inputs(seed: int = 0) -> dict:
    key_list = jax.random.split(jax.random.key(seed), 9)
    return {
        "depth_tiles": noise(key_list[0], (N_ROW, N_COL * K, TILE), 1.0, 6.0, ((0, 8), (1, 16))),
        "conf_tiles": jnp.clip(jnp.exp(math.log(2.0) - 2.306499 * jax.random.uniform(key_list[1], (N_ROW, N_COL * K, TILE), jnp.float32) ** block_scale(key_list[1], (N_ROW, N_COL * K, TILE), ((0, 8), (1, 16)), -0.2, 0.2)), 0.19921875, 2.0).astype(jnp.bfloat16),
        "tile_owner": draw_tile_owner(jax.random.fold_in(key_list[8], 71), 0),
        "tile_offset": set_ends(jax.random.randint(key_list[3], (N_ROW, N_COL * K), 0, TPB), jax.random.fold_in(key_list[3], 1), 0, TPB - 1).astype(jnp.int32),
        "tile_count": draw_tile_count(jax.random.fold_in(key_list[8], 71), 0),
        "prior": noise(key_list[5], (NR, NC), 1.0, 6.0, ((0, 8), (1, 16)), jnp.float32),
        "edge_rows": jnp.clip(jnp.exp(math.log(4.0) - 2.7725887 * jax.random.uniform(key_list[6], (NR, NC), jnp.float32) ** block_scale(key_list[6], (NR, NC), ((0, 8), (1, 16)), -0.2, 0.2)), 0.25, 4.0),
        "edge_cols": jnp.clip(jnp.exp(math.log(4.0) - 2.7725887 * jax.random.uniform(key_list[7], (NR, NC), jnp.float32) ** block_scale(key_list[7], (NR, NC), ((0, 8), (1, 16)), -0.2, 0.2)), 0.25, 4.0),
    }


LAM = 0.05
HUBER = 0.5


def make_operator(weight_sum, edge_rows, edge_cols):
    total_rows, total_cols = edge_rows.shape
    row_ids = jnp.arange(total_rows, dtype=jnp.int32)[:, None]
    col_ids = jnp.arange(total_cols, dtype=jnp.int32)[None, :]
    row_edge = jnp.where(row_ids == total_rows - 1, jnp.float32(0.0), edge_rows)
    col_edge = jnp.where(col_ids == total_cols - 1, jnp.float32(0.0), edge_cols)
    row_above = jnp.pad(row_edge, ((1, 0), (0, 0)))[:-1]
    col_before = jnp.pad(col_edge, ((0, 0), (1, 0)))[:, :-1]
    diagonal = weight_sum + LAM + row_edge + row_above + col_edge + col_before

    def operate(field):
        padded = jnp.pad(field, 1)
        return (diagonal * field - row_edge * padded[2:, 1:-1] - row_above * padded[:-2, 1:-1]
                - col_edge * padded[1:-1, 2:] - col_before * padded[1:-1, :-2])

    return operate


def reference(depth_tiles, conf_tiles, tile_owner, tile_offset, tile_count, prior, edge_rows, edge_cols):
    prior_tiles = prior.reshape(N_ROW, CR // TS, TS, N_COL, CC // TS, TS)
    prior_tiles = prior_tiles.transpose(0, 3, 1, 4, 2, 5).reshape(N_ROW, N_COL * TPB, TILE)
    landing = (tile_owner * TPB + tile_offset).astype(jnp.int32)
    prior_at = jax.vmap(lambda tiles, keys: tiles[keys])(prior_tiles, landing)
    depths = depth_tiles.astype(jnp.float32)
    weights = conf_tiles.astype(jnp.float32) * HUBER / jnp.maximum(jnp.abs(depths - prior_at), HUBER)
    within = (jnp.arange(N_COL * K, dtype=jnp.int32) % K)[None, :]
    is_live = within < jnp.repeat(tile_count, K, axis=1)
    weights = jnp.where(is_live[:, :, None], weights, jnp.float32(0.0))
    row_base = (jnp.arange(N_ROW, dtype=jnp.int32) * (N_COL * TPB))[:, None]
    segment = (row_base + landing).reshape(-1)
    stacked = jnp.concatenate([weights, weights * depths], axis=-1).reshape(-1, 2 * TILE)
    sums = jax.ops.segment_sum(stacked, segment, num_segments=N_ROW * N_COL * TPB)
    sums = sums.reshape(N_ROW, N_COL, CR // TS, CC // TS, 2, TS, TS)
    sums = sums.transpose(4, 0, 2, 5, 1, 3, 6).reshape(2, NR, NC)
    weight_sum, data_sum = sums[0], sums[1]
    operate = make_operator(weight_sum, edge_rows, edge_cols)
    right_side = data_sum + LAM * prior
    height = prior
    residual = right_side - operate(prior)
    direction = residual
    norm_now = jnp.sum(residual * residual)
    for iteration in range(ITERS):
        image = operate(direction)
        alpha = norm_now / jnp.sum(direction * image)
        height = height + alpha * direction
        residual = residual - alpha * image
        norm_next = jnp.sum(residual * residual)
        direction = residual + (norm_next / norm_now) * direction
        norm_now = norm_next
    return height, residual
```

```python
import functools

import jax
import jax.numpy as jnp
from jax import lax
from jax.experimental import pallas as pl
from jax.experimental.pallas import tpu as pltpu
from jax.sharding import PartitionSpec as P

TS = 32
GROUPS = 8
LAM = 0.05
HUBER = 0.5
META = 16
LANES = 128
F32 = jnp.float32
VMEM_LIMIT = 56 * 1024 * 1024


def lane_ids(shape):
    return lax.broadcasted_iota(jnp.int32, shape, len(shape) - 1)


def row_ids(shape):
    return lax.broadcasted_iota(jnp.int32, shape, len(shape) - 2)


def rows_up(block, below):
    count = block.shape[0]
    return jnp.where(row_ids(block.shape) == count - 1, below, pltpu.roll(block, count - 1, axis=0))


def rows_down(block, above):
    return jnp.where(row_ids(block.shape) == 0, above, pltpu.roll(block, 1, axis=0))


def cols_up(block, after):
    count = block.shape[1]
    rolled = pltpu.roll(block, count - 1, axis=1)
    tail = rolled[:, count - LANES :]
    tail = jnp.where(lane_ids(tail.shape) == LANES - 1, after, tail)
    if count == LANES:
        return tail
    return jnp.concatenate([rolled[:, : count - LANES], tail], axis=1)


def cols_down(block, before):
    rolled = pltpu.roll(block, 1, axis=1)
    head = rolled[:, :LANES]
    head = jnp.where(lane_ids(head.shape) == 0, before, head)
    if block.shape[1] == LANES:
        return head
    return jnp.concatenate([head, rolled[:, LANES:]], axis=1)


def swap_blocks(four):
    lane = lane_ids((8, LANES))
    low_half = lane < 64
    even = (lane & 32) == 0
    half = [None] * 4
    for q in range(2):
        a, b = four[q], four[q + 2]
        half[q] = jnp.where(low_half, a, pltpu.roll(b, 64, axis=1))
        half[q + 2] = jnp.where(low_half, pltpu.roll(a, 64, axis=1), b)
    out = [None] * 4
    for q in (0, 2):
        a, b = half[q], half[q + 1]
        out[q] = jnp.where(even, a, pltpu.roll(b, 32, axis=1))
        out[q + 1] = jnp.where(even, pltpu.roll(a, 96, axis=1), b)
    return out


def pack_kernel(
    owner_ref, count_ref, offset_ref, depth_hbm, conf_hbm, out_hbm,
    depth, conf, packed, blank, scratch, in_sems, blank_sems, out_sems,
):
    slots = out_hbm.shape[0]
    run = depth.shape[0] // GROUPS
    chunks = depth.shape[1] // LANES
    cells = run * chunks
    loads = []
    for g in range(GROUPS):
        part = pl.ds(g * run, run)
        for which, (source, target) in enumerate(((depth_hbm, depth), (conf_hbm, conf))):
            copy = pltpu.make_async_copy(source.at[part], target.at[part], in_sems.at[which, g])
            copy.start()
            loads.append(copy)
    blank[...] = jnp.zeros_like(blank)
    marks = []
    for s in range(slots):
        copy = pltpu.make_async_copy(
            blank, out_hbm.at[s, pl.ds(2 * cells, META)], blank_sems.at[s]
        )
        copy.start()
        marks.append(copy)
    rows = row_ids((META, LANES))
    count = count_ref[0, 0]
    for pair in range(GROUPS // 2):
        offsets = jnp.broadcast_to(offset_ref[:, pair * LANES : (pair + 1) * LANES], (META, LANES))
        high = (offsets >> 4).astype(F32)
        low = (offsets & 15).astype(F32)
        for side in range(2):
            g = 2 * pair + side
            if side:
                high, low = pltpu.roll(high, run, axis=1), pltpu.roll(low, run, axis=1)
            live = jnp.clip(count - g * run, 0, run).astype(F32)
            meta = jnp.where(rows == 0, high, jnp.where(rows == 1, low, jnp.where(rows == 2, live, 0.0)))
            packed[g, 2 * cells :, :] = meta.astype(jnp.bfloat16)
    for copy in marks:
        copy.wait()
    stores = []
    for g in range(GROUPS):
        for which, source in enumerate((depth, conf)):
            loads[2 * g + which].wait()
            for m in range(run // 16):
                buffer = scratch.at[(which * 4 + m) % scratch.shape[0]]
                block = source[g * run + 16 * m : g * run + 16 * m + 16, :].astype(F32)
                for c in range(chunks):
                    buffer[pl.ds(c, 16, stride=chunks), :] = block[:, c * LANES : (c + 1) * LANES]
                first = which * cells + m * 16 * chunks
                packed[g, first : first + 16 * chunks, :] = buffer[...].astype(jnp.bfloat16)
        copy = pltpu.make_async_copy(packed.at[g], out_hbm.at[owner_ref[0, g * run]], out_sems.at[g])
        copy.start()
        stores.append(copy)
    for copy in stores:
        copy.wait()


def pack(owners, offsets, count, depth, conf, slots):
    tiles, cells = depth.shape
    run = tiles // GROUPS
    rows = 2 * run * (cells // LANES) + META
    return pl.pallas_call(
        pack_kernel,
        out_shape=jax.ShapeDtypeStruct((slots, rows, LANES), jnp.bfloat16),
        in_specs=[
            pl.BlockSpec(memory_space=pltpu.SMEM),
            pl.BlockSpec(memory_space=pltpu.SMEM),
            pl.BlockSpec(memory_space=pltpu.VMEM),
            pl.BlockSpec(memory_space=pl.ANY),
            pl.BlockSpec(memory_space=pl.ANY),
        ],
        out_specs=pl.BlockSpec(memory_space=pl.ANY),
        scratch_shapes=[
            pltpu.VMEM((tiles, cells), jnp.bfloat16),
            pltpu.VMEM((tiles, cells), jnp.bfloat16),
            pltpu.VMEM((GROUPS, rows, LANES), jnp.bfloat16),
            pltpu.VMEM((META, LANES), jnp.bfloat16),
            pltpu.VMEM((8, 16 * (cells // LANES), LANES), F32),
            pltpu.SemaphoreType.DMA((2, GROUPS)),
            pltpu.SemaphoreType.DMA((slots,)),
            pltpu.SemaphoreType.DMA((GROUPS,)),
        ],
        compiler_params=pltpu.CompilerParams(vmem_limit_bytes=16 * 1024 * 1024),
        cost_estimate=pl.CostEstimate(flops=1 << 20, bytes_accessed=4 << 20, transcendentals=0),
        name="pack",
    )(owners, count, offsets, depth, conf)


def strips_kernel(top, bottom, kx_bottom, left, right, ky_right, up_out, down_out, left_out, right_out):
    up_out[...] = top[0:1, :]
    down_out[0:1, :] = bottom[7:8, :]
    down_out[1:2, :] = kx_bottom[7:8, :]
    lane = lane_ids(left.shape)
    left_out[...] = left[...].T[0:1, :]
    both = jnp.where(lane == LANES - 1, right[...], pltpu.roll(ky_right[...], LANES - 1, axis=1))
    turned = both.T
    right_out[0:1, :] = turned[LANES - 1 : LANES, :]
    right_out[1:2, :] = turned[LANES - 2 : LANES - 1, :]


def strips(prior, kx, ky):
    rows, cols = prior.shape
    last_rows = pl.BlockSpec((8, cols), lambda i: (rows // 8 - 1, 0))
    last_cols = pl.BlockSpec((rows, LANES), lambda i: (0, cols // LANES - 1))
    whole = lambda shape: pl.BlockSpec(shape, lambda i: (0, 0))
    shapes = ((1, cols), (2, cols), (1, rows), (2, rows))
    return pl.pallas_call(
        strips_kernel,
        grid=(1,),
        out_shape=[jax.ShapeDtypeStruct(s, F32) for s in shapes],
        in_specs=[
            whole((8, cols)), last_rows, last_rows, whole((rows, LANES)), last_cols, last_cols,
        ],
        out_specs=[whole(s) for s in shapes],
        name="strips",
    )(prior, prior, kx, prior, prior, ky)


def column_block(row):
    return jnp.broadcast_to(row, (LANES, row.shape[1])).T


def prepare_kernel(
    flags, prior, kx, ky, from_up, from_down, from_left, from_right,
    flow_out, diag_out, tiles_out, left_p, left_k, right_p, staging,
):
    rows, cols = prior.shape
    steps = rows // 8
    is_last_row, is_last_col = flags[0, 0] == 1, flags[0, 1] == 1
    left_p[...] = column_block(from_left[0:1, :])
    left_k[...] = column_block(from_left[1:2, :])
    own_edge = prior[:, cols - LANES :]
    own_edge = jnp.broadcast_to(own_edge[:, LANES - 1 :], (rows, LANES))
    right_p[...] = jnp.where(is_last_col, own_edge, column_block(from_right[0:1, :]))
    keep_col = jnp.where(is_last_col & (lane_ids((8, cols)) == cols - 1), 0.0, 1.0)

    def step(i, carry):
        above_flow, above_k = carry
        part = pl.ds(pl.multiple_of(i * 8, 8), 8)
        p, k, h = prior[part, :], kx[part, :], ky[part, :]
        following = prior[pl.ds(jnp.minimum(i * 8 + 8, rows - 1), 1), :]
        edge = jnp.where(is_last_row, prior[rows - 1 : rows, :], from_down[...])
        below = jnp.where(i == steps - 1, edge, following)
        down_flow = k * (rows_up(p, below) - p)
        right_flow = h * (cols_up(p, right_p[part, :]) - p)
        first_flow = left_k[part, :] * (p[:, :LANES] - left_p[part, :])
        first_flow = jnp.broadcast_to(first_flow[:, 0:1], (8, LANES))
        flow_out[part, :] = (
            (down_flow - rows_down(down_flow, above_flow))
            + (right_flow - cols_down(right_flow, first_flow))
        )
        last = (row_ids(k.shape) == 7) & (i == steps - 1) & is_last_row
        k = jnp.where(last, 0.0, k)
        h = h * keep_col
        diag_out[part, :] = (
            LAM + (k + rows_down(k, above_k)) + (h + cols_down(h, left_k[part, :]))
        )
        return down_flow[7:8, :], k[7:8, :]

    first = from_up[1:2, :]
    lax.fori_loop(0, steps, step, (first * (prior[0:1, :] - from_up[0:1, :]), first))

    def to_tiles(strip, carry):
        base = pl.multiple_of(strip * TS, TS)
        for b in range(cols // LANES):
            buffer = staging.at[b]
            buffer[...] = prior[pl.ds(base, TS), b * LANES : (b + 1) * LANES]
            four = swap_blocks([buffer[pl.ds(a, 8, stride=4), :] for a in range(4)])
            first_tile = strip * (cols // TS) + 4 * b
            for q in range(4):
                tiles_out[pl.ds(pl.multiple_of((first_tile + q) * 8, 8), 8), :] = four[q]
        return carry

    lax.fori_loop(0, rows // TS, to_tiles, 0)


def prepare(flags, prior, kx, ky, from_up, from_down, from_left, from_right):
    rows, cols = prior.shape
    vmem = pl.BlockSpec(memory_space=pltpu.VMEM)
    cells = rows * cols
    return pl.pallas_call(
        prepare_kernel,
        out_shape=[
            jax.ShapeDtypeStruct((rows, cols), F32),
            jax.ShapeDtypeStruct((rows, cols), F32),
            jax.ShapeDtypeStruct((cells // LANES, LANES), F32),
        ],
        in_specs=[pl.BlockSpec(memory_space=pltpu.SMEM)] + [vmem] * 7,
        out_specs=[vmem] * 3,
        scratch_shapes=[pltpu.VMEM((rows, LANES), F32)] * 3
        + [pltpu.VMEM((cols // LANES, TS, LANES), F32)],
        compiler_params=pltpu.CompilerParams(vmem_limit_bytes=24 * 1024 * 1024),
        cost_estimate=pl.CostEstimate(flops=20 * cells, bytes_accessed=24 * cells, transcendentals=0),
        name="prepare",
    )(flags, prior, kx, ky, from_up, from_down, from_left, from_right)


BANKS = 4
BATCH = 16


def join_kernel(
    got_hbm, prior_hbm, flow_hbm, diag_hbm, kx_top, ky_top, kx_bottom, ky_bottom,
    kx_left, ky_left, kx_right, ky_right,
    r_out, diag_out, up_out, down_out, left_out, right_out,
    got, prior, flow, diag, meta, table_v, table, staging, *rest,
):
    weights, pulls = rest[:BANKS], rest[BANKS : 2 * BANKS]
    got_sems, sems = rest[2 * BANKS], rest[2 * BANKS + 1]
    slots, rows_in = got_hbm.shape[0], got_hbm.shape[1]
    cells = (rows_in - META) // 2
    run = cells // 8
    rows, cols = r_out.shape
    meta_copy = pltpu.make_async_copy(
        got_hbm.at[:, pl.ds(2 * cells, META)], meta, sems.at[0]
    )
    meta_copy.start()
    prior_copy = pltpu.make_async_copy(prior_hbm, prior, sems.at[1])
    prior_copy.start()
    copies = []
    for s in range(slots):
        copy = pltpu.make_async_copy(
            got_hbm.at[s, pl.ds(0, 2 * cells)], got.at[s], got_sems.at[s]
        )
        copy.start()
        copies.append(copy)
    flow_copy = pltpu.make_async_copy(flow_hbm, flow, sems.at[2])
    flow_copy.start()
    diag_copy = pltpu.make_async_copy(diag_hbm, diag, sems.at[3])
    diag_copy.start()

    zero = jnp.zeros((TS, LANES), F32)

    def clear(i, carry):
        part = pl.ds(pl.multiple_of(i * TS, TS), TS)
        for bank in weights + pulls:
            bank[part, :] = zero
        return carry

    lax.fori_loop(0, rows * cols // LANES // TS, clear, 0)
    meta_copy.wait()
    for s in range(slots):
        fields = meta[s].astype(F32)
        target = fields[0:1, :] * 16.0 + fields[1:2, :]
        table_v[s, 0:1, :] = target.astype(jnp.int32)
        table_v[s, 1:2, :] = fields[2:3, :].astype(jnp.int32)
    table_copy = pltpu.make_async_copy(table_v, table, sems.at[4])
    table_copy.start()
    table_copy.wait()
    prior_copy.wait()

    for s in range(slots):
        copies[s].wait()
        live = table[s, 1, 0]

        def batch(step, carry, s=s, live=live):
            first = step * BATCH
            places, terms = [], []
            for pair in range(BATCH // 2):
                at = pl.multiple_of((first + 2 * pair) * 8, 16)
                depths = got[s, pl.ds(at, 16), :].astype(F32)
                confs = got[s, pl.ds(cells + at, 16), :].astype(F32) * HUBER
                for side in range(2):
                    tile = first + 2 * pair + side
                    place = pl.ds(pl.multiple_of(table[s, 0, tile] * 8, 8), 8)
                    error = depths[8 * side : 8 * side + 8] - prior[place, :]
                    weight = confs[8 * side : 8 * side + 8] / jnp.maximum(jnp.abs(error), HUBER)
                    weight = jnp.where(tile < live, weight, 0.0)
                    places.append(place)
                    terms.append((weight, weight * error))
            for k, (place, (weight, pull)) in enumerate(zip(places, terms)):
                weights[k % BANKS][place, :] += weight
                pulls[k % BANKS][place, :] += pull
            return carry

        lax.fori_loop(0, (live + BATCH - 1) // BATCH, batch, 0)

    flow_copy.wait()
    diag_copy.wait()

    def to_grid(strip, carry):
        base = pl.multiple_of(strip * TS, TS)
        for b in range(cols // LANES):
            place = pl.ds(pl.multiple_of((strip * (cols // TS) + 4 * b) * 8, TS), TS)
            lanes = slice(b * LANES, (b + 1) * LANES)
            for n, (banks, base_ref, out) in enumerate(
                ((weights, diag, diag_out), (pulls, flow, r_out))
            ):
                total = (banks[0][place, :] + banks[1][place, :]) + (
                    banks[2][place, :] + banks[3][place, :]
                )
                four = swap_blocks([total[8 * q : 8 * q + 8] for q in range(4)])
                buffer = staging.at[2 * b + n]
                for a in range(4):
                    buffer[pl.ds(a, 8, stride=4), :] = four[a]
                out[pl.ds(base, TS), lanes] = buffer[...] + base_ref[pl.ds(base, TS), lanes]
        return carry

    lax.fori_loop(0, rows // TS, to_grid, 0)

    zero_row = jnp.zeros((1, cols), F32)
    zero_cols = jnp.zeros((8, LANES), F32)

    def across(field, k):
        flow = k * field
        return k * cols_up(field, zero_cols) + cols_down(flow, zero_cols)

    top = r_out[0:8, :]
    image = diag_out[0:8, :] * top - kx_top[...] * rows_up(top, zero_row) - across(top, ky_top[...])
    up_out[0:1, :] = top[0:1, :]
    up_out[1:2, :] = image[0:1, :]
    low = r_out[rows - 8 : rows, :]
    image = (
        diag_out[rows - 8 : rows, :] * low
        - rows_down(kx_bottom[...] * low, zero_row)
        - across(low, ky_bottom[...])
    )
    down_out[0:1, :] = low[7:8, :]
    down_out[1:2, :] = image[7:8, :]
    zero_lane = jnp.zeros((1, LANES), F32)

    def along(field, d, k):
        return d * field - k * rows_up(field, zero_lane) - rows_down(k * field, zero_lane)

    lane = lane_ids((rows, LANES))
    side = r_out[:, 0:LANES]
    image = along(side, diag_out[:, 0:LANES], kx_left[...])
    image = image - ky_left[...] * pltpu.roll(side, LANES - 1, axis=1)
    turned = jnp.where(lane == 0, side, pltpu.roll(image, 1, axis=1)).T
    left_out[...] = turned[0:2, :]
    side = r_out[:, cols - LANES :]
    image = along(side, diag_out[:, cols - LANES :], kx_right[...])
    image = image - pltpu.roll(ky_right[...] * side, 1, axis=1)
    turned = jnp.where(lane == LANES - 1, side, pltpu.roll(image, LANES - 1, axis=1)).T
    right_out[0:1, :] = turned[LANES - 1 : LANES, :]
    right_out[1:2, :] = turned[LANES - 2 : LANES - 1, :]


def join(got, prior_tiles, flow, diag, kx, ky):
    rows, cols = flow.shape
    cells = rows * cols
    slots, rows_in, _ = got.shape
    whole = lambda shape: pl.BlockSpec(shape, lambda i: (0, 0))
    top, bottom = whole((8, cols)), pl.BlockSpec((8, cols), lambda i: (rows // 8 - 1, 0))
    left, right = whole((rows, LANES)), pl.BlockSpec((rows, LANES), lambda i: (0, cols // LANES - 1))
    shapes = ((rows, cols), (rows, cols), (2, cols), (2, cols), (2, rows), (2, rows))
    return pl.pallas_call(
        join_kernel,
        grid=(1,),
        out_shape=[jax.ShapeDtypeStruct(s, F32) for s in shapes],
        in_specs=[pl.BlockSpec(memory_space=pl.ANY)] * 4
        + [top, top, bottom, bottom, left, left, right, right],
        out_specs=[whole(s) for s in shapes],
        scratch_shapes=[
            pltpu.VMEM((slots, rows_in - META, LANES), jnp.bfloat16),
            pltpu.VMEM((cells // LANES, LANES), F32),
            pltpu.VMEM((rows, cols), F32),
            pltpu.VMEM((rows, cols), F32),
            pltpu.VMEM((slots, META, LANES), jnp.bfloat16),
            pltpu.VMEM((slots, 8, LANES), jnp.int32),
            pltpu.SMEM((slots, 8, LANES), jnp.int32),
            pltpu.VMEM((2 * cols // LANES, TS, LANES), F32),
        ]
        + [pltpu.VMEM((cells // LANES, LANES), F32)] * (2 * BANKS)
        + [pltpu.SemaphoreType.DMA((slots,)), pltpu.SemaphoreType.DMA((5,))],
        compiler_params=pltpu.CompilerParams(vmem_limit_bytes=VMEM_LIMIT),
        cost_estimate=pl.CostEstimate(flops=30 * cells, bytes_accessed=24 * cells, transcendentals=0),
        name="join",
    )(got, prior_tiles, flow, diag, kx, ky, kx, ky, kx, ky, kx, ky)


def add_pair(total, other):
    (a, rest_a), (b, rest_b) = total, other
    s = a + b
    back = s - a
    error = (a - (s - back)) + (b - back)
    return s, rest_a + rest_b + error


def fold(pair, axis):
    size = pair[0].shape[axis] // 2
    while size:
        other = tuple(pltpu.roll(part, size, axis=axis) for part in pair)
        pair = add_pair(pair, other)
        size //= 2
    return pair


def moments_kernel(
    flags, r_ref, diag_ref, kx_ref, ky_ref, r_up, r_down, r_left, r_right, k_up, k_left,
    q_out, s_out, table_out, left_r, left_k, left_q, right_r, right_q,
):
    rows, cols = r_ref.shape
    steps = rows // 8
    keep_row = jnp.where(flags[0, 0] == 1, 0.0, 1.0).astype(F32)
    keep_col = jnp.where(flags[0, 1] == 1, 0.0, 1.0).astype(F32)
    up_k = k_up[1:2, :]
    left_r[...] = column_block(r_left[0:1, :])
    left_k[...] = column_block(k_left[1:2, :])
    right_r[...] = column_block(r_right[0:1, :])
    edge_r = jnp.broadcast_to(r_ref[:, 0:1], (rows, LANES))
    left_q[...] = column_block(r_left[1:2, :]) - left_k[...] * edge_r
    own_flow = ky_ref[:, cols - LANES :] * r_ref[:, cols - LANES :]
    own_flow = jnp.broadcast_to(own_flow[:, LANES - 1 :], (rows, LANES))
    right_q[...] = (column_block(r_right[1:2, :]) - own_flow) * keep_col
    up_q = r_up[1:2, :] - up_k * r_ref[0:1, :]
    down_q = (r_down[1:2, :] - kx_ref[rows - 1 : rows, :] * r_ref[rows - 1 : rows, :]) * keep_row

    def operate(source, i, part, above_flow, below_edge, before, after):
        field = source[part, :]
        following = source[pl.ds(jnp.minimum(i * 8 + 8, rows - 1), 1), :]
        below = jnp.where(i == steps - 1, below_edge, following)
        k, h = kx_ref[part, :], ky_ref[part, :]
        row_flow = k * field
        col_flow = h * field
        entering = (left_k[part, :] * before[part, :])
        image = (
            diag_ref[part, :] * field
            - k * rows_up(field, below)
            - rows_down(row_flow, above_flow)
            - h * cols_up(field, after[part, :])
            - cols_down(col_flow, entering)
        )
        return field, image, row_flow[7:8, :]

    def folded(values):
        parts = [values[:, b * LANES : (b + 1) * LANES] for b in range(cols // LANES)]
        while len(parts) > 1:
            parts = [a + b for a, b in zip(parts[::2], parts[1::2])]
        return parts[0]

    def first(i, carry):
        above, m0, m1, m2 = carry
        part = pl.ds(pl.multiple_of(i * 8, 8), 8)
        field, image, above = operate(r_ref, i, part, above, r_down[0:1, :], left_r, right_r)
        q_out[part, :] = image
        return (
            above,
            m0 + folded(field * field),
            m1 + folded(field * image),
            m2 + folded(image * image),
        )

    zero = jnp.zeros((8, LANES), F32)
    _, m0, m1, m2 = lax.fori_loop(0, steps, first, (up_k * r_up[0:1, :], zero, zero, zero))

    def second(i, carry):
        above, m3 = carry
        part = pl.ds(pl.multiple_of(i * 8, 8), 8)
        field, image, above = operate(q_out, i, part, above, down_q, left_q, right_q)
        s_out[part, :] = image
        return above, m3 + folded(field * image)

    _, m3 = lax.fori_loop(0, steps, second, (up_k * up_q, zero))

    sums = []
    for m in (m0, m1, m2, m3):
        pair = fold((m, jnp.zeros_like(m)), 0)
        sums.append(fold(pair, 1))
    corners = ((0, 0), (0, cols - 1), (rows - 1, 0), (rows - 1, cols - 1))

    def cell(ref, i, j):
        block = ref[i // 8 * 8 : i // 8 * 8 + 8, j // LANES * LANES : j // LANES * LANES + LANES]
        return block[i % 8 : i % 8 + 1, j % LANES : j % LANES + 1]

    values = [value[0:1, 0:1] for value, _ in sums] + [rest[0:1, 0:1] for _, rest in sums]
    values += [cell(r_ref, i, j) for i, j in corners]
    values += [cell(q_out, i, j) for i, j in corners]
    values += [cell(kx_ref, i, j) * keep_row for i, j in corners[2:]]
    values += [cell(ky_ref, i, j) * keep_col for i, j in corners[1::2]]
    lane = lane_ids((1, LANES))
    row = jnp.zeros((1, LANES), F32)
    for place, value in enumerate(values):
        row = jnp.where(lane == place, jnp.broadcast_to(value, (1, LANES)), row)
    table_out[...] = jnp.broadcast_to(row, table_out.shape)


def moments(flags, r, diag, kx, ky, r_up, r_down, r_left, r_right, k_up, k_left, devices):
    rows, cols = r.shape
    vmem = pl.BlockSpec(memory_space=pltpu.VMEM)
    cells = rows * cols
    return pl.pallas_call(
        moments_kernel,
        out_shape=[
            jax.ShapeDtypeStruct((rows, cols), F32),
            jax.ShapeDtypeStruct((rows, cols), F32),
            jax.ShapeDtypeStruct((devices, LANES), F32),
        ],
        in_specs=[pl.BlockSpec(memory_space=pltpu.SMEM)] + [vmem] * 10,
        out_specs=[vmem] * 3,
        scratch_shapes=[pltpu.VMEM((rows, LANES), F32)] * 5,
        compiler_params=pltpu.CompilerParams(vmem_limit_bytes=24 * 1024 * 1024),
        cost_estimate=pl.CostEstimate(flops=40 * cells, bytes_accessed=24 * cells, transcendentals=0),
        name="moments",
    )(flags, r, diag, kx, ky, r_up, r_down, r_left, r_right, k_up, k_left)


def split(a):
    high = a * 4097.0
    high = high - (high - a)
    return high, a - high


def product(a, b):
    p = a * b
    a1, a2 = split(a)
    b1, b2 = split(b)
    return p, ((a1 * b1 - p) + a1 * b2 + a2 * b1) + a2 * b2


def quotient(top, bottom):
    q = top[0] / bottom[0]
    p, error = product(q, bottom[0])
    rest = ((top[0] - p) - error + top[1] - q * bottom[1]) / bottom[0]
    return q, rest


def finish_kernel(col_count, where_ref, table_ref, prior, r, q, s, height_out, residual_out, coeff):
    step = pl.program_id(0)
    steps = pl.num_programs(0)
    rows, cols = r.shape

    @pl.when(step == 0)
    def _():
        turned = table_ref[...].T
        devices = turned.shape[1]
        field = [turned[i : i + 1, :] for i in range(20)]

        def at(index, down, right):
            shift = -(down * col_count + right)
            return pltpu.roll(jnp.broadcast_to(field[index], (8, devices)), shift % devices, axis=1)

        r_tl, r_tr, r_bl, r_br = 8, 9, 10, 11
        kx_l, kx_r, ky_t, ky_b = 16, 17, 18, 19
        extra = [
            (at(kx_l, -1, 0) * at(ky_b, -1, -1) + at(ky_t, 0, -1) * at(kx_r, -1, -1)) * at(r_br, -1, -1),
            (at(kx_r, -1, 0) * at(ky_b, -1, 0) + at(ky_t, 0, 0) * at(kx_l, -1, 1)) * at(r_bl, -1, 1),
            (at(kx_l, 0, 0) * at(ky_t, 1, -1) + at(ky_b, 0, -1) * at(kx_r, 0, -1)) * at(r_tr, 1, -1),
            (at(kx_r, 0, 0) * at(ky_t, 1, 0) + at(ky_b, 0, 0) * at(kx_l, 0, 1)) * at(r_tl, 1, 1),
        ]
        pairs = [
            [jnp.broadcast_to(field[i], (8, devices)), jnp.broadcast_to(field[4 + i], (8, devices))]
            for i in range(4)
        ]
        for corner in range(4):
            pairs[3][1] = pairs[3][1] + extra[corner] * field[12 + corner]
        m = [fold(tuple(pair), 1) for pair in pairs]
        m = [tuple(part[0:1, 0:1] for part in pair) for pair in m]
        x1, x2, x3 = (quotient(m[i + 1], m[i]) for i in range(3))
        gap_1 = (x2[0] - x1[0]) + (x2[1] - x1[1])
        gap_2 = (x3[0] - x2[0]) + (x3[1] - x2[1])
        alpha = 1.0 / x1[0]
        ratio = 1.0 + gap_1 / x1[0]
        alpha_1 = gap_1 / (x2[0] * gap_2)
        mine = lane_ids((8, devices)) == where_ref[0, 2]
        values = [alpha + alpha_1 * ratio, alpha_1 * alpha]
        for corner in range(4):
            own = jnp.sum(jnp.where(mine, extra[corner], 0.0), axis=1, keepdims=True)
            values.append(own[0:1, 0:1])
        for i, value in enumerate(values):
            coeff[i] = jnp.broadcast_to(value, (8, LANES))

    one, two = coeff[0][0:1, 0:1], coeff[1][0:1, 0:1]
    height_out[...] = prior[...] + (one * r[...] - two * q[...])
    residual_out[...] = r[...] - (one * q[...] - two * s[...])

    def mend(corner, i, j):
        place = (slice(i // 8 * 8, i // 8 * 8 + 8), slice(j // LANES * LANES, j // LANES * LANES + LANES))
        here = (row_ids((8, LANES)) == i % 8) & (lane_ids((8, LANES)) == j % LANES)
        residual_out[place] += jnp.where(here, coeff[1] * coeff[2 + corner], 0.0)

    @pl.when(step == 0)
    def _():
        mend(0, 0, 0)
        mend(1, 0, cols - 1)

    @pl.when(step == steps - 1)
    def _():
        mend(2, rows - 1, 0)
        mend(3, rows - 1, cols - 1)


def finish(where, table, prior, r, q, s, col_count):
    rows, cols = r.shape
    block = pl.BlockSpec((64, cols), lambda i: (i, 0))
    cells = rows * cols
    return pl.pallas_call(
        functools.partial(finish_kernel, col_count),
        grid=(rows // 64,),
        out_shape=[jax.ShapeDtypeStruct((rows, cols), F32)] * 2,
        in_specs=[
            pl.BlockSpec(memory_space=pltpu.SMEM),
            pl.BlockSpec(table.shape, lambda i: (0, 0)),
        ]
        + [block] * 4,
        out_specs=[block] * 2,
        scratch_shapes=[pltpu.VMEM((8, 8, LANES), F32)],
        compiler_params=pltpu.CompilerParams(vmem_limit_bytes=16 * 1024 * 1024),
        cost_estimate=pl.CostEstimate(flops=8 * cells, bytes_accessed=24 * cells, transcendentals=0),
        name="finish",
    )(where, table, prior, r, q, s)


def send(strip, axis, by):
    count = lax.axis_size(axis)
    return lax.ppermute(
        strip, axis, [(i, i + by) for i in range(count) if 0 <= i + by < count]
    )


def exchange(up, down, left, right):
    return (
        send(down, "row", 1), send(up, "row", -1), send(right, "col", 1), send(left, "col", -1),
    )


def shards(
    depth_tiles, conf_tiles, tile_owner, tile_offset, tile_count, prior, edge_rows, edge_cols
):
    row, col = lax.axis_index("row"), lax.axis_index("col")
    row_count, col_count = lax.axis_size("row"), lax.axis_size("col")
    flags = jnp.stack(
        [row == row_count - 1, col == col_count - 1, row * col_count + col]
    ).astype(jnp.int32)[None]
    early = exchange(*strips(prior, edge_rows, edge_cols))
    payload = pack(tile_owner, tile_offset, tile_count, depth_tiles[0], conf_tiles[0], col_count)
    got = lax.all_to_all(payload, "col", split_axis=0, concat_axis=0, tiled=True)
    flow, diag_0, prior_tiles = prepare(flags, prior, edge_rows, edge_cols, *early)
    r, diag, *edges = join(got, prior_tiles, flow, diag_0, edge_rows, edge_cols)
    late = exchange(*edges)
    q, s, table = moments(
        flags, r, diag, edge_rows, edge_cols, *late, early[0], early[2], row_count * col_count
    )
    table = lax.all_to_all(table, ("row", "col"), split_axis=0, concat_axis=0, tiled=True)
    return tuple(finish(flags, table, prior, r, q, s, col_count))


def solution(mesh):
    return jax.shard_map(
        shards,
        mesh=mesh,
        in_specs=(
            P("row", "col", None),
            P("row", "col", None),
            P("row", "col"),
            P("row", "col"),
            P("row", "col"),
            P("row", "col"),
            P("row", "col"),
            P("row", "col"),
        ),
        out_specs=(P("row", "col"), P("row", "col")),
        check_vma=False,
    )
```

```python
import functools

import jax
import jax.numpy as jnp
from jax import lax
from jax.experimental import pallas as pl
from jax.experimental.pallas import tpu as pltpu
from jax.sharding import PartitionSpec as P

TS = 32
GROUPS = 8
LAM = 0.05
HUBER = 0.5
META = 16
LANES = 128
PAD = 8
F32 = jnp.float32
SMALL_VMEM = 20 * 1024 * 1024


def lane_ids(shape):
    return lax.broadcasted_iota(jnp.int32, shape, len(shape) - 1)


def row_ids(shape):
    return lax.broadcasted_iota(jnp.int32, shape, len(shape) - 2)


def cols_up(parts, after):
    rolled = [pltpu.roll(x, LANES - 1, axis=1) for x in parts] + [after]
    last = lane_ids(parts[0].shape) == LANES - 1
    return [jnp.where(last, rolled[b + 1], rolled[b]) for b in range(len(parts))]


def cols_down(parts, before):
    rolled = [before] + [pltpu.roll(x, 1, axis=1) for x in parts]
    first = lane_ids(parts[0].shape) == 0
    return [jnp.where(first, rolled[b], rolled[b + 1]) for b in range(len(parts))]


def side_columns(first, last):
    shape = (LANES, first.shape[1])
    rows = row_ids(shape)
    return jnp.where(rows == 0, first, jnp.where(rows == LANES - 1, last, 0.0)).T


def at_row(i, shift=0):
    if shift:
        return pl.ds(PAD + 8 * i + shift, 8)
    return pl.ds(pl.multiple_of(PAD + 8 * i, 8), 8)


def swap_blocks(four):
    lane = lane_ids(four[0].shape)
    low_half = lane < 64
    even = (lane & 32) == 0
    half = [None] * 4
    for q in range(2):
        a, b = four[q], four[q + 2]
        half[q] = jnp.where(low_half, a, pltpu.roll(b, 64, axis=1))
        half[q + 2] = jnp.where(low_half, pltpu.roll(a, 64, axis=1), b)
    out = [None] * 4
    for q in (0, 2):
        a, b = half[q], half[q + 1]
        out[q] = jnp.where(even, a, pltpu.roll(b, 32, axis=1))
        out[q + 1] = jnp.where(even, pltpu.roll(a, 96, axis=1), b)
    return out


def pack_kernel(owner_ref, count_ref, offset_ref, depth, conf, out, scratch):
    slots = out.shape[0]
    run = depth.shape[0] // GROUPS
    chunks = depth.shape[1] // LANES
    cells = run * chunks
    blank = jnp.zeros((META, LANES), jnp.bfloat16)
    for s in range(slots):
        out[s, 2 * cells :, :] = blank
    rows = row_ids((META, LANES))
    count = count_ref[0, 0]
    for pair in range(GROUPS // 2):
        offsets = jnp.broadcast_to(offset_ref[:, pair * LANES : (pair + 1) * LANES], (META, LANES))
        high = (offsets >> 4).astype(F32)
        low = (offsets & 15).astype(F32)
        for side in range(2):
            g = 2 * pair + side
            if side:
                high, low = pltpu.roll(high, run, axis=1), pltpu.roll(low, run, axis=1)
            live = jnp.clip(count - g * run, 0, run).astype(F32)
            meta = jnp.where(rows == 0, high, jnp.where(rows == 1, low, jnp.where(rows == 2, live, 0.0)))
            out[owner_ref[0, g * run], 2 * cells :, :] = meta.astype(jnp.bfloat16)

    def one_run(g, carry):
        slot = owner_ref[0, g * run]
        for which, source in enumerate((depth, conf)):
            for m in range(run // 16):
                buffer = scratch.at[which * (run // 16) + m]
                block = source[pl.ds(pl.multiple_of(g * run + 16 * m, 16), 16), :].astype(F32)
                if which:
                    tile = row_ids(block.shape) + (g * run + 16 * m)
                    block = jnp.where(tile < count, block * HUBER, 0.0)
                for c in range(chunks):
                    buffer[pl.ds(c, 16, stride=chunks), :] = block[:, c * LANES : (c + 1) * LANES]
                first = which * cells + m * 16 * chunks
                out[slot, first : first + 16 * chunks, :] = buffer[...].astype(jnp.bfloat16)
        return carry

    lax.fori_loop(0, GROUPS, one_run, 0)


def pack(owners, offsets, count, depth, conf, slots):
    tiles, cells = depth.shape
    run = tiles // GROUPS
    rows = 2 * run * (cells // LANES) + META
    vmem = pl.BlockSpec(memory_space=pltpu.VMEM)
    smem = pl.BlockSpec(memory_space=pltpu.SMEM)
    return pl.pallas_call(
        pack_kernel,
        out_shape=jax.ShapeDtypeStruct((slots, rows, LANES), jnp.bfloat16),
        in_specs=[smem, smem, vmem, vmem, vmem],
        out_specs=vmem,
        scratch_shapes=[pltpu.VMEM((2 * run // 16, 16 * (cells // LANES), LANES), F32)],
        compiler_params=pltpu.CompilerParams(vmem_limit_bytes=SMALL_VMEM),
        cost_estimate=pl.CostEstimate(flops=1 << 20, bytes_accessed=4 << 20, transcendentals=0),
        name="pack",
    )(owners, count, offsets, depth, conf)


def strips_kernel(top, bottom, kx_bottom, left, right, ky_right, up_out, down_out, left_out, right_out):
    up_out[...] = top[0:1, :]
    down_out[0:1, :] = bottom[7:8, :]
    down_out[1:2, :] = kx_bottom[7:8, :]
    lane = lane_ids(left.shape)
    left_out[...] = left[...].T[0:1, :]
    both = jnp.where(lane == LANES - 1, right[...], pltpu.roll(ky_right[...], LANES - 1, axis=1))
    turned = both.T
    right_out[0:1, :] = turned[LANES - 1 : LANES, :]
    right_out[1:2, :] = turned[LANES - 2 : LANES - 1, :]


def strips(prior, kx, ky):
    rows, cols = prior.shape
    last_rows = pl.BlockSpec((8, cols), lambda i: (rows // 8 - 1, 0))
    last_cols = pl.BlockSpec((rows, LANES), lambda i: (0, cols // LANES - 1))
    whole = lambda shape: pl.BlockSpec(shape, lambda i: (0, 0))
    shapes = ((1, cols), (2, cols), (1, rows), (2, rows))
    return pl.pallas_call(
        strips_kernel,
        grid=(1,),
        out_shape=[jax.ShapeDtypeStruct(s, F32) for s in shapes],
        in_specs=[
            whole((8, cols)), last_rows, last_rows, whole((rows, LANES)), last_cols, last_cols,
        ],
        out_specs=[whole(s) for s in shapes],
        name="strips",
    )(prior, prior, kx, prior, prior, ky)


BATCH = 16
UF = 4
US = 16
UM = 8


def join_kernel(
    flags, got, prior_in, kx_in, ky_in, from_up, from_down, from_left, from_right,
    r_out, diag_out, kx, ky, up_out, down_out, left_out, right_out,
    prior, table_v, table, tiles, weights, pulls, side_p, left_k, table_sem,
):
    slots, rows_in = got.shape[0], got.shape[1]
    cells = (rows_in - META) // 2
    blocks, rows = diag_out.shape[0], diag_out.shape[1]
    steps = rows // 8
    for s in range(slots):
        fields = got[s, 2 * cells :, :].astype(F32)
        target = fields[0:1, :] * 128.0 + fields[1:2, :] * 8.0
        table_v[s, 0:1, :] = target.astype(jnp.int32)
        table_v[s, 1:2, :] = fields[2:3, :].astype(jnp.int32)
    table_copy = pltpu.make_async_copy(table_v, table, table_sem)
    table_copy.start()

    zero = jnp.zeros((TS, LANES), F32)

    def clear(i, carry):
        part = pl.ds(pl.multiple_of(i * TS, TS), TS)
        weights[part, :] = zero
        pulls[part, :] = zero
        return carry

    lax.fori_loop(0, rows * blocks // TS, clear, 0)
    side_p[...] = side_columns(from_left[0:1, :], from_right[...])
    left_k[...] = side_columns(from_left[1:2, :], from_left[1:2, :])
    for b in range(blocks):
        lanes = slice(b * LANES, (b + 1) * LANES)
        prior[b, PAD - 1 : PAD, :] = from_up[0:1, lanes]
        kx[b, PAD - 1 : PAD, :] = from_up[1:2, lanes]
        prior[b, PAD + rows : PAD + rows + 1, :] = from_down[0:1, lanes]
        r_out[b, PAD - 1 : PAD, :] = jnp.zeros((1, LANES), F32)
        r_out[b, PAD + rows : PAD + rows + 1, :] = jnp.zeros((1, LANES), F32)
    def tile_rows(strip, b):
        first = (strip * (blocks * LANES // TS) + 4 * b) * 8
        return [pl.ds(pl.multiple_of(first + 8 * q, 8), 8) for q in range(4)]

    def grid_rows(pad, strip, a):
        return pl.ds(pad + TS * strip + a, 8, stride=4)

    def to_tiles(strip, carry):
        base = pl.multiple_of(TS * strip, TS)
        rows_here = pl.ds(base, TS)
        padded = pl.ds(pl.multiple_of(PAD + base, 8), TS)
        for b in range(blocks):
            lanes = slice(b * LANES, (b + 1) * LANES)
            prior[b, padded, :] = prior_in[rows_here, lanes]
            kx[b, padded, :] = kx_in[rows_here, lanes]
            ky[b, rows_here, :] = ky_in[rows_here, lanes]
        for b in range(blocks):
            four = swap_blocks([prior[b, grid_rows(PAD, strip, a), :] for a in range(4)])
            for place, part in zip(tile_rows(strip, b), four):
                tiles[place, :] = part
        return carry

    lax.fori_loop(0, rows // TS, to_tiles, 0)
    table_copy.wait()

    def one_slot(slot, carry):
        live = table[slot, 1, 0]

        def batch(step, carry):
            first = step * BATCH
            places, terms = [], []
            for pair in range(BATCH // 2):
                at = pl.multiple_of((first + 2 * pair) * 8, 16)
                depths = got[slot, pl.ds(at, 16), :].astype(F32)
                confs = got[slot, pl.ds(cells + at, 16), :].astype(F32)
                for side in range(2):
                    tile = first + 2 * pair + side
                    place = pl.ds(pl.multiple_of(table[slot, 0, tile], 8), 8)
                    error = depths[8 * side : 8 * side + 8] - tiles[place, :]
                    weight = confs[8 * side : 8 * side + 8] / jnp.maximum(jnp.abs(error), HUBER)
                    places.append(place)
                    terms.append((weight, weight * error))
            for place, (weight, pull) in zip(places, terms):
                weights[place, :] += weight
                pulls[place, :] += pull
            return carry

        return lax.fori_loop(0, (live + BATCH - 1) // BATCH, batch, carry)

    lax.fori_loop(0, slots, one_slot, 0)
    @pl.when(flags[0, 0] == 1)
    def _():
        for b in range(blocks):
            kx[b, PAD + rows - 1 : PAD + rows, :] = jnp.zeros((1, LANES), F32)

    @pl.when(flags[0, 1] == 1)
    def _():
        edge = ky[blocks - 1]
        ky[blocks - 1] = jnp.where(lane_ids(edge.shape) == LANES - 1, 0.0, edge)

    def to_grid(strip, carry):
        for b in range(blocks):
            places = tile_rows(strip, b)
            for total, out, pad in ((weights, diag_out, 0), (pulls, r_out, PAD)):
                for a, part in enumerate(swap_blocks([total[place, :] for place in places])):
                    out[b, grid_rows(pad, strip, a), :] = part
        return carry

    lax.fori_loop(0, rows // TS, to_grid, 0)

    def flows(i, carry):
        here, above, below = at_row(i), at_row(i, -1), at_row(i, 1)
        part = pl.ds(pl.multiple_of(8 * i, 8), 8)
        p = [prior[b, here, :] for b in range(blocks)]
        h = [ky[b, part, :] for b in range(blocks)]
        p_right = cols_up(p, side_p[part, :])
        p_left = cols_down(p, side_p[part, :])
        h_left = cols_down(h, left_k[part, :])
        for b in range(blocks):
            k, k_up = kx[b, here, :], kx[b, above, :]
            down_flow = k * (prior[b, below, :] - p[b])
            up_flow = k_up * (p[b] - prior[b, above, :])
            side_flow = h[b] * (p_right[b] - p[b]) - h_left[b] * (p[b] - p_left[b])
            r_out[b, here, :] += (down_flow - up_flow) + side_flow
            diag_out[b, part, :] += LAM + (k + k_up) + (h[b] + h_left[b])
        return carry

    lax.fori_loop(0, steps, flows, 0, unroll=UF)

    zeros = jnp.zeros((8, LANES), F32)
    for i, out, row in ((0, up_out, 0), (steps - 1, down_out, 7)):
        image = operate(r_out, diag_out, kx, ky, i, zeros, zeros)
        for b in range(blocks):
            lanes = slice(b * LANES, (b + 1) * LANES)
            out[0:1, lanes] = r_out[b, at_row(i), :][row : row + 1, :]
            out[1:2, lanes] = image[b][row : row + 1, :]
    lane = lane_ids((8, LANES))

    def sides(i, carry):
        here = at_row(i)
        part = pl.ds(pl.multiple_of(8 * i, 8), 8)
        for b, edge, sign, target in ((0, 0, 1, side_p), (blocks - 1, LANES - 1, -1, left_k)):
            field = r_out[b, here, :]
            if edge:
                across = pltpu.roll(ky[b, part, :] * field, 1, axis=1)
            else:
                across = ky[b, part, :] * pltpu.roll(field, LANES - 1, axis=1)
            image = diag_out[b, part, :] * field - across - vertical(r_out, kx, b, i)
            target[part, :] = jnp.where(lane == edge, image, pltpu.roll(field, sign % LANES, axis=1))
        return carry

    lax.fori_loop(0, steps, sides, 0, unroll=US)
    turned = side_p[...].T
    left_out[0:1, :] = turned[1:2, :]
    left_out[1:2, :] = turned[0:1, :]
    right_out[...] = left_k[...].T[LANES - 2 :, :]


def join(flags, got, prior, kx, ky, from_up, from_down, from_left, from_right):
    rows, cols = prior.shape
    cells = rows * cols
    blocks = cols // LANES
    slots = got.shape[0]
    vmem = pl.BlockSpec(memory_space=pltpu.VMEM)
    padded, plain = (blocks, rows + 2 * PAD, LANES), (blocks, rows, LANES)
    shapes = (padded, plain, padded, plain, (2, cols), (2, cols), (2, rows), (2, rows))
    in_tiles = pltpu.VMEM((cells // LANES, LANES), F32)
    return pl.pallas_call(
        join_kernel,
        out_shape=[jax.ShapeDtypeStruct(s, F32) for s in shapes],
        in_specs=[pl.BlockSpec(memory_space=pltpu.SMEM)] + [vmem] * 8,
        out_specs=[vmem] * len(shapes),
        scratch_shapes=[
            pltpu.VMEM(padded, F32),
            pltpu.VMEM((slots, 8, LANES), jnp.int32),
            pltpu.SMEM((slots, 8, LANES), jnp.int32),
            in_tiles,
            in_tiles,
            in_tiles,
            pltpu.VMEM((rows, LANES), F32),
            pltpu.VMEM((rows, LANES), F32),
            pltpu.SemaphoreType.DMA,
        ],
        compiler_params=pltpu.CompilerParams(vmem_limit_bytes=SMALL_VMEM),
        cost_estimate=pl.CostEstimate(flops=30 * cells, bytes_accessed=24 * cells, transcendentals=0),
        name="join",
    )(flags, got, prior, kx, ky, from_up, from_down, from_left, from_right)


def vertical(field, kx, b, i):
    here, above, below = at_row(i), at_row(i, -1), at_row(i, 1)
    return kx[b, here, :] * field[b, below, :] + kx[b, above, :] * field[b, above, :]


def operate(field, diag, kx, ky, i, entering, after):
    blocks = diag.shape[0]
    part = pl.ds(8 * i, 8) if isinstance(i, int) else pl.ds(pl.multiple_of(8 * i, 8), 8)
    x = [field[b, at_row(i), :] for b in range(blocks)]
    h = [ky[b, part, :] for b in range(blocks)]
    right = cols_up(x, after)
    left = cols_down([h[b] * x[b] for b in range(blocks)], entering)
    return [
        (diag[b, part, :] * x[b] - vertical(field, kx, b, i)) - (h[b] * right[b] + left[b])
        for b in range(blocks)
    ]


def add_pair(total, other):
    (a, rest_a), (b, rest_b) = total, other
    s = a + b
    back = s - a
    error = (a - (s - back)) + (b - back)
    return s, rest_a + rest_b + error


def fold(pair, axis):
    size = pair[0].shape[axis] // 2
    while size:
        other = tuple(pltpu.roll(part, size, axis=axis) for part in pair)
        pair = add_pair(pair, other)
        size //= 2
    return pair


def moments_kernel(
    r_in, diag, kx, ky, r_up, r_down, r_left, r_right, k_left, own_left, own_right, own_ky,
    r, q, s, table_out, side_r, side_q,
):
    blocks, rows = diag.shape[0], diag.shape[1]
    steps = rows // 8
    last = blocks - 1
    k = k_left[1:2, :]
    side_r[...] = side_columns(k * r_left[0:1, :], r_right[0:1, :])
    side_q[...] = side_columns(
        k * (r_left[1:2, :] - k * own_left[0:1, :]),
        r_right[1:2, :] - own_ky[1:2, :] * own_right[0:1, :],
    )
    top, low = slice(PAD - 1, PAD), slice(PAD + rows, PAD + rows + 1)
    for b in range(blocks):
        lanes = slice(b * LANES, (b + 1) * LANES)
        r[b, top, :] = r_up[0:1, lanes]
        r[b, low, :] = r_down[0:1, lanes]
        q[b, top, :] = r_up[1:2, lanes] - kx[b, top, :] * r[b, PAD : PAD + 1, :]
        final = slice(PAD + rows - 1, PAD + rows)
        q[b, low, :] = r_down[1:2, lanes] - kx[b, final, :] * r[b, final, :]

    def folded(parts):
        while len(parts) > 1:
            parts = [a + b for a, b in zip(parts[::2], parts[1::2])]
        return parts[0]

    def products(left, right):
        return folded([a * b for a, b in zip(left, right)])

    def first(i, carry):
        m0, m1, m2 = carry
        part = pl.ds(pl.multiple_of(8 * i, 8), 8)
        image = operate(r, diag, kx, ky, i, side_r[part, :], side_r[part, :])
        field = [r[b, at_row(i), :] for b in range(blocks)]
        for b in range(blocks):
            q[b, at_row(i), :] = image[b]
        return (
            m0 + products(field, field), m1 + products(field, image), m2 + products(image, image),
        )

    zero = jnp.zeros((8, LANES), F32)
    m0, m1, m2 = lax.fori_loop(0, steps, first, (zero, zero, zero), unroll=UM)

    def second(i, m3):
        part = pl.ds(pl.multiple_of(8 * i, 8), 8)
        image = operate(q, diag, kx, ky, i, side_q[part, :], side_q[part, :])
        for b in range(blocks):
            s[b, part, :] = image[b]
        return m3 + products([q[b, at_row(i), :] for b in range(blocks)], image)

    m3 = lax.fori_loop(0, steps, second, zero, unroll=UM)

    sums = []
    for m in (m0, m1, m2, m3):
        pair = fold((m, jnp.zeros_like(m)), 0)
        sums.append(fold(pair, 1))
    corners = ((0, 0), (last, 0), (0, rows - 1), (last, rows - 1))

    def cell(ref, corner, pad=PAD):
        b, i = corner
        j = LANES - 1 if b else 0
        first = (pad + i) // 8 * 8
        return ref[b, first : first + 8, :][(pad + i) % 8 : (pad + i) % 8 + 1, j : j + 1]

    values = [value[0:1, 0:1] for value, _ in sums] + [rest[0:1, 0:1] for _, rest in sums]
    values += [cell(r, corner) for corner in corners]
    values += [cell(q, corner) for corner in corners]
    values += [cell(kx, corner) for corner in corners[2:]]
    values += [cell(ky, corner, 0) for corner in corners[1::2]]
    lane = lane_ids((1, LANES))
    row = jnp.zeros((1, LANES), F32)
    for place, value in enumerate(values):
        row = jnp.where(lane == place, jnp.broadcast_to(value, (1, LANES)), row)
    table_out[...] = jnp.broadcast_to(row, table_out.shape)


def moments(devices, r, diag, *others):
    blocks, rows, _ = diag.shape
    vmem = pl.BlockSpec(memory_space=pltpu.VMEM)
    cells = blocks * rows * LANES
    return pl.pallas_call(
        moments_kernel,
        out_shape=[
            jax.ShapeDtypeStruct(r.shape, F32),
            jax.ShapeDtypeStruct(r.shape, F32),
            jax.ShapeDtypeStruct(diag.shape, F32),
            jax.ShapeDtypeStruct((devices, LANES), F32),
        ],
        in_specs=[vmem] * (2 + len(others)),
        out_specs=[vmem] * 4,
        scratch_shapes=[pltpu.VMEM((rows, LANES), F32)] * 2,
        input_output_aliases={0: 0},
        compiler_params=pltpu.CompilerParams(vmem_limit_bytes=SMALL_VMEM),
        cost_estimate=pl.CostEstimate(flops=40 * cells, bytes_accessed=24 * cells, transcendentals=0),
        name="moments",
    )(r, diag, *others)


def split(a):
    high = a * 4097.0
    high = high - (high - a)
    return high, a - high


def product(a, b):
    p = a * b
    a1, a2 = split(a)
    b1, b2 = split(b)
    return p, ((a1 * b1 - p) + a1 * b2 + a2 * b1) + a2 * b2


def quotient(top, bottom):
    q = top[0] / bottom[0]
    p, error = product(q, bottom[0])
    rest = ((top[0] - p) - error + top[1] - q * bottom[1]) / bottom[0]
    return q, rest


def finish_kernel(
    col_count, where_ref, table_ref, prior, r, q, s, height_hbm, residual_hbm,
    height, residual, coeff, sems,
):
    blocks, rows = s.shape[0], s.shape[1]
    turned = table_ref[...].T
    devices = turned.shape[1]
    field = [turned[i : i + 1, :] for i in range(20)]

    def at(index, down, right):
        shift = -(down * col_count + right)
        return pltpu.roll(jnp.broadcast_to(field[index], (8, devices)), shift % devices, axis=1)

    r_tl, r_tr, r_bl, r_br = 8, 9, 10, 11
    kx_l, kx_r, ky_t, ky_b = 16, 17, 18, 19
    extra = [
        (at(kx_l, -1, 0) * at(ky_b, -1, -1) + at(ky_t, 0, -1) * at(kx_r, -1, -1)) * at(r_br, -1, -1),
        (at(kx_r, -1, 0) * at(ky_b, -1, 0) + at(ky_t, 0, 0) * at(kx_l, -1, 1)) * at(r_bl, -1, 1),
        (at(kx_l, 0, 0) * at(ky_t, 1, -1) + at(ky_b, 0, -1) * at(kx_r, 0, -1)) * at(r_tr, 1, -1),
        (at(kx_r, 0, 0) * at(ky_t, 1, 0) + at(ky_b, 0, 0) * at(kx_l, 0, 1)) * at(r_tl, 1, 1),
    ]
    pairs = [
        [jnp.broadcast_to(field[i], (8, devices)), jnp.broadcast_to(field[4 + i], (8, devices))]
        for i in range(4)
    ]
    for corner in range(4):
        pairs[3][1] = pairs[3][1] + extra[corner] * field[12 + corner]
    m = [fold(tuple(pair), 1) for pair in pairs]
    m = [tuple(part[0:1, 0:1] for part in pair) for pair in m]
    x1, x2, x3 = (quotient(m[i + 1], m[i]) for i in range(3))
    gap_1 = (x2[0] - x1[0]) + (x2[1] - x1[1])
    gap_2 = (x3[0] - x2[0]) + (x3[1] - x2[1])
    alpha = 1.0 / x1[0]
    ratio = 1.0 + gap_1 / x1[0]
    alpha_1 = gap_1 / (x2[0] * gap_2)
    mine = lane_ids((8, devices)) == where_ref[0, 2]
    values = [alpha + alpha_1 * ratio, alpha_1 * alpha]
    for corner in range(4):
        own = jnp.sum(jnp.where(mine, extra[corner], 0.0), axis=1, keepdims=True)
        values.append(own[0:1, 0:1])
    for i, value in enumerate(values):
        coeff[i] = jnp.broadcast_to(value, (8, LANES))

    one, two = coeff[0][0:1, 0:1], coeff[1][0:1, 0:1]

    def mend(corner, b, i):
        here = (row_ids((8, LANES)) == i % 8) & (
            lane_ids((8, LANES)) == (LANES - 1 if b else 0)
        )
        residual[b, i // 8 * 8 : i // 8 * 8 + 8, :] += jnp.where(
            here, coeff[1] * coeff[2 + corner], 0.0
        )

    copies = []
    for b in range(blocks):

        def step(i, carry, b=b):
            part = pl.ds(pl.multiple_of(8 * i, 8), 8)
            here = at_row(i)
            x, y = r[b, here, :], q[b, here, :]
            height[b, part, :] = prior[part, b * LANES : (b + 1) * LANES] + (one * x - two * y)
            residual[b, part, :] = x - (one * y - two * s[b, part, :])
            return carry

        lax.fori_loop(0, rows // 8, step, 0, unroll=8)
        if b == 0:
            mend(0, b, 0)
            mend(2, b, rows - 1)
        if b == blocks - 1:
            mend(1, b, 0)
            mend(3, b, rows - 1)
        for which, (source, target) in enumerate(((height, height_hbm), (residual, residual_hbm))):
            copy = pltpu.make_async_copy(
                source.at[b], target.at[:, pl.ds(b * LANES, LANES)], sems.at[which, b]
            )
            copy.start()
            copies.append(copy)
    for copy in copies:
        copy.wait()


def finish(where, table, prior, r, q, s, col_count):
    blocks, rows, _ = s.shape
    cells = rows * blocks * LANES
    vmem = pl.BlockSpec(memory_space=pltpu.VMEM)
    return pl.pallas_call(
        functools.partial(finish_kernel, col_count),
        out_shape=[jax.ShapeDtypeStruct((rows, blocks * LANES), F32)] * 2,
        in_specs=[pl.BlockSpec(memory_space=pltpu.SMEM)] + [vmem] * 5,
        out_specs=[pl.BlockSpec(memory_space=pltpu.HBM)] * 2,
        scratch_shapes=[
            pltpu.VMEM(s.shape, F32),
            pltpu.VMEM(s.shape, F32),
            pltpu.VMEM((8, 8, LANES), F32),
            pltpu.SemaphoreType.DMA((2, blocks)),
        ],
        compiler_params=pltpu.CompilerParams(vmem_limit_bytes=SMALL_VMEM),
        cost_estimate=pl.CostEstimate(flops=8 * cells, bytes_accessed=24 * cells, transcendentals=0),
        name="finish",
    )(where, table, prior, r, q, s)


def send(strip, axis, by):
    count = lax.axis_size(axis)
    return lax.ppermute(
        strip, axis, [(i, i + by) for i in range(count) if 0 <= i + by < count]
    )


def exchange(up, down, left, right):
    return (
        send(down, "row", 1), send(up, "row", -1), send(right, "col", 1), send(left, "col", -1),
    )


def shards(
    depth_tiles, conf_tiles, tile_owner, tile_offset, tile_count, prior, edge_rows, edge_cols
):
    row, col = lax.axis_index("row"), lax.axis_index("col")
    row_count, col_count = lax.axis_size("row"), lax.axis_size("col")
    flags = jnp.stack(
        [row == row_count - 1, col == col_count - 1, row * col_count + col]
    ).astype(jnp.int32)[None]
    own = strips(prior, edge_rows, edge_cols)
    early = exchange(*own)
    payload = pack(tile_owner, tile_offset, tile_count, depth_tiles[0], conf_tiles[0], col_count)
    payload, early, flags = lax.optimization_barrier((payload, early, flags))
    got = lax.all_to_all(payload, "col", split_axis=0, concat_axis=0, tiled=True)
    r, diag, kx, ky, *edges = join(flags, got, prior, edge_rows, edge_cols, *early)
    late = exchange(*edges)
    r, q, s, table = moments(
        row_count * col_count, r, diag, kx, ky, *late, early[2], edges[2], edges[3], own[3]
    )
    table = lax.all_to_all(table, ("row", "col"), split_axis=0, concat_axis=0, tiled=True)
    return tuple(finish(flags, table, prior, r, q, s, col_count))


def solution(mesh):
    return jax.shard_map(
        shards,
        mesh=mesh,
        in_specs=(
            P("row", "col", None),
            P("row", "col", None),
            P("row", "col"),
            P("row", "col"),
            P("row", "col"),
            P("row", "col"),
            P("row", "col"),
            P("row", "col"),
        ),
        out_specs=(P("row", "col"), P("row", "col")),
        check_vma=False,
    )
```

```python
import functools

import jax
import jax.numpy as jnp
from jax import lax
from jax.experimental import pallas as pl
from jax.experimental.pallas import tpu as pltpu
from jax.sharding import PartitionSpec as P

TS = 32
GROUPS = 8
LAM = 0.05
HUBER = 0.5
META = 16
LANES = 128
PAD = 8
F32 = jnp.float32
SMALL_VMEM = 16 * 1024 * 1024


def lane_ids(shape):
    return lax.broadcasted_iota(jnp.int32, shape, len(shape) - 1)


def row_ids(shape):
    return lax.broadcasted_iota(jnp.int32, shape, len(shape) - 2)


def cols_up(parts, after):
    rolled = [pltpu.roll(x, LANES - 1, axis=1) for x in parts] + [after]
    last = lane_ids(parts[0].shape) == LANES - 1
    return [jnp.where(last, rolled[b + 1], rolled[b]) for b in range(len(parts))]


def cols_down(parts, before):
    rolled = [before] + [pltpu.roll(x, 1, axis=1) for x in parts]
    first = lane_ids(parts[0].shape) == 0
    return [jnp.where(first, rolled[b], rolled[b + 1]) for b in range(len(parts))]


def side_columns(first, last):
    shape = (LANES, first.shape[1])
    rows = row_ids(shape)
    return jnp.where(rows == 0, first, jnp.where(rows == LANES - 1, last, 0.0)).T


def at_row(i, shift=0):
    if shift:
        return pl.ds(PAD + 8 * i + shift, 8)
    return pl.ds(pl.multiple_of(PAD + 8 * i, 8), 8)


def swap_blocks(four):
    lane = lane_ids(four[0].shape)
    low_half = lane < 64
    even = (lane & 32) == 0
    half = [None] * 4
    for q in range(2):
        a, b = four[q], four[q + 2]
        half[q] = jnp.where(low_half, a, pltpu.roll(b, 64, axis=1))
        half[q + 2] = jnp.where(low_half, pltpu.roll(a, 64, axis=1), b)
    out = [None] * 4
    for q in (0, 2):
        a, b = half[q], half[q + 1]
        out[q] = jnp.where(even, a, pltpu.roll(b, 32, axis=1))
        out[q + 1] = jnp.where(even, pltpu.roll(a, 96, axis=1), b)
    return out


def pack_kernel(owner_ref, count_ref, offset_ref, depth, conf, out, scratch):
    slots = out.shape[0]
    run = depth.shape[0] // GROUPS
    chunks = depth.shape[1] // LANES
    cells = run * chunks
    blank = jnp.zeros((META, LANES), jnp.bfloat16)
    for s in range(slots):
        out[s, 2 * cells :, :] = blank
    rows = row_ids((META, LANES))
    count = count_ref[0, 0]
    for pair in range(GROUPS // 2):
        offsets = jnp.broadcast_to(offset_ref[:, pair * LANES : (pair + 1) * LANES], (META, LANES))
        high = (offsets >> 4).astype(F32)
        low = (offsets & 15).astype(F32)
        for side in range(2):
            g = 2 * pair + side
            if side:
                high, low = pltpu.roll(high, run, axis=1), pltpu.roll(low, run, axis=1)
            live = jnp.clip(count - g * run, 0, run).astype(F32)
            meta = jnp.where(rows == 0, high, jnp.where(rows == 1, low, jnp.where(rows == 2, live, 0.0)))
            out[owner_ref[0, g * run], 2 * cells :, :] = meta.astype(jnp.bfloat16)

    def one_run(g, carry):
        slot = owner_ref[0, g * run]
        for which, source in enumerate((depth, conf)):
            for m in range(run // 16):
                buffer = scratch.at[which * (run // 16) + m]
                block = source[pl.ds(pl.multiple_of(g * run + 16 * m, 16), 16), :].astype(F32)
                if which:
                    tile = row_ids(block.shape) + (g * run + 16 * m)
                    block = jnp.where(tile < count, block * HUBER, 0.0)
                for c in range(chunks):
                    buffer[pl.ds(c, 16, stride=chunks), :] = block[:, c * LANES : (c + 1) * LANES]
                first = which * cells + m * 16 * chunks
                out[slot, first : first + 16 * chunks, :] = buffer[...].astype(jnp.bfloat16)
        return carry

    lax.fori_loop(0, GROUPS, one_run, 0)


def pack(owners, offsets, count, depth, conf, slots):
    tiles, cells = depth.shape
    run = tiles // GROUPS
    rows = 2 * run * (cells // LANES) + META
    vmem = pl.BlockSpec(memory_space=pltpu.VMEM)
    smem = pl.BlockSpec(memory_space=pltpu.SMEM)
    return pl.pallas_call(
        pack_kernel,
        out_shape=jax.ShapeDtypeStruct((slots, rows, LANES), jnp.bfloat16),
        in_specs=[smem, smem, vmem, vmem, vmem],
        out_specs=vmem,
        scratch_shapes=[pltpu.VMEM((2 * run // 16, 16 * (cells // LANES), LANES), F32)],
        compiler_params=pltpu.CompilerParams(vmem_limit_bytes=SMALL_VMEM),
        cost_estimate=pl.CostEstimate(flops=1 << 20, bytes_accessed=4 << 20, transcendentals=0),
        name="pack",
    )(owners, count, offsets, depth, conf)


def strips_kernel(
    flags, top, bottom, kx_bottom, left, right, ky_right, up_out, down_out, left_out, right_out
):
    up_out[...] = top[0:1, :]
    down_out[0:1, :] = bottom[7:8, :]
    down_out[1:2, :] = jnp.where(flags[0, 0] == 1, 0.0, kx_bottom[7:8, :])
    lane = lane_ids(left.shape)
    left_out[...] = left[...].T[0:1, :]
    both = jnp.where(lane == LANES - 1, right[...], pltpu.roll(ky_right[...], LANES - 1, axis=1))
    turned = both.T
    right_out[0:1, :] = turned[LANES - 1 : LANES, :]
    right_out[1:2, :] = jnp.where(flags[0, 1] == 1, 0.0, turned[LANES - 2 : LANES - 1, :])


def strips(flags, prior, kx, ky):
    rows, cols = prior.shape
    last_rows = pl.BlockSpec((8, cols), lambda i: (rows // 8 - 1, 0))
    last_cols = pl.BlockSpec((rows, LANES), lambda i: (0, cols // LANES - 1))
    whole = lambda shape: pl.BlockSpec(shape, lambda i: (0, 0))
    shapes = ((1, cols), (2, cols), (1, rows), (2, rows))
    return pl.pallas_call(
        strips_kernel,
        grid=(1,),
        out_shape=[jax.ShapeDtypeStruct(s, F32) for s in shapes],
        in_specs=[
            pl.BlockSpec(memory_space=pltpu.SMEM), whole((8, cols)), last_rows, last_rows, whole((rows, LANES)), last_cols, last_cols,
        ],
        out_specs=[whole(s) for s in shapes],
        name="strips",
    )(flags, prior, prior, kx, prior, prior, ky)


BATCH = 16
UF = 4
UO = 8
US = 16
UM = 8


def tile_rows(strip, b, blocks):
    first = (strip * (blocks * LANES // TS) + 4 * b) * 8
    return [pl.ds(pl.multiple_of(first + 8 * q, 8), 8) for q in range(4)]


def grid_rows(pad, strip, a):
    return pl.ds(pad + TS * strip + a, 8, stride=4)


def to_grid(weights, pulls, diag, r, strip, chosen):
    for b in chosen:
        places = tile_rows(strip, b, diag.shape[0])
        for total, out, pad in ((weights, diag, 0), (pulls, r, PAD)):
            for a, part in enumerate(swap_blocks([total[place, :] for place in places])):
                out[b, grid_rows(pad, strip, a), :] = part


def add_flows(r, diag, prior, kx, ky, side_p, left_k, i, chosen):
    last = diag.shape[0] - 1
    here, above, below = at_row(i), at_row(i, -1), at_row(i, 1)
    part = pl.ds(pl.multiple_of(8 * i, 8), 8)
    near = sorted({n for b in chosen for n in (b - 1, b, b + 1) if 0 <= n <= last})
    p = {b: prior[b, here, :] for b in near}
    h = {b: ky[b, part, :] for b in near}
    lane = lane_ids((8, LANES))
    up = {b: pltpu.roll(p[b], LANES - 1, axis=1) for b in near}
    down = {b: pltpu.roll(p[b], 1, axis=1) for b in near}
    h_down = {b: pltpu.roll(h[b], 1, axis=1) for b in near}
    for b in chosen:
        p_right = jnp.where(lane == LANES - 1, up[b + 1] if b < last else side_p[part, :], up[b])
        p_left = jnp.where(lane == 0, down[b - 1] if b else side_p[part, :], down[b])
        h_left = jnp.where(lane == 0, h_down[b - 1] if b else left_k[part, :], h_down[b])
        k, k_up = kx[b, here, :], kx[b, above, :]
        down_flow = k * (prior[b, below, :] - p[b])
        up_flow = k_up * (p[b] - prior[b, above, :])
        side_flow = h[b] * (p_right - p[b]) - h_left * (p[b] - p_left)
        r[b, here, :] += (down_flow - up_flow) + side_flow
        diag[b, part, :] += LAM + (k + k_up) + (h[b] + h_left)


def join_kernel(
    flags, got, prior_in, kx_in, ky_in, from_up, from_down, from_left, from_right,
    r_out, diag_out, prior, kx, ky, weights, pulls, up_out, down_out, left_out, right_out,
    table_v, table, tiles, side_p, left_k, table_sem,
):
    slots, rows_in = got.shape[0], got.shape[1]
    cells = (rows_in - META) // 2
    blocks, rows = diag_out.shape[0], diag_out.shape[1]
    steps = rows // 8
    for s in range(slots):
        fields = got[s, 2 * cells :, :].astype(F32)
        target = fields[0:1, :] * 128.0 + fields[1:2, :] * 8.0
        table_v[s, 0:1, :] = target.astype(jnp.int32)
        table_v[s, 1:2, :] = fields[2:3, :].astype(jnp.int32)
    table_copy = pltpu.make_async_copy(table_v, table, table_sem)
    table_copy.start()

    zero = jnp.zeros((TS, LANES), F32)

    def clear(i, carry):
        part = pl.ds(pl.multiple_of(i * TS, TS), TS)
        weights[part, :] = zero
        pulls[part, :] = zero
        return carry

    lax.fori_loop(0, rows * blocks // TS, clear, 0)
    side_p[...] = side_columns(from_left[0:1, :], from_right[...])
    left_k[...] = side_columns(from_left[1:2, :], from_left[1:2, :])
    for b in range(blocks):
        lanes = slice(b * LANES, (b + 1) * LANES)
        prior[b, PAD - 1 : PAD, :] = from_up[0:1, lanes]
        kx[b, PAD - 1 : PAD, :] = from_up[1:2, lanes]
        prior[b, PAD + rows : PAD + rows + 1, :] = from_down[0:1, lanes]
        r_out[b, PAD - 1 : PAD, :] = jnp.zeros((1, LANES), F32)
        r_out[b, PAD + rows : PAD + rows + 1, :] = jnp.zeros((1, LANES), F32)
    def to_tiles(strip, carry):
        base = pl.multiple_of(TS * strip, TS)
        rows_here = pl.ds(base, TS)
        padded = pl.ds(pl.multiple_of(PAD + base, 8), TS)
        for b in range(blocks):
            lanes = slice(b * LANES, (b + 1) * LANES)
            prior[b, padded, :] = prior_in[rows_here, lanes]
            kx[b, padded, :] = kx_in[rows_here, lanes]
            ky[b, rows_here, :] = ky_in[rows_here, lanes]
        for b in range(blocks):
            four = swap_blocks([prior[b, grid_rows(PAD, strip, a), :] for a in range(4)])
            for place, part in zip(tile_rows(strip, b, blocks), four):
                tiles[place, :] = part
        return carry

    lax.fori_loop(0, rows // TS, to_tiles, 0)
    table_copy.wait()

    def one_slot(slot, carry):
        live = table[slot, 1, 0]

        def batch(step, carry):
            first = step * BATCH
            places, terms = [], []
            for pair in range(BATCH // 2):
                at = pl.multiple_of((first + 2 * pair) * 8, 16)
                depths = got[slot, pl.ds(at, 16), :].astype(F32)
                confs = got[slot, pl.ds(cells + at, 16), :].astype(F32)
                for side in range(2):
                    tile = first + 2 * pair + side
                    place = pl.ds(pl.multiple_of(table[slot, 0, tile], 8), 8)
                    error = depths[8 * side : 8 * side + 8] - tiles[place, :]
                    weight = confs[8 * side : 8 * side + 8] / jnp.maximum(jnp.abs(error), HUBER)
                    places.append(place)
                    terms.append((weight, weight * error))
            for place, (weight, pull) in zip(places, terms):
                weights[place, :] += weight
                pulls[place, :] += pull
            return carry

        return lax.fori_loop(0, (live + BATCH - 1) // BATCH, batch, carry)

    lax.fori_loop(0, slots, one_slot, 0)
    @pl.when(flags[0, 0] == 1)
    def _():
        for b in range(blocks):
            kx[b, PAD + rows - 1 : PAD + rows, :] = jnp.zeros((1, LANES), F32)

    @pl.when(flags[0, 1] == 1)
    def _():
        edge = ky[blocks - 1]
        ky[blocks - 1] = jnp.where(lane_ids(edge.shape) == LANES - 1, 0.0, edge)

    last = blocks - 1

    def outer(pair, carry):
        for strip in (2 * pair, 2 * pair + 1):
            to_grid(weights, pulls, diag_out, r_out, strip, (0, last))
        return carry

    def ends(n, carry):
        to_grid(weights, pulls, diag_out, r_out, n * (rows // TS - 1), range(1, last))
        return carry

    lax.fori_loop(0, rows // TS // 2, outer, 0)
    lax.fori_loop(0, 2, ends, 0)

    def outer_flows(i, carry):
        add_flows(r_out, diag_out, prior, kx, ky, side_p, left_k, i, (0, last))
        return carry

    def end_flows(n, carry):
        i = n * (steps - 1)
        add_flows(r_out, diag_out, prior, kx, ky, side_p, left_k, i, range(1, last))
        return carry

    lax.fori_loop(0, steps, outer_flows, 0, unroll=UO)
    lax.fori_loop(0, 2, end_flows, 0)

    zeros = jnp.zeros((8, LANES), F32)
    for i, out, row in ((0, up_out, 0), (steps - 1, down_out, 7)):
        image = operate(r_out, diag_out, kx, ky, i, zeros, zeros)
        for b in range(blocks):
            lanes = slice(b * LANES, (b + 1) * LANES)
            out[0:1, lanes] = r_out[b, at_row(i), :][row : row + 1, :]
            out[1:2, lanes] = image[b][row : row + 1, :]
    lane = lane_ids((8, LANES))

    def sides(i, carry):
        here = at_row(i)
        part = pl.ds(pl.multiple_of(8 * i, 8), 8)
        for b, edge, sign, target in ((0, 0, 1, side_p), (blocks - 1, LANES - 1, -1, left_k)):
            field = r_out[b, here, :]
            if edge:
                across = pltpu.roll(ky[b, part, :] * field, 1, axis=1)
            else:
                across = ky[b, part, :] * pltpu.roll(field, LANES - 1, axis=1)
            image = diag_out[b, part, :] * field - across - vertical(r_out, kx, b, i)
            target[part, :] = jnp.where(lane == edge, image, pltpu.roll(field, sign % LANES, axis=1))
        return carry

    lax.fori_loop(0, steps, sides, 0, unroll=US)
    turned = side_p[...].T
    left_out[0:1, :] = turned[1:2, :]
    left_out[1:2, :] = turned[0:1, :]
    right_out[...] = left_k[...].T[LANES - 2 :, :]


def join(flags, got, prior, kx, ky, from_up, from_down, from_left, from_right):
    rows, cols = prior.shape
    cells = rows * cols
    blocks = cols // LANES
    slots = got.shape[0]
    vmem = pl.BlockSpec(memory_space=pltpu.VMEM)
    padded, plain = (blocks, rows + 2 * PAD, LANES), (blocks, rows, LANES)
    in_tiles = (cells // LANES, LANES)
    shapes = (padded, plain, padded, padded, plain, in_tiles, in_tiles, (2, cols), (2, cols), (2, rows), (2, rows))
    return pl.pallas_call(
        join_kernel,
        out_shape=[jax.ShapeDtypeStruct(s, F32) for s in shapes],
        in_specs=[pl.BlockSpec(memory_space=pltpu.SMEM)] + [vmem] * 8,
        out_specs=[vmem] * len(shapes),
        scratch_shapes=[
            pltpu.VMEM((slots, 8, LANES), jnp.int32),
            pltpu.SMEM((slots, 8, LANES), jnp.int32),
            pltpu.VMEM(in_tiles, F32),
            pltpu.VMEM((rows, LANES), F32),
            pltpu.VMEM((rows, LANES), F32),
            pltpu.SemaphoreType.DMA,
        ],
        compiler_params=pltpu.CompilerParams(vmem_limit_bytes=SMALL_VMEM),
        cost_estimate=pl.CostEstimate(flops=30 * cells, bytes_accessed=24 * cells, transcendentals=0),
        name="join",
    )(flags, got, prior, kx, ky, from_up, from_down, from_left, from_right)


def fill_kernel(weights, pulls, prior, kx, ky, r_in, diag_in, r, diag):
    blocks, rows = diag.shape[0], diag.shape[1]
    inner = range(1, blocks - 1)

    def grid_step(strip, carry):
        to_grid(weights, pulls, diag, r, strip, inner)
        return carry

    def flow_step(i, carry):
        add_flows(r, diag, prior, kx, ky, None, None, i, inner)
        return carry

    lax.fori_loop(0, rows // TS, grid_step, 0)
    lax.fori_loop(0, rows // 8, flow_step, 0, unroll=UF)


def fill(weights, pulls, prior, kx, ky, r, diag):
    vmem = pl.BlockSpec(memory_space=pltpu.VMEM)
    return pl.pallas_call(
        fill_kernel,
        out_shape=[jax.ShapeDtypeStruct(x.shape, F32) for x in (r, diag)],
        in_specs=[vmem] * 7,
        out_specs=[vmem] * 2,
        input_output_aliases={5: 0, 6: 1},
        compiler_params=pltpu.CompilerParams(vmem_limit_bytes=SMALL_VMEM),
        cost_estimate=pl.CostEstimate(flops=1 << 25, bytes_accessed=16 << 20, transcendentals=0),
        name="fill",
    )(weights, pulls, prior, kx, ky, r, diag)


def vertical(field, kx, b, i):
    here, above, below = at_row(i), at_row(i, -1), at_row(i, 1)
    return kx[b, here, :] * field[b, below, :] + kx[b, above, :] * field[b, above, :]


def operate(field, diag, kx, ky, i, entering, after):
    blocks = diag.shape[0]
    part = pl.ds(8 * i, 8) if isinstance(i, int) else pl.ds(pl.multiple_of(8 * i, 8), 8)
    x = [field[b, at_row(i), :] for b in range(blocks)]
    h = [ky[b, part, :] for b in range(blocks)]
    right = cols_up(x, after)
    left = cols_down([h[b] * x[b] for b in range(blocks)], entering)
    return [
        (diag[b, part, :] * x[b] - vertical(field, kx, b, i)) - (h[b] * right[b] + left[b])
        for b in range(blocks)
    ]


def add_pair(total, other):
    (a, rest_a), (b, rest_b) = total, other
    s = a + b
    back = s - a
    error = (a - (s - back)) + (b - back)
    return s, rest_a + rest_b + error


def fold(pair, axis):
    size = pair[0].shape[axis] // 2
    while size:
        other = tuple(pltpu.roll(part, size, axis=axis) for part in pair)
        pair = add_pair(pair, other)
        size //= 2
    return pair


def moments_kernel(
    r_in, diag, kx, ky, r_up, r_down, r_left, r_right, k_left, own_left, own_right, own_ky,
    r, q, s, table_out, side_r, side_q,
):
    blocks, rows = diag.shape[0], diag.shape[1]
    steps = rows // 8
    last = blocks - 1
    k = k_left[1:2, :]
    side_r[...] = side_columns(k * r_left[0:1, :], r_right[0:1, :])
    side_q[...] = side_columns(
        k * (r_left[1:2, :] - k * own_left[0:1, :]),
        r_right[1:2, :] - own_ky[1:2, :] * own_right[0:1, :],
    )
    top, low = slice(PAD - 1, PAD), slice(PAD + rows, PAD + rows + 1)
    for b in range(blocks):
        lanes = slice(b * LANES, (b + 1) * LANES)
        r[b, top, :] = r_up[0:1, lanes]
        r[b, low, :] = r_down[0:1, lanes]
        q[b, top, :] = r_up[1:2, lanes] - kx[b, top, :] * r[b, PAD : PAD + 1, :]
        final = slice(PAD + rows - 1, PAD + rows)
        q[b, low, :] = r_down[1:2, lanes] - kx[b, final, :] * r[b, final, :]

    def folded(parts):
        while len(parts) > 1:
            parts = [a + b for a, b in zip(parts[::2], parts[1::2])]
        return parts[0]

    def products(left, right):
        return folded([a * b for a, b in zip(left, right)])

    def first(i, carry):
        m0, m1, m2 = carry
        part = pl.ds(pl.multiple_of(8 * i, 8), 8)
        image = operate(r, diag, kx, ky, i, side_r[part, :], side_r[part, :])
        field = [r[b, at_row(i), :] for b in range(blocks)]
        for b in range(blocks):
            q[b, at_row(i), :] = image[b]
        return (
            m0 + products(field, field), m1 + products(field, image), m2 + products(image, image),
        )

    zero = jnp.zeros((8, LANES), F32)
    m0, m1, m2 = lax.fori_loop(0, steps, first, (zero, zero, zero), unroll=UM)

    def second(i, m3):
        part = pl.ds(pl.multiple_of(8 * i, 8), 8)
        image = operate(q, diag, kx, ky, i, side_q[part, :], side_q[part, :])
        for b in range(blocks):
            s[b, part, :] = image[b]
        return m3 + products([q[b, at_row(i), :] for b in range(blocks)], image)

    m3 = lax.fori_loop(0, steps, second, zero, unroll=UM)

    sums = []
    for m in (m0, m1, m2, m3):
        pair = fold((m, jnp.zeros_like(m)), 0)
        sums.append(fold(pair, 1))
    corners = ((0, 0), (last, 0), (0, rows - 1), (last, rows - 1))

    def cell(ref, corner, pad=PAD):
        b, i = corner
        j = LANES - 1 if b else 0
        first = (pad + i) // 8 * 8
        return ref[b, first : first + 8, :][(pad + i) % 8 : (pad + i) % 8 + 1, j : j + 1]

    values = [value[0:1, 0:1] for value, _ in sums] + [rest[0:1, 0:1] for _, rest in sums]
    values += [cell(r, corner) for corner in corners]
    values += [cell(q, corner) for corner in corners]
    values += [cell(kx, corner) for corner in corners[2:]]
    values += [cell(ky, corner, 0) for corner in corners[1::2]]
    lane = lane_ids((1, LANES))
    row = jnp.zeros((1, LANES), F32)
    for place, value in enumerate(values):
        row = jnp.where(lane == place, jnp.broadcast_to(value, (1, LANES)), row)
    table_out[...] = jnp.broadcast_to(row, table_out.shape)


def moments(devices, r, diag, *others):
    blocks, rows, _ = diag.shape
    vmem = pl.BlockSpec(memory_space=pltpu.VMEM)
    cells = blocks * rows * LANES
    return pl.pallas_call(
        moments_kernel,
        out_shape=[
            jax.ShapeDtypeStruct(r.shape, F32),
            jax.ShapeDtypeStruct(r.shape, F32),
            jax.ShapeDtypeStruct(diag.shape, F32),
            jax.ShapeDtypeStruct((devices, LANES), F32),
        ],
        in_specs=[vmem] * (2 + len(others)),
        out_specs=[vmem] * 4,
        scratch_shapes=[pltpu.VMEM((rows, LANES), F32)] * 2,
        input_output_aliases={0: 0},
        compiler_params=pltpu.CompilerParams(vmem_limit_bytes=SMALL_VMEM),
        cost_estimate=pl.CostEstimate(flops=40 * cells, bytes_accessed=24 * cells, transcendentals=0),
        name="moments",
    )(r, diag, *others)


def split(a):
    high = a * 4097.0
    high = high - (high - a)
    return high, a - high


def product(a, b):
    p = a * b
    a1, a2 = split(a)
    b1, b2 = split(b)
    return p, ((a1 * b1 - p) + a1 * b2 + a2 * b1) + a2 * b2


def quotient(top, bottom):
    q = top[0] / bottom[0]
    p, error = product(q, bottom[0])
    rest = ((top[0] - p) - error + top[1] - q * bottom[1]) / bottom[0]
    return q, rest


def finish_kernel(
    col_count, where_ref, table_ref, prior, r, q, s, height_hbm, residual_hbm,
    height, residual, coeff, sems,
):
    blocks, rows = s.shape[0], s.shape[1]
    turned = table_ref[...].T
    devices = turned.shape[1]
    field = [turned[i : i + 1, :] for i in range(20)]

    def at(index, down, right):
        shift = -(down * col_count + right)
        return pltpu.roll(jnp.broadcast_to(field[index], (8, devices)), shift % devices, axis=1)

    r_tl, r_tr, r_bl, r_br = 8, 9, 10, 11
    kx_l, kx_r, ky_t, ky_b = 16, 17, 18, 19
    extra = [
        (at(kx_l, -1, 0) * at(ky_b, -1, -1) + at(ky_t, 0, -1) * at(kx_r, -1, -1)) * at(r_br, -1, -1),
        (at(kx_r, -1, 0) * at(ky_b, -1, 0) + at(ky_t, 0, 0) * at(kx_l, -1, 1)) * at(r_bl, -1, 1),
        (at(kx_l, 0, 0) * at(ky_t, 1, -1) + at(ky_b, 0, -1) * at(kx_r, 0, -1)) * at(r_tr, 1, -1),
        (at(kx_r, 0, 0) * at(ky_t, 1, 0) + at(ky_b, 0, 0) * at(kx_l, 0, 1)) * at(r_tl, 1, 1),
    ]
    pairs = [
        [jnp.broadcast_to(field[i], (8, devices)), jnp.broadcast_to(field[4 + i], (8, devices))]
        for i in range(4)
    ]
    for corner in range(4):
        pairs[3][1] = pairs[3][1] + extra[corner] * field[12 + corner]
    m = [fold(tuple(pair), 1) for pair in pairs]
    m = [tuple(part[0:1, 0:1] for part in pair) for pair in m]
    x1, x2, x3 = (quotient(m[i + 1], m[i]) for i in range(3))
    gap_1 = (x2[0] - x1[0]) + (x2[1] - x1[1])
    gap_2 = (x3[0] - x2[0]) + (x3[1] - x2[1])
    alpha = 1.0 / x1[0]
    ratio = 1.0 + gap_1 / x1[0]
    alpha_1 = gap_1 / (x2[0] * gap_2)
    mine = lane_ids((8, devices)) == where_ref[0, 2]
    values = [alpha + alpha_1 * ratio, alpha_1 * alpha]
    for corner in range(4):
        own = jnp.sum(jnp.where(mine, extra[corner], 0.0), axis=1, keepdims=True)
        values.append(own[0:1, 0:1])
    for i, value in enumerate(values):
        coeff[i] = jnp.broadcast_to(value, (8, LANES))

    one, two = coeff[0][0:1, 0:1], coeff[1][0:1, 0:1]

    def mend(corner, b, i):
        here = (row_ids((8, LANES)) == i % 8) & (
            lane_ids((8, LANES)) == (LANES - 1 if b else 0)
        )
        residual[b, i // 8 * 8 : i // 8 * 8 + 8, :] += jnp.where(
            here, coeff[1] * coeff[2 + corner], 0.0
        )

    copies = []
    for b in range(blocks):

        def step(i, carry, b=b):
            part = pl.ds(pl.multiple_of(8 * i, 8), 8)
            here = at_row(i)
            x, y = r[b, here, :], q[b, here, :]
            height[b, part, :] = prior[part, b * LANES : (b + 1) * LANES] + (one * x - two * y)
            residual[b, part, :] = x - (one * y - two * s[b, part, :])
            return carry

        lax.fori_loop(0, rows // 8, step, 0, unroll=8)
        if b == 0:
            mend(0, b, 0)
            mend(2, b, rows - 1)
        if b == blocks - 1:
            mend(1, b, 0)
            mend(3, b, rows - 1)
        for which, (source, target) in enumerate(((height, height_hbm), (residual, residual_hbm))):
            copy = pltpu.make_async_copy(
                source.at[b], target.at[:, pl.ds(b * LANES, LANES)], sems.at[which, b]
            )
            copy.start()
            copies.append(copy)
    for copy in copies:
        copy.wait()


def finish(where, table, prior, r, q, s, col_count):
    blocks, rows, _ = s.shape
    cells = rows * blocks * LANES
    vmem = pl.BlockSpec(memory_space=pltpu.VMEM)
    return pl.pallas_call(
        functools.partial(finish_kernel, col_count),
        out_shape=[jax.ShapeDtypeStruct((rows, blocks * LANES), F32)] * 2,
        in_specs=[pl.BlockSpec(memory_space=pltpu.SMEM)] + [vmem] * 5,
        out_specs=[pl.BlockSpec(memory_space=pltpu.HBM)] * 2,
        scratch_shapes=[
            pltpu.VMEM(s.shape, F32),
            pltpu.VMEM(s.shape, F32),
            pltpu.VMEM((8, 8, LANES), F32),
            pltpu.SemaphoreType.DMA((2, blocks)),
        ],
        compiler_params=pltpu.CompilerParams(vmem_limit_bytes=SMALL_VMEM),
        cost_estimate=pl.CostEstimate(flops=8 * cells, bytes_accessed=24 * cells, transcendentals=0),
        name="finish",
    )(where, table, prior, r, q, s)


def send(strip, axis, by):
    count = lax.axis_size(axis)
    return lax.ppermute(strip, axis, [(i, (i + by) % count) for i in range(count)])


def exchange(up, down, left, right):
    return (
        send(down, "row", 1), send(up, "row", -1), send(right, "col", 1), send(left, "col", -1),
    )


def shards(
    depth_tiles, conf_tiles, tile_owner, tile_offset, tile_count, prior, edge_rows, edge_cols
):
    row, col = lax.axis_index("row"), lax.axis_index("col")
    row_count, col_count = lax.axis_size("row"), lax.axis_size("col")
    flags = jnp.stack(
        [row == row_count - 1, col == col_count - 1, row * col_count + col]
    ).astype(jnp.int32)[None]
    own = strips(flags, prior, edge_rows, edge_cols)
    early = exchange(*own)
    payload = pack(tile_owner, tile_offset, tile_count, depth_tiles[0], conf_tiles[0], col_count)
    payload, early, flags = lax.optimization_barrier((payload, early, flags))
    got = lax.all_to_all(payload, "col", split_axis=0, concat_axis=0, tiled=True)
    r, diag, blocked, kx, ky, weights, pulls, *edges = join(
        flags, got, prior, edge_rows, edge_cols, *early
    )
    late = exchange(*edges)
    r, diag = fill(weights, pulls, blocked, kx, ky, r, diag)
    r, q, s, table = moments(
        row_count * col_count, r, diag, kx, ky, *late, early[2], edges[2], edges[3], own[3]
    )
    table = lax.all_to_all(table, ("row", "col"), split_axis=0, concat_axis=0, tiled=True)
    return tuple(finish(flags, table, prior, r, q, s, col_count))


def solution(mesh):
    return jax.shard_map(
        shards,
        mesh=mesh,
        in_specs=(
            P("row", "col", None),
            P("row", "col", None),
            P("row", "col"),
            P("row", "col"),
            P("row", "col"),
            P("row", "col"),
            P("row", "col"),
            P("row", "col"),
        ),
        out_specs=(P("row", "col"), P("row", "col")),
        check_vma=False,
    )
```

```python
import jax
import jax.numpy as jnp
from jax import lax
from jax.experimental import pallas as pl
from jax.experimental.pallas import tpu as pltpu
from jax.sharding import PartitionSpec as P

TS = 32
GROUPS = 8
LAM = 0.05
HUBER = 0.5
META = 16
LANES = 128
PAD = 8
F32 = jnp.float32
SMALL_VMEM = 16 * 1024 * 1024


def is_last(axis):
    return lax.axis_index(axis) == lax.axis_size(axis) - 1


def lane_ids(shape):
    return lax.broadcasted_iota(jnp.int32, shape, len(shape) - 1)


def row_ids(shape):
    return lax.broadcasted_iota(jnp.int32, shape, len(shape) - 2)


def cols_up(parts, after):
    rolled = [pltpu.roll(x, LANES - 1, axis=1) for x in parts] + [after]
    last = lane_ids(parts[0].shape) == LANES - 1
    return [jnp.where(last, rolled[b + 1], rolled[b]) for b in range(len(parts))]


def cols_down(parts, before):
    rolled = [before] + [pltpu.roll(x, 1, axis=1) for x in parts]
    first = lane_ids(parts[0].shape) == 0
    return [jnp.where(first, rolled[b], rolled[b + 1]) for b in range(len(parts))]


def side_columns(first, last):
    shape = (LANES, first.shape[1])
    rows = row_ids(shape)
    return jnp.where(rows == 0, first, jnp.where(rows == LANES - 1, last, 0.0)).T


def at_row(i, shift=0):
    if shift:
        return pl.ds(PAD + 8 * i + shift, 8)
    return pl.ds(pl.multiple_of(PAD + 8 * i, 8), 8)


def swap_blocks(four):
    lane = lane_ids(four[0].shape)
    low_half = lane < 64
    even = (lane & 32) == 0
    half = [None] * 4
    for q in range(2):
        a, b = four[q], four[q + 2]
        half[q] = jnp.where(low_half, a, pltpu.roll(b, 64, axis=1))
        half[q + 2] = jnp.where(low_half, pltpu.roll(a, 64, axis=1), b)
    out = [None] * 4
    for q in (0, 2):
        a, b = half[q], half[q + 1]
        out[q] = jnp.where(even, a, pltpu.roll(b, 32, axis=1))
        out[q + 1] = jnp.where(even, pltpu.roll(a, 96, axis=1), b)
    return out


def pack_kernel(owner_ref, count_ref, offset_ref, depth, conf, out, scratch):
    slots = out.shape[0]
    run = depth.shape[0] // GROUPS
    chunks = depth.shape[1] // LANES
    cells = run * chunks
    blank = jnp.zeros((META, LANES), jnp.bfloat16)
    for s in range(slots):
        out[s, 2 * cells :, :] = blank
    rows = row_ids((META, LANES))
    count = count_ref[0, 0]
    for pair in range(GROUPS // 2):
        offsets = jnp.broadcast_to(offset_ref[:, pair * LANES : (pair + 1) * LANES], (META, LANES))
        high = (offsets >> 4).astype(F32)
        low = (offsets & 15).astype(F32)
        for side in range(2):
            g = 2 * pair + side
            if side:
                high, low = pltpu.roll(high, run, axis=1), pltpu.roll(low, run, axis=1)
            live = jnp.clip(count - g * run, 0, run).astype(F32)
            meta = jnp.where(rows == 0, high, jnp.where(rows == 1, low, jnp.where(rows == 2, live, 0.0)))
            out[owner_ref[0, g * run], 2 * cells :, :] = meta.astype(jnp.bfloat16)

    def one_run(g, carry):
        slot = owner_ref[0, g * run]
        for which, source in enumerate((depth, conf)):
            for m in range(run // 16):
                buffer = scratch.at[which * (run // 16) + m]
                block = source[pl.ds(pl.multiple_of(g * run + 16 * m, 16), 16), :].astype(F32)
                if which:
                    tile = row_ids(block.shape) + (g * run + 16 * m)
                    block = jnp.where(tile < count, block * HUBER, 0.0)
                for c in range(chunks):
                    buffer[pl.ds(c, 16, stride=chunks), :] = block[:, c * LANES : (c + 1) * LANES]
                first = which * cells + m * 16 * chunks
                out[slot, first : first + 16 * chunks, :] = buffer[...].astype(jnp.bfloat16)
        return carry

    lax.fori_loop(0, GROUPS, one_run, 0)


def pack(owners, offsets, count, depth, conf, slots):
    tiles, cells = depth.shape
    run = tiles // GROUPS
    rows = 2 * run * (cells // LANES) + META
    vmem = pl.BlockSpec(memory_space=pltpu.VMEM)
    smem = pl.BlockSpec(memory_space=pltpu.SMEM)
    return pl.pallas_call(
        pack_kernel,
        out_shape=jax.ShapeDtypeStruct((slots, rows, LANES), jnp.bfloat16),
        in_specs=[smem, smem, vmem, vmem, vmem],
        out_specs=vmem,
        scratch_shapes=[pltpu.VMEM((2 * run // 16, 16 * (cells // LANES), LANES), F32)],
        compiler_params=pltpu.CompilerParams(vmem_limit_bytes=SMALL_VMEM),
        cost_estimate=pl.CostEstimate(flops=1 << 20, bytes_accessed=4 << 20, transcendentals=0),
        name="pack",
    )(owners, count, offsets, depth, conf)


def strips_kernel(
    top, bottom, kx_bottom, left, right, ky_right, up_out, down_out, left_out, right_out
):
    up_out[...] = top[0:1, :]
    down_out[0:1, :] = bottom[7:8, :]
    down_out[1:2, :] = jnp.where(is_last("row"), 0.0, kx_bottom[7:8, :])
    lane = lane_ids(left.shape)
    both = jnp.where(lane == LANES - 1, right[...], pltpu.roll(ky_right[...], LANES - 1, axis=1))
    turned = jnp.where(lane == 0, left[...], both).T
    left_out[...] = turned[0:1, :]
    right_out[0:1, :] = turned[LANES - 1 : LANES, :]
    right_out[1:2, :] = jnp.where(is_last("col"), 0.0, turned[LANES - 2 : LANES - 1, :])


def strips(prior, kx, ky):
    rows, cols = prior.shape
    last_rows = pl.BlockSpec((8, cols), lambda i: (rows // 8 - 1, 0))
    last_cols = pl.BlockSpec((rows, LANES), lambda i: (0, cols // LANES - 1))
    whole = lambda shape: pl.BlockSpec(shape, lambda i: (0, 0))
    shapes = ((1, cols), (2, cols), (1, rows), (2, rows))
    return pl.pallas_call(
        strips_kernel,
        grid=(1,),
        out_shape=[jax.ShapeDtypeStruct(s, F32) for s in shapes],
        in_specs=[
            whole((8, cols)), last_rows, last_rows, whole((rows, LANES)), last_cols, last_cols,
        ],
        out_specs=[whole(s) for s in shapes],
        name="strips",
    )(prior, prior, kx, prior, prior, ky)


def arrange_kernel(prior_in, kx_in, ky_in, tiles, prior, kx, ky):
    blocks, rows = ky.shape[0], ky.shape[1]

    def one_strip(strip, carry):
        base = pl.multiple_of(TS * strip, TS)
        here = pl.ds(base, TS)
        padded = pl.ds(pl.multiple_of(PAD + base, 8), TS)
        for b in range(blocks):
            lanes = slice(b * LANES, (b + 1) * LANES)
            prior[b, padded, :] = prior_in[here, lanes]
            kx[b, padded, :] = kx_in[here, lanes]
            ky[b, here, :] = ky_in[here, lanes]
        for b in range(blocks):
            four = swap_blocks([prior[b, grid_rows(PAD, strip, a), :] for a in range(4)])
            for place, part in zip(tiles_of(strip, b, blocks), four):
                tiles[place] = part
        return carry

    lax.fori_loop(0, rows // TS, one_strip, 0, unroll=2)

    @pl.when(is_last("row"))
    def _():
        for b in range(blocks):
            kx[b, PAD + rows - 1 : PAD + rows, :] = jnp.zeros((1, LANES), F32)

    @pl.when(is_last("col"))
    def _():
        edge = ky[blocks - 1]
        ky[blocks - 1] = jnp.where(lane_ids(edge.shape) == LANES - 1, 0.0, edge)


def arrange(prior, kx, ky):
    rows, cols = prior.shape
    blocks = cols // LANES
    vmem = pl.BlockSpec(memory_space=pltpu.VMEM)
    padded, plain = (blocks, rows + 2 * PAD, LANES), (blocks, rows, LANES)
    shapes = ((rows * cols // (8 * LANES), 8, LANES), padded, padded, plain)
    return pl.pallas_call(
        arrange_kernel,
        out_shape=[jax.ShapeDtypeStruct(s, F32) for s in shapes],
        in_specs=[vmem] * 3,
        out_specs=[vmem] * 4,
        compiler_params=pltpu.CompilerParams(vmem_limit_bytes=SMALL_VMEM),
        cost_estimate=pl.CostEstimate(flops=1 << 22, bytes_accessed=14 << 20, transcendentals=0),
        name="arrange",
    )(prior, kx, ky)


BATCH = 16
UF = 4
UO = 16
US = 16
UM = 8


def tiles_of(strip, b, blocks):
    first = strip * (blocks * LANES // TS) + 4 * b
    return [first + q for q in range(4)]


def grid_rows(pad, strip, a):
    return pl.ds(pad + TS * strip + a, 8, stride=4)


def to_grid(weights, pulls, diag, r, strip, chosen):
    for b in chosen:
        places = tiles_of(strip, b, diag.shape[0])
        for total, out, pad in ((weights, diag, 0), (pulls, r, PAD)):
            for a, part in enumerate(swap_blocks([total[place] for place in places])):
                out[b, grid_rows(pad, strip, a), :] = part


def add_flows(r, diag, prior, kx, ky, side_p, left_k, i, chosen):
    last = diag.shape[0] - 1
    here, above, below = at_row(i), at_row(i, -1), at_row(i, 1)
    part = pl.ds(pl.multiple_of(8 * i, 8), 8)
    near = sorted({n for b in chosen for n in (b - 1, b, b + 1) if 0 <= n <= last})
    p = {b: prior[b, here, :] for b in near}
    h = {b: ky[b, part, :] for b in near}
    lane = lane_ids((8, LANES))
    up = {b: pltpu.roll(p[b], LANES - 1, axis=1) for b in near}
    down = {b: pltpu.roll(p[b], 1, axis=1) for b in near}
    h_down = {b: pltpu.roll(h[b], 1, axis=1) for b in near}
    for b in chosen:
        p_right = jnp.where(lane == LANES - 1, up[b + 1] if b < last else side_p[part, :], up[b])
        p_left = jnp.where(lane == 0, down[b - 1] if b else side_p[part, :], down[b])
        h_left = jnp.where(lane == 0, h_down[b - 1] if b else left_k[part, :], h_down[b])
        k, k_up = kx[b, here, :], kx[b, above, :]
        down_flow = k * (prior[b, below, :] - p[b])
        up_flow = k_up * (p[b] - prior[b, above, :])
        side_flow = h[b] * (p_right - p[b]) - h_left * (p[b] - p_left)
        r[b, here, :] += (down_flow - up_flow) + side_flow
        diag[b, part, :] += LAM + (k + k_up) + (h[b] + h_left)


def join_kernel(
    got, tiles, prior_in, kx_in, ky, from_up, from_down, from_left, from_right,
    r_out, diag_out, prior, kx, weights, pulls, up_out, down_out, left_out, right_out,
    table_v, table, side_p, left_k, table_sem,
):
    slots, rows_in = got.shape[0], got.shape[1]
    cells = (rows_in - META) // 2
    blocks, rows = diag_out.shape[0], diag_out.shape[1]
    steps = rows // 8
    for s in range(slots):
        fields = got[s, 2 * cells :, :].astype(F32)
        target = fields[0:1, :] * 16.0 + fields[1:2, :]
        table_v[s, 0:1, :] = target.astype(jnp.int32)
        table_v[s, 1:2, :] = fields[2:3, :].astype(jnp.int32)
    table_copy = pltpu.make_async_copy(table_v, table, table_sem)
    table_copy.start()

    zero = jnp.zeros((8, LANES), F32)

    def clear(i, carry):
        weights[i] = zero
        pulls[i] = zero
        return carry

    lax.fori_loop(0, tiles.shape[0], clear, 0, unroll=8)
    side_p[...] = side_columns(from_left[0:1, :], from_right[...])
    left_k[...] = side_columns(from_left[1:2, :], from_left[1:2, :])
    for b in range(blocks):
        lanes = slice(b * LANES, (b + 1) * LANES)
        prior[b, PAD - 1 : PAD, :] = from_up[0:1, lanes]
        kx[b, PAD - 1 : PAD, :] = from_up[1:2, lanes]
        prior[b, PAD + rows : PAD + rows + 1, :] = from_down[0:1, lanes]
        r_out[b, PAD - 1 : PAD, :] = jnp.zeros((1, LANES), F32)
        r_out[b, PAD + rows : PAD + rows + 1, :] = jnp.zeros((1, LANES), F32)
    table_copy.wait()

    def one_slot(slot, carry):
        live = table[slot, 1, 0]

        def batch(step, carry):
            first = step * BATCH
            places, terms = [], []
            for pair in range(BATCH // 2):
                at = pl.multiple_of((first + 2 * pair) * 8, 16)
                depths = got[slot, pl.ds(at, 16), :].astype(F32)
                confs = got[slot, pl.ds(cells + at, 16), :].astype(F32)
                for side in range(2):
                    tile = first + 2 * pair + side
                    place = table[slot, 0, tile]
                    error = depths[8 * side : 8 * side + 8] - tiles[place]
                    weight = confs[8 * side : 8 * side + 8] / jnp.maximum(jnp.abs(error), HUBER)
                    places.append(place)
                    terms.append((weight, weight * error))
            for place, (weight, pull) in zip(places, terms):
                weights[place] += weight
                pulls[place] += pull
            return carry

        return lax.fori_loop(0, (live + BATCH - 1) // BATCH, batch, carry)

    lax.fori_loop(0, slots, one_slot, 0)
    last = blocks - 1

    def outer(pair, carry):
        for strip in (2 * pair, 2 * pair + 1):
            to_grid(weights, pulls, diag_out, r_out, strip, (0, last))
        return carry

    def ends(n, carry):
        to_grid(weights, pulls, diag_out, r_out, n * (rows // TS - 1), range(1, last))
        return carry

    lax.fori_loop(0, rows // TS // 2, outer, 0)
    lax.fori_loop(0, 2, ends, 0)

    def outer_flows(i, carry):
        add_flows(r_out, diag_out, prior, kx, ky, side_p, left_k, i, (0, last))
        return carry

    def end_flows(n, carry):
        i = n * (steps - 1)
        add_flows(r_out, diag_out, prior, kx, ky, side_p, left_k, i, range(1, last))
        return carry

    lax.fori_loop(0, steps, outer_flows, 0, unroll=UO)
    lax.fori_loop(0, 2, end_flows, 0)

    zeros = jnp.zeros((8, LANES), F32)
    for i, out, row in ((0, up_out, 0), (steps - 1, down_out, 7)):
        image = operate(r_out, diag_out, kx, ky, i, zeros, zeros)
        for b in range(blocks):
            lanes = slice(b * LANES, (b + 1) * LANES)
            out[0:1, lanes] = r_out[b, at_row(i), :][row : row + 1, :]
            out[1:2, lanes] = image[b][row : row + 1, :]
    lane = lane_ids((8, LANES))

    def sides(i, carry):
        here = at_row(i)
        part = pl.ds(pl.multiple_of(8 * i, 8), 8)
        edges = []
        for b, edge, sign in ((0, 0, 1), (blocks - 1, LANES - 1, -1)):
            field = r_out[b, here, :]
            if edge:
                across = pltpu.roll(ky[b, part, :] * field, 1, axis=1)
            else:
                across = ky[b, part, :] * pltpu.roll(field, LANES - 1, axis=1)
            image = diag_out[b, part, :] * field - across - vertical(r_out, kx, b, i)
            edges.append(
                jnp.where(lane == edge, image, pltpu.roll(field, sign % LANES, axis=1))
            )
        side_p[part, :] = jnp.where(lane < LANES // 2, edges[0], edges[1])
        return carry

    lax.fori_loop(0, steps, sides, 0, unroll=US)
    turned = side_p[...].T
    left_out[0:1, :] = turned[1:2, :]
    left_out[1:2, :] = turned[0:1, :]
    right_out[...] = turned[LANES - 2 :, :]


def join(got, tiles, prior, kx, ky, from_up, from_down, from_left, from_right):
    blocks, rows, _ = ky.shape
    cols = blocks * LANES
    slots = got.shape[0]
    vmem = pl.BlockSpec(memory_space=pltpu.VMEM)
    strip_shapes = ((2, cols), (2, cols), (2, rows), (2, rows))
    shapes = (prior.shape, ky.shape, prior.shape, kx.shape, tiles.shape, tiles.shape) + strip_shapes
    cells = rows * cols
    return pl.pallas_call(
        join_kernel,
        out_shape=[jax.ShapeDtypeStruct(s, F32) for s in shapes],
        in_specs=[vmem] * 9,
        out_specs=[vmem] * len(shapes),
        scratch_shapes=[
            pltpu.VMEM((slots, 8, LANES), jnp.int32),
            pltpu.SMEM((slots, 8, LANES), jnp.int32),
            pltpu.VMEM((rows, LANES), F32),
            pltpu.VMEM((rows, LANES), F32),
            pltpu.SemaphoreType.DMA,
        ],
        input_output_aliases={2: 2, 3: 3},
        compiler_params=pltpu.CompilerParams(vmem_limit_bytes=SMALL_VMEM),
        cost_estimate=pl.CostEstimate(flops=30 * cells, bytes_accessed=24 * cells, transcendentals=0),
        name="join",
    )(got, tiles, prior, kx, ky, from_up, from_down, from_left, from_right)


def fill_kernel(weights, pulls, prior, kx, ky, r_in, diag_in, r, diag):
    blocks, rows = diag.shape[0], diag.shape[1]
    inner = range(1, blocks - 1)

    def grid_step(strip, carry):
        to_grid(weights, pulls, diag, r, strip, inner)
        return carry

    def flow_step(i, carry):
        add_flows(r, diag, prior, kx, ky, None, None, i, inner)
        return carry

    lax.fori_loop(0, rows // TS, grid_step, 0)
    lax.fori_loop(0, rows // 8, flow_step, 0, unroll=UF)


def fill(weights, pulls, prior, kx, ky, r, diag):
    vmem = pl.BlockSpec(memory_space=pltpu.VMEM)
    return pl.pallas_call(
        fill_kernel,
        out_shape=[jax.ShapeDtypeStruct(x.shape, F32) for x in (r, diag)],
        in_specs=[vmem] * 7,
        out_specs=[vmem] * 2,
        input_output_aliases={5: 0, 6: 1},
        compiler_params=pltpu.CompilerParams(vmem_limit_bytes=SMALL_VMEM),
        cost_estimate=pl.CostEstimate(flops=1 << 25, bytes_accessed=16 << 20, transcendentals=0),
        name="fill",
    )(weights, pulls, prior, kx, ky, r, diag)


def vertical(field, kx, b, i):
    here, above, below = at_row(i), at_row(i, -1), at_row(i, 1)
    return kx[b, here, :] * field[b, below, :] + kx[b, above, :] * field[b, above, :]


def operate(field, diag, kx, ky, i, entering, after):
    blocks = diag.shape[0]
    part = pl.ds(8 * i, 8) if isinstance(i, int) else pl.ds(pl.multiple_of(8 * i, 8), 8)
    x = [field[b, at_row(i), :] for b in range(blocks)]
    h = [ky[b, part, :] for b in range(blocks)]
    right = cols_up(x, after)
    left = cols_down([h[b] * x[b] for b in range(blocks)], entering)
    return [
        (diag[b, part, :] * x[b] - vertical(field, kx, b, i)) - (h[b] * right[b] + left[b])
        for b in range(blocks)
    ]


def add_pair(total, other):
    (a, rest_a), (b, rest_b) = total, other
    s = a + b
    back = s - a
    error = (a - (s - back)) + (b - back)
    return s, rest_a + rest_b + error


def fold(pair, axis):
    size = pair[0].shape[axis] // 2
    while size:
        other = tuple(pltpu.roll(part, size, axis=axis) for part in pair)
        pair = add_pair(pair, other)
        size //= 2
    return pair


def moments_kernel(
    r_in, diag, kx, ky, r_up, r_down, r_left, r_right, k_left, own_left, own_right, own_ky,
    r, q, s, table_out, side_r, side_q,
):
    blocks, rows = diag.shape[0], diag.shape[1]
    steps = rows // 8
    last = blocks - 1
    k = k_left[1:2, :]
    side_r[...] = side_columns(k * r_left[0:1, :], r_right[0:1, :])
    side_q[...] = side_columns(
        k * (r_left[1:2, :] - k * own_left[0:1, :]),
        r_right[1:2, :] - own_ky[1:2, :] * own_right[0:1, :],
    )
    top, low = slice(PAD - 1, PAD), slice(PAD + rows, PAD + rows + 1)
    for b in range(blocks):
        lanes = slice(b * LANES, (b + 1) * LANES)
        r[b, top, :] = r_up[0:1, lanes]
        r[b, low, :] = r_down[0:1, lanes]
        q[b, top, :] = r_up[1:2, lanes] - kx[b, top, :] * r[b, PAD : PAD + 1, :]
        final = slice(PAD + rows - 1, PAD + rows)
        q[b, low, :] = r_down[1:2, lanes] - kx[b, final, :] * r[b, final, :]

    def folded(parts):
        while len(parts) > 1:
            parts = [a + b for a, b in zip(parts[::2], parts[1::2])]
        return parts[0]

    def products(left, right):
        return folded([a * b for a, b in zip(left, right)])

    def first(i, carry):
        m0, m1, m2 = carry
        part = pl.ds(pl.multiple_of(8 * i, 8), 8)
        image = operate(r, diag, kx, ky, i, side_r[part, :], side_r[part, :])
        field = [r[b, at_row(i), :] for b in range(blocks)]
        for b in range(blocks):
            q[b, at_row(i), :] = image[b]
        return (
            m0 + products(field, field), m1 + products(field, image), m2 + products(image, image),
        )

    zero = jnp.zeros((8, LANES), F32)
    m0, m1, m2 = lax.fori_loop(0, steps, first, (zero, zero, zero), unroll=UM)

    def second(i, m3):
        part = pl.ds(pl.multiple_of(8 * i, 8), 8)
        image = operate(q, diag, kx, ky, i, side_q[part, :], side_q[part, :])
        for b in range(blocks):
            s[b, part, :] = image[b]
        return m3 + products([q[b, at_row(i), :] for b in range(blocks)], image)

    m3 = lax.fori_loop(0, steps, second, zero, unroll=UM)

    sums = []
    for m in (m0, m1, m2, m3):
        sums.append(fold(fold((m, jnp.zeros_like(m)), 0), 1))
    corners = ((0, 0), (last, 0), (0, rows - 1), (last, rows - 1))

    def cell(ref, corner, pad=PAD):
        b, i = corner
        j = LANES - 1 if b else 0
        first = (pad + i) // 8 * 8
        return ref[b, first : first + 8, :][(pad + i) % 8 : (pad + i) % 8 + 1, j : j + 1]

    values = [value[0:1, 0:1] for value, _ in sums] + [rest[0:1, 0:1] for _, rest in sums]
    values += [cell(r, corner) for corner in corners]
    values += [cell(q, corner) for corner in corners]
    values += [cell(kx, corner) for corner in corners[2:]]
    values += [cell(ky, corner, 0) for corner in corners[1::2]]
    lane = lane_ids((1, LANES))
    row = jnp.zeros((1, LANES), F32)
    for place, value in enumerate(values):
        row = jnp.where(lane == place, jnp.broadcast_to(value, (1, LANES)), row)
    table_out[...] = jnp.broadcast_to(row, table_out.shape)


def moments(devices, r, diag, *others):
    blocks, rows, _ = diag.shape
    vmem = pl.BlockSpec(memory_space=pltpu.VMEM)
    cells = blocks * rows * LANES
    return pl.pallas_call(
        moments_kernel,
        out_shape=[
            jax.ShapeDtypeStruct(r.shape, F32),
            jax.ShapeDtypeStruct(r.shape, F32),
            jax.ShapeDtypeStruct(diag.shape, F32),
            jax.ShapeDtypeStruct((devices, LANES), F32),
        ],
        in_specs=[vmem] * (2 + len(others)),
        out_specs=[vmem] * 4,
        scratch_shapes=[pltpu.VMEM((rows, LANES), F32)] * 2,
        input_output_aliases={0: 0},
        compiler_params=pltpu.CompilerParams(vmem_limit_bytes=SMALL_VMEM),
        cost_estimate=pl.CostEstimate(flops=40 * cells, bytes_accessed=24 * cells, transcendentals=0),
        name="moments",
    )(r, diag, *others)


def split(a):
    high = a * 4097.0
    high = high - (high - a)
    return high, a - high


def product(a, b):
    p = a * b
    a1, a2 = split(a)
    b1, b2 = split(b)
    return p, ((a1 * b1 - p) + a1 * b2 + a2 * b1) + a2 * b2


def quotient(top, bottom):
    q = top[0] / bottom[0]
    p, error = product(q, bottom[0])
    rest = ((top[0] - p) - error + top[1] - q * bottom[1]) / bottom[0]
    return q, rest


def finish_kernel(
    table_ref, prior, r, q, s, height_hbm, residual_hbm,
    height, residual, coeff, sems,
):
    blocks, rows = s.shape[0], s.shape[1]
    turned = table_ref[...].T
    devices = turned.shape[1]
    field = [turned[i : i + 1, :] for i in range(20)]

    def at(index, down, right):
        shift = -(down * lax.axis_size("col") + right)
        return pltpu.roll(jnp.broadcast_to(field[index], (8, devices)), shift % devices, axis=1)

    r_tl, r_tr, r_bl, r_br = 8, 9, 10, 11
    kx_l, kx_r, ky_t, ky_b = 16, 17, 18, 19
    extra = [
        (at(kx_l, -1, 0) * at(ky_b, -1, -1) + at(ky_t, 0, -1) * at(kx_r, -1, -1)) * at(r_br, -1, -1),
        (at(kx_r, -1, 0) * at(ky_b, -1, 0) + at(ky_t, 0, 0) * at(kx_l, -1, 1)) * at(r_bl, -1, 1),
        (at(kx_l, 0, 0) * at(ky_t, 1, -1) + at(ky_b, 0, -1) * at(kx_r, 0, -1)) * at(r_tr, 1, -1),
        (at(kx_r, 0, 0) * at(ky_t, 1, 0) + at(ky_b, 0, 0) * at(kx_l, 0, 1)) * at(r_tl, 1, 1),
    ]
    rows_of = [(table_ref[8 * n : 8 * n + 8, :], 0.0) for n in range(devices // 8)]
    while len(rows_of) > 1:
        rows_of = [add_pair(a, b) for a, b in zip(rows_of[::2], rows_of[1::2])]
    total, rest = fold(rows_of[0], 0)
    m = [
        (total[0:1, i : i + 1], rest[0:1, i : i + 1] + total[0:1, 4 + i : 5 + i]) for i in range(4)
    ]
    mended = sum(extra[corner] * field[12 + corner] for corner in range(4))
    mended = jnp.sum(mended, axis=1, keepdims=True)[0:1, :]
    m[3] = (m[3][0], m[3][1] + mended)
    x1, x2, x3 = (quotient(m[i + 1], m[i]) for i in range(3))
    gap_1 = (x2[0] - x1[0]) + (x2[1] - x1[1])
    gap_2 = (x3[0] - x2[0]) + (x3[1] - x2[1])
    alpha = 1.0 / x1[0]
    ratio = 1.0 + gap_1 / x1[0]
    alpha_1 = gap_1 / (x2[0] * gap_2)
    place = lax.axis_index("row") * lax.axis_size("col") + lax.axis_index("col")
    mine = lane_ids((8, devices)) == place
    values = [alpha + alpha_1 * ratio, alpha_1 * alpha]
    for corner in range(4):
        own = jnp.sum(jnp.where(mine, extra[corner], 0.0), axis=1, keepdims=True)
        values.append(own[0:1, 0:1])
    for i, value in enumerate(values):
        coeff[i] = jnp.broadcast_to(value, (8, LANES))

    one, two = coeff[0][0:1, 0:1], coeff[1][0:1, 0:1]

    def mend(corner, b, i):
        here = (row_ids((8, LANES)) == i % 8) & (
            lane_ids((8, LANES)) == (LANES - 1 if b else 0)
        )
        residual[b, i // 8 * 8 : i // 8 * 8 + 8, :] += jnp.where(
            here, coeff[1] * coeff[2 + corner], 0.0
        )

    copies = []
    for b in range(blocks):

        def step(i, carry, b=b):
            part = pl.ds(pl.multiple_of(8 * i, 8), 8)
            here = at_row(i)
            x, y = r[b, here, :], q[b, here, :]
            height[b, part, :] = prior[part, b * LANES : (b + 1) * LANES] + (one * x - two * y)
            residual[b, part, :] = x - (one * y - two * s[b, part, :])
            return carry

        lax.fori_loop(0, rows // 8, step, 0, unroll=8)
        if b == 0:
            mend(0, b, 0)
            mend(2, b, rows - 1)
        if b == blocks - 1:
            mend(1, b, 0)
            mend(3, b, rows - 1)
        for which, (source, target) in enumerate(((height, height_hbm), (residual, residual_hbm))):
            copy = pltpu.make_async_copy(
                source.at[b], target.at[:, pl.ds(b * LANES, LANES)], sems.at[which, b]
            )
            copy.start()
            copies.append(copy)
    for copy in copies:
        copy.wait()


def finish(table, prior, r, q, s):
    blocks, rows, _ = s.shape
    cells = rows * blocks * LANES
    vmem = pl.BlockSpec(memory_space=pltpu.VMEM)
    return pl.pallas_call(
        finish_kernel,
        out_shape=[jax.ShapeDtypeStruct((rows, blocks * LANES), F32)] * 2,
        in_specs=[vmem] * 5,
        out_specs=[pl.BlockSpec(memory_space=pltpu.HBM)] * 2,
        scratch_shapes=[
            pltpu.VMEM(s.shape, F32),
            pltpu.VMEM(s.shape, F32),
            pltpu.VMEM((8, 8, LANES), F32),
            pltpu.SemaphoreType.DMA((2, blocks)),
        ],
        compiler_params=pltpu.CompilerParams(vmem_limit_bytes=SMALL_VMEM),
        cost_estimate=pl.CostEstimate(flops=8 * cells, bytes_accessed=24 * cells, transcendentals=0),
        name="finish",
    )(table, prior, r, q, s)


def send(strip, axis, by):
    count = lax.axis_size(axis)
    return lax.ppermute(strip, axis, [(i, (i + by) % count) for i in range(count)])


def exchange(up, down, left, right):
    return (
        send(down, "row", 1), send(up, "row", -1), send(right, "col", 1), send(left, "col", -1),
    )


def shards(
    depth_tiles, conf_tiles, tile_owner, tile_offset, tile_count, prior, edge_rows, edge_cols
):
    row_count, col_count = lax.axis_size("row"), lax.axis_size("col")
    own = strips(prior, edge_rows, edge_cols)
    early = exchange(*own)
    payload = pack(tile_owner, tile_offset, tile_count, depth_tiles[0], conf_tiles[0], col_count)
    arranged = arrange(prior, edge_rows, edge_cols)
    payload, early, arranged = lax.optimization_barrier((payload, early, arranged))
    got = lax.all_to_all(payload, "col", split_axis=0, concat_axis=0, tiled=True)
    ky = arranged[3]
    r, diag, blocked, kx, weights, pulls, *edges = join(got, *arranged, *early)
    late = exchange(*edges)
    r, diag = fill(weights, pulls, blocked, kx, ky, r, diag)
    r, q, s, table = moments(
        row_count * col_count, r, diag, kx, ky, *late, early[2], edges[2], edges[3], own[3]
    )
    table = lax.all_to_all(table, ("row", "col"), split_axis=0, concat_axis=0, tiled=True)
    return tuple(finish(table, prior, r, q, s))


def solution(mesh):
    return jax.shard_map(
        shards,
        mesh=mesh,
        in_specs=(
            P("row", "col", None),
            P("row", "col", None),
            P("row", "col"),
            P("row", "col"),
            P("row", "col"),
            P("row", "col"),
            P("row", "col"),
            P("row", "col"),
        ),
        out_specs=(P("row", "col"), P("row", "col")),
        check_vma=False,
    )
```

```python
import jax
import jax.numpy as jnp
from jax import lax
from jax.experimental import pallas as pl
from jax.experimental.pallas import tpu as pltpu
from jax.sharding import PartitionSpec as P

TS = 32
GROUPS = 8
LAM = 0.05
HUBER = 0.5
META = 16
LANES = 128
PAD = 8
F32 = jnp.float32
SMALL_VMEM = 16 * 1024 * 1024


def is_last(axis):
    return lax.axis_index(axis) == lax.axis_size(axis) - 1


def lane_ids(shape):
    return lax.broadcasted_iota(jnp.int32, shape, len(shape) - 1)


def row_ids(shape):
    return lax.broadcasted_iota(jnp.int32, shape, len(shape) - 2)


def cols_up(parts, after):
    rolled = [pltpu.roll(x, LANES - 1, axis=1) for x in parts] + [after]
    last = lane_ids(parts[0].shape) == LANES - 1
    return [jnp.where(last, rolled[b + 1], rolled[b]) for b in range(len(parts))]


def cols_down(parts, before):
    rolled = [before] + [pltpu.roll(x, 1, axis=1) for x in parts]
    first = lane_ids(parts[0].shape) == 0
    return [jnp.where(first, rolled[b], rolled[b + 1]) for b in range(len(parts))]


def side_columns(first, last):
    shape = (LANES, first.shape[1])
    rows = row_ids(shape)
    return jnp.where(rows == 0, first, jnp.where(rows == LANES - 1, last, 0.0)).T


def right_edges(ky, part, b):
    edges = ky[part, b * LANES : (b + 1) * LANES]
    if (b + 1) * LANES < ky.shape[1]:
        return edges
    return jnp.where(is_last("col") & (lane_ids(edges.shape) == LANES - 1), 0.0, edges)


def at_row(i, shift=0):
    if shift:
        return pl.ds(PAD + 8 * i + shift, 8)
    return pl.ds(pl.multiple_of(PAD + 8 * i, 8), 8)


def swap_blocks(four):
    lane = lane_ids(four[0].shape)
    low_half = lane < 64
    even = (lane & 32) == 0
    half = [None] * 4
    for q in range(2):
        a, b = four[q], four[q + 2]
        half[q] = jnp.where(low_half, a, pltpu.roll(b, 64, axis=1))
        half[q + 2] = jnp.where(low_half, pltpu.roll(a, 64, axis=1), b)
    out = [None] * 4
    for q in (0, 2):
        a, b = half[q], half[q + 1]
        out[q] = jnp.where(even, a, pltpu.roll(b, 32, axis=1))
        out[q + 1] = jnp.where(even, pltpu.roll(a, 96, axis=1), b)
    return out


def pack_kernel(owner_ref, count_ref, offset_ref, depth, conf, out, scratch):
    slots = out.shape[0]
    run = depth.shape[0] // GROUPS
    chunks = depth.shape[1] // LANES
    cells = run * chunks
    blank = jnp.zeros((META, LANES), jnp.bfloat16)
    for s in range(slots):
        out[s, 2 * cells :, :] = blank
    rows = row_ids((META, LANES))
    count = count_ref[0, 0]
    for pair in range(GROUPS // 2):
        offsets = jnp.broadcast_to(offset_ref[:, pair * LANES : (pair + 1) * LANES], (META, LANES))
        high = (offsets >> 4).astype(F32)
        low = (offsets & 15).astype(F32)
        for side in range(2):
            g = 2 * pair + side
            if side:
                high, low = pltpu.roll(high, run, axis=1), pltpu.roll(low, run, axis=1)
            live = jnp.clip(count - g * run, 0, run).astype(F32)
            meta = jnp.where(rows == 0, high, jnp.where(rows == 1, low, jnp.where(rows == 2, live, 0.0)))
            out[owner_ref[0, g * run], 2 * cells :, :] = meta.astype(jnp.bfloat16)

    def one_run(g, carry):
        slot = owner_ref[0, g * run]
        for which, source in enumerate((depth, conf)):
            for m in range(run // 16):
                buffer = scratch.at[which * (run // 16) + m]
                block = source[pl.ds(pl.multiple_of(g * run + 16 * m, 16), 16), :].astype(F32)
                if which:
                    tile = row_ids(block.shape) + (g * run + 16 * m)
                    block = jnp.where(tile < count, block * HUBER, 0.0)
                for c in range(chunks):
                    buffer[pl.ds(c, 16, stride=chunks), :] = block[:, c * LANES : (c + 1) * LANES]
                first = which * cells + m * 16 * chunks
                out[slot, first : first + 16 * chunks, :] = buffer[...].astype(jnp.bfloat16)
        return carry

    lax.fori_loop(0, GROUPS, one_run, 0)


def pack(owners, offsets, count, depth, conf, slots):
    tiles, cells = depth.shape
    run = tiles // GROUPS
    rows = 2 * run * (cells // LANES) + META
    vmem = pl.BlockSpec(memory_space=pltpu.VMEM)
    smem = pl.BlockSpec(memory_space=pltpu.SMEM)
    return pl.pallas_call(
        pack_kernel,
        out_shape=jax.ShapeDtypeStruct((slots, rows, LANES), jnp.bfloat16),
        in_specs=[smem, smem, vmem, vmem, vmem],
        out_specs=vmem,
        scratch_shapes=[pltpu.VMEM((2 * run // 16, 16 * (cells // LANES), LANES), F32)],
        compiler_params=pltpu.CompilerParams(vmem_limit_bytes=SMALL_VMEM),
        cost_estimate=pl.CostEstimate(flops=1 << 20, bytes_accessed=4 << 20, transcendentals=0),
        name="pack",
    )(owners, count, offsets, depth, conf)


def strips_kernel(
    top, bottom, kx_bottom, left, right, ky_right, up_out, down_out, left_out, right_out
):
    up_out[...] = top[0:1, :]
    down_out[0:1, :] = bottom[7:8, :]
    down_out[1:2, :] = jnp.where(is_last("row"), 0.0, kx_bottom[7:8, :])
    lane = lane_ids(left.shape)
    both = jnp.where(lane == LANES - 1, right[...], pltpu.roll(ky_right[...], LANES - 1, axis=1))
    turned = jnp.where(lane == 0, left[...], both).T
    left_out[...] = turned[0:1, :]
    right_out[0:1, :] = turned[LANES - 1 : LANES, :]
    right_out[1:2, :] = jnp.where(is_last("col"), 0.0, turned[LANES - 2 : LANES - 1, :])


def strips(prior, kx, ky):
    rows, cols = prior.shape
    last_rows = pl.BlockSpec((8, cols), lambda i: (rows // 8 - 1, 0))
    last_cols = pl.BlockSpec((rows, LANES), lambda i: (0, cols // LANES - 1))
    whole = lambda shape: pl.BlockSpec(shape, lambda i: (0, 0))
    shapes = ((1, cols), (2, cols), (1, rows), (2, rows))
    return pl.pallas_call(
        strips_kernel,
        grid=(1,),
        out_shape=[jax.ShapeDtypeStruct(s, F32) for s in shapes],
        in_specs=[
            whole((8, cols)), last_rows, last_rows, whole((rows, LANES)), last_cols, last_cols,
        ],
        out_specs=[pl.BlockSpec(memory_space=pltpu.VMEM)] * 4,
        name="strips",
    )(prior, prior, kx, prior, prior, ky)


def arrange_kernel(prior_in, kx_in, tiles, prior, kx):
    rows, cols = prior_in.shape
    blocks = cols // LANES

    def one_strip(strip, carry):
        base = pl.multiple_of(TS * strip, TS)
        here = pl.ds(base, TS)
        padded = pl.ds(pl.multiple_of(PAD + base, 8), TS)
        for b in range(blocks):
            lanes = slice(b * LANES, (b + 1) * LANES)
            prior[b, padded, :] = prior_in[here, lanes]
            kx[b, padded, :] = kx_in[here, lanes]
        for b in range(blocks):
            four = swap_blocks([prior[b, grid_rows(PAD, strip, a), :] for a in range(4)])
            for place, part in zip(tiles_of(strip, b, blocks), four):
                tiles[place] = part
        return carry

    lax.fori_loop(0, rows // TS, one_strip, 0, unroll=2)

    @pl.when(is_last("row"))
    def _():
        for b in range(blocks):
            kx[b, PAD + rows - 1 : PAD + rows, :] = jnp.zeros((1, LANES), F32)


def arrange(prior, kx):
    rows, cols = prior.shape
    blocks = cols // LANES
    vmem = pl.BlockSpec(memory_space=pltpu.VMEM)
    padded = (blocks, rows + 2 * PAD, LANES)
    shapes = ((rows * cols // (8 * LANES), 8, LANES), padded, padded)
    return pl.pallas_call(
        arrange_kernel,
        out_shape=[jax.ShapeDtypeStruct(s, F32) for s in shapes],
        in_specs=[vmem] * 2,
        out_specs=[vmem] * 3,
        compiler_params=pltpu.CompilerParams(vmem_limit_bytes=SMALL_VMEM),
        cost_estimate=pl.CostEstimate(flops=1 << 22, bytes_accessed=14 << 20, transcendentals=0),
        name="arrange",
    )(prior, kx)


BATCH = 32
UF = 16
UO = 16
US = 32
UM = 16


def tiles_of(strip, b, blocks):
    first = strip * (blocks * LANES // TS) + 4 * b
    return [first + q for q in range(4)]


def grid_rows(pad, strip, a):
    return pl.ds(pad + TS * strip + a, 8, stride=4)


def to_grid(weights, pulls, diag, r, strip, chosen):
    for b in chosen:
        places = tiles_of(strip, b, diag.shape[0])
        for total, out, pad in ((weights, diag, 0), (pulls, r, PAD)):
            for a, part in enumerate(swap_blocks([total[place] for place in places])):
                out[b, grid_rows(pad, strip, a), :] = part


def add_flows(r, diag, prior, kx, ky, side_p, left_k, i, chosen):
    last = diag.shape[0] - 1
    here, above, below = at_row(i), at_row(i, -1), at_row(i, 1)
    part = pl.ds(pl.multiple_of(8 * i, 8), 8)
    near = sorted({n for b in chosen for n in (b - 1, b, b + 1) if 0 <= n <= last})
    p = {b: prior[b, here, :] for b in near}
    h = {b: right_edges(ky, part, b) for b in near}
    lane = lane_ids((8, LANES))
    up = {b: pltpu.roll(p[b], LANES - 1, axis=1) for b in near}
    down = {b: pltpu.roll(p[b], 1, axis=1) for b in near}
    h_down = {b: pltpu.roll(h[b], 1, axis=1) for b in near}
    for b in chosen:
        p_right = jnp.where(lane == LANES - 1, up[b + 1] if b < last else side_p[part, :], up[b])
        p_left = jnp.where(lane == 0, down[b - 1] if b else side_p[part, :], down[b])
        h_left = jnp.where(lane == 0, h_down[b - 1] if b else left_k[part, :], h_down[b])
        k, k_up = kx[b, here, :], kx[b, above, :]
        down_flow = k * (prior[b, below, :] - p[b])
        up_flow = k_up * (p[b] - prior[b, above, :])
        side_flow = h[b] * (p_right - p[b]) - h_left * (p[b] - p_left)
        r[b, here, :] += (down_flow - up_flow) + side_flow
        diag[b, part, :] += LAM + (k + k_up) + (h[b] + h_left)


def join_kernel(
    got, tiles, prior_in, kx_in, ky, from_up, from_down, from_left, from_right,
    r_out, diag_out, prior, kx, weights, pulls, up_out, down_out, left_out, right_out,
    table_v, table, side_p, left_k, table_sem,
):
    slots, rows_in = got.shape[0], got.shape[1]
    cells = (rows_in - META) // 2
    blocks, rows = diag_out.shape[0], diag_out.shape[1]
    steps = rows // 8
    for s in range(slots):
        fields = got[s, 2 * cells :, :].astype(F32)
        target = jnp.broadcast_to(fields[0:1, :] * 16.0 + fields[1:2, :], (8, LANES))
        target = target + 1024.0 * pltpu.roll(target, LANES - 1, axis=1)
        table_v[s, 0:1, :] = target[0:1, :].astype(jnp.int32)
        table_v[s, 1:2, :] = fields[2:3, :].astype(jnp.int32)
    table_copy = pltpu.make_async_copy(table_v, table, table_sem)
    table_copy.start()

    zero = jnp.zeros((8, LANES), F32)

    def clear(i, carry):
        weights[i] = zero
        pulls[i] = zero
        return carry

    lax.fori_loop(0, tiles.shape[0], clear, 0, unroll=8)
    side_p[...] = side_columns(from_left[0:1, :], from_right[...])
    left_k[...] = side_columns(from_left[1:2, :], from_left[1:2, :])
    for b in range(blocks):
        lanes = slice(b * LANES, (b + 1) * LANES)
        prior[b, PAD - 1 : PAD, :] = from_up[0:1, lanes]
        kx[b, PAD - 1 : PAD, :] = from_up[1:2, lanes]
        prior[b, PAD + rows : PAD + rows + 1, :] = from_down[0:1, lanes]
        r_out[b, PAD - 1 : PAD, :] = jnp.zeros((1, LANES), F32)
        r_out[b, PAD + rows : PAD + rows + 1, :] = jnp.zeros((1, LANES), F32)
    table_copy.wait()

    def one_slot(slot, carry):
        live = table[slot, 1, 0]

        def batch(step, carry):
            first = step * BATCH
            places, terms = [], []
            for pair in range(BATCH // 2):
                at = pl.multiple_of((first + 2 * pair) * 8, 16)
                depths = got[slot, pl.ds(at, 16), :].astype(F32)
                confs = got[slot, pl.ds(cells + at, 16), :].astype(F32)
                word = table[slot, 0, first + 2 * pair]
                for side in range(2):
                    place = word >> 10 if side else word & 1023
                    error = depths[8 * side : 8 * side + 8] - tiles[place]
                    weight = confs[8 * side : 8 * side + 8] / jnp.maximum(jnp.abs(error), HUBER)
                    places.append(place)
                    terms.append((weight, weight * error))
            for place, (weight, pull) in zip(places, terms):
                weights[place] += weight
                pulls[place] += pull
            return carry

        return lax.fori_loop(0, (live + BATCH - 1) // BATCH, batch, carry)

    lax.fori_loop(0, slots, one_slot, 0)
    last = blocks - 1

    def outer(four, carry):
        for n in range(4):
            to_grid(weights, pulls, diag_out, r_out, 4 * four + n, (0, last))
        return carry

    def ends(n, carry):
        to_grid(weights, pulls, diag_out, r_out, n * (rows // TS - 1), range(1, last))
        return carry

    lax.fori_loop(0, rows // TS // 4, outer, 0)
    lax.fori_loop(0, 2, ends, 0)

    def outer_flows(i, carry):
        add_flows(r_out, diag_out, prior, kx, ky, side_p, left_k, i, (0, last))
        return carry

    def end_flows(n, carry):
        i = n * (steps - 1)
        add_flows(r_out, diag_out, prior, kx, ky, side_p, left_k, i, range(1, last))
        return carry

    lax.fori_loop(0, steps, outer_flows, 0, unroll=UO)
    lax.fori_loop(0, 2, end_flows, 0)

    zeros = jnp.zeros((8, LANES), F32)
    for i, out, row in ((0, up_out, 0), (steps - 1, down_out, 7)):
        image = operate(r_out, diag_out, kx, ky, i, zeros, zeros)
        for b in range(blocks):
            lanes = slice(b * LANES, (b + 1) * LANES)
            out[0:1, lanes] = r_out[b, at_row(i), :][row : row + 1, :]
            out[1:2, lanes] = image[b][row : row + 1, :]
    lane = lane_ids((8, LANES))

    def sides(i, carry):
        here = at_row(i)
        part = pl.ds(pl.multiple_of(8 * i, 8), 8)
        edges = []
        for b, edge, sign in ((0, 0, 1), (blocks - 1, LANES - 1, -1)):
            field = r_out[b, here, :]
            if edge:
                across = pltpu.roll(right_edges(ky, part, b) * field, 1, axis=1)
            else:
                across = right_edges(ky, part, b) * pltpu.roll(field, LANES - 1, axis=1)
            image = diag_out[b, part, :] * field - across - vertical(r_out, kx, b, i)
            edges.append(
                jnp.where(lane == edge, image, pltpu.roll(field, sign % LANES, axis=1))
            )
        side_p[part, :] = jnp.where(lane < LANES // 2, edges[0], edges[1])
        return carry

    lax.fori_loop(0, steps, sides, 0, unroll=US)
    turned = side_p[...].T
    left_out[0:1, :] = turned[1:2, :]
    left_out[1:2, :] = turned[0:1, :]
    right_out[...] = turned[LANES - 2 :, :]


def join(got, tiles, prior, kx, ky, from_up, from_down, from_left, from_right):
    rows, cols = ky.shape
    blocks = cols // LANES
    slots = got.shape[0]
    vmem = pl.BlockSpec(memory_space=pltpu.VMEM)
    strip_shapes = ((2, cols), (2, cols), (2, rows), (2, rows))
    shapes = (prior.shape, (blocks, rows, LANES), prior.shape, kx.shape, tiles.shape, tiles.shape) + strip_shapes
    cells = rows * cols
    return pl.pallas_call(
        join_kernel,
        out_shape=[jax.ShapeDtypeStruct(s, F32) for s in shapes],
        in_specs=[vmem] * 9,
        out_specs=[vmem] * len(shapes),
        scratch_shapes=[
            pltpu.VMEM((slots, 8, LANES), jnp.int32),
            pltpu.SMEM((slots, 8, LANES), jnp.int32),
            pltpu.VMEM((rows, LANES), F32),
            pltpu.VMEM((rows, LANES), F32),
            pltpu.SemaphoreType.DMA,
        ],
        input_output_aliases={2: 2, 3: 3},
        compiler_params=pltpu.CompilerParams(vmem_limit_bytes=SMALL_VMEM),
        cost_estimate=pl.CostEstimate(flops=30 * cells, bytes_accessed=24 * cells, transcendentals=0),
        name="join",
    )(got, tiles, prior, kx, ky, from_up, from_down, from_left, from_right)


def fill_kernel(weights, pulls, prior, kx, ky, r_in, diag_in, r, diag):
    blocks, rows = diag.shape[0], diag.shape[1]
    inner = range(1, blocks - 1)

    def grid_step(strip, carry):
        to_grid(weights, pulls, diag, r, strip, inner)
        return carry

    def flow_step(i, carry):
        add_flows(r, diag, prior, kx, ky, None, None, i, inner)
        return carry

    lax.fori_loop(0, rows // TS, grid_step, 0)
    lax.fori_loop(0, rows // 8, flow_step, 0, unroll=UF)


def fill(weights, pulls, prior, kx, ky, r, diag):
    vmem = pl.BlockSpec(memory_space=pltpu.VMEM)
    return pl.pallas_call(
        fill_kernel,
        out_shape=[jax.ShapeDtypeStruct(x.shape, F32) for x in (r, diag)],
        in_specs=[vmem] * 7,
        out_specs=[vmem] * 2,
        input_output_aliases={5: 0, 6: 1},
        compiler_params=pltpu.CompilerParams(vmem_limit_bytes=SMALL_VMEM),
        cost_estimate=pl.CostEstimate(flops=1 << 25, bytes_accessed=16 << 20, transcendentals=0),
        name="fill",
    )(weights, pulls, prior, kx, ky, r, diag)


def vertical(field, kx, b, i):
    here, above, below = at_row(i), at_row(i, -1), at_row(i, 1)
    return kx[b, here, :] * field[b, below, :] + kx[b, above, :] * field[b, above, :]


def operate(field, diag, kx, ky, i, entering, after):
    blocks = diag.shape[0]
    part = pl.ds(8 * i, 8) if isinstance(i, int) else pl.ds(pl.multiple_of(8 * i, 8), 8)
    x = [field[b, at_row(i), :] for b in range(blocks)]
    h = [right_edges(ky, part, b) for b in range(blocks)]
    right = cols_up(x, after)
    left = cols_down([h[b] * x[b] for b in range(blocks)], entering)
    return [
        (diag[b, part, :] * x[b] - vertical(field, kx, b, i)) - (h[b] * right[b] + left[b])
        for b in range(blocks)
    ]


def add_pair(total, other):
    (a, rest_a), (b, rest_b) = total, other
    s = a + b
    back = s - a
    error = (a - (s - back)) + (b - back)
    return s, rest_a + rest_b + error


def fold(pair, axis):
    size = pair[0].shape[axis] // 2
    while size:
        other = tuple(pltpu.roll(part, size, axis=axis) for part in pair)
        pair = add_pair(pair, other)
        size //= 2
    return pair


def moments_kernel(
    r_in, diag, kx, ky, r_up, r_down, r_left, r_right, k_left, own_left, own_right, own_ky,
    r, q, s, table_out, side_r, side_q,
):
    blocks, rows = diag.shape[0], diag.shape[1]
    steps = rows // 8
    last = blocks - 1
    k = k_left[1:2, :]
    side_r[...] = side_columns(k * r_left[0:1, :], r_right[0:1, :])
    side_q[...] = side_columns(
        k * (r_left[1:2, :] - k * own_left[0:1, :]),
        r_right[1:2, :] - own_ky[1:2, :] * own_right[0:1, :],
    )
    top, low = slice(PAD - 1, PAD), slice(PAD + rows, PAD + rows + 1)
    for b in range(blocks):
        lanes = slice(b * LANES, (b + 1) * LANES)
        r[b, top, :] = r_up[0:1, lanes]
        r[b, low, :] = r_down[0:1, lanes]
        q[b, top, :] = r_up[1:2, lanes] - kx[b, top, :] * r[b, PAD : PAD + 1, :]
        final = slice(PAD + rows - 1, PAD + rows)
        q[b, low, :] = r_down[1:2, lanes] - kx[b, final, :] * r[b, final, :]

    def folded(parts):
        while len(parts) > 1:
            parts = [a + b for a, b in zip(parts[::2], parts[1::2])]
        return parts[0]

    def products(left, right):
        return folded([a * b for a, b in zip(left, right)])

    def first(i, carry):
        m0, m1, m2 = carry
        part = pl.ds(pl.multiple_of(8 * i, 8), 8)
        image = operate(r, diag, kx, ky, i, side_r[part, :], side_r[part, :])
        field = [r[b, at_row(i), :] for b in range(blocks)]
        for b in range(blocks):
            q[b, at_row(i), :] = image[b]
        return (
            m0 + products(field, field), m1 + products(field, image), m2 + products(image, image),
        )

    zero = jnp.zeros((8, LANES), F32)
    m0, m1, m2 = lax.fori_loop(0, steps, first, (zero, zero, zero), unroll=UM)

    def second(i, m3):
        part = pl.ds(pl.multiple_of(8 * i, 8), 8)
        image = operate(q, diag, kx, ky, i, side_q[part, :], side_q[part, :])
        for b in range(blocks):
            s[b, part, :] = image[b]
        return m3 + products([q[b, at_row(i), :] for b in range(blocks)], image)

    m3 = lax.fori_loop(0, steps, second, zero, unroll=UM)

    sums = []
    for m in (m0, m1, m2, m3):
        sums.append(fold(fold((m, jnp.zeros_like(m)), 0), 1))
    corners = ((0, 0), (last, 0), (0, rows - 1), (last, rows - 1))

    def cell(ref, corner, pad=PAD):
        b, i = corner
        j = LANES - 1 if b else 0
        first = (pad + i) // 8 * 8
        return ref[b, first : first + 8, :][(pad + i) % 8 : (pad + i) % 8 + 1, j : j + 1]

    values = [value[0:1, 0:1] for value, _ in sums] + [rest[0:1, 0:1] for _, rest in sums]
    values += [cell(r, corner) for corner in corners]
    values += [cell(q, corner) for corner in corners]
    values += [cell(kx, corner) for corner in corners[2:]]
    for _, i in corners[1::2]:
        part = slice(i // 8 * 8, i // 8 * 8 + 8)
        values.append(right_edges(ky, part, last)[i % 8 : i % 8 + 1, LANES - 1 :])
    lane = lane_ids((1, LANES))
    row = jnp.zeros((1, LANES), F32)
    for place, value in enumerate(values):
        row = jnp.where(lane == place, jnp.broadcast_to(value, (1, LANES)), row)
    table_out[...] = jnp.broadcast_to(row, table_out.shape)


def moments(devices, r, diag, *others):
    blocks, rows, _ = diag.shape
    vmem = pl.BlockSpec(memory_space=pltpu.VMEM)
    cells = blocks * rows * LANES
    return pl.pallas_call(
        moments_kernel,
        out_shape=[
            jax.ShapeDtypeStruct(r.shape, F32),
            jax.ShapeDtypeStruct(r.shape, F32),
            jax.ShapeDtypeStruct(diag.shape, F32),
            jax.ShapeDtypeStruct((devices, LANES), F32),
        ],
        in_specs=[vmem] * (2 + len(others)),
        out_specs=[vmem] * 4,
        scratch_shapes=[pltpu.VMEM((rows, LANES), F32)] * 2,
        input_output_aliases={0: 0},
        compiler_params=pltpu.CompilerParams(vmem_limit_bytes=SMALL_VMEM),
        cost_estimate=pl.CostEstimate(flops=40 * cells, bytes_accessed=24 * cells, transcendentals=0),
        name="moments",
    )(r, diag, *others)


def split(a):
    high = a * 4097.0
    high = high - (high - a)
    return high, a - high


def product(a, b):
    p = a * b
    a1, a2 = split(a)
    b1, b2 = split(b)
    return p, ((a1 * b1 - p) + a1 * b2 + a2 * b1) + a2 * b2


def quotient(top, bottom):
    q = top[0] / bottom[0]
    p, error = product(q, bottom[0])
    rest = ((top[0] - p) - error + top[1] - q * bottom[1]) / bottom[0]
    return q, rest


def finish_kernel(
    table_ref, prior, r, q, s, height_hbm, residual_hbm,
    height, residual, coeff, sems,
):
    blocks, rows = s.shape[0], s.shape[1]
    turned = table_ref[...].T
    devices = turned.shape[1]
    field = [turned[i : i + 1, :] for i in range(20)]

    def at(index, down, right):
        shift = -(down * lax.axis_size("col") + right)
        return pltpu.roll(jnp.broadcast_to(field[index], (8, devices)), shift % devices, axis=1)

    r_tl, r_tr, r_bl, r_br = 8, 9, 10, 11
    kx_l, kx_r, ky_t, ky_b = 16, 17, 18, 19
    extra = [
        (at(kx_l, -1, 0) * at(ky_b, -1, -1) + at(ky_t, 0, -1) * at(kx_r, -1, -1)) * at(r_br, -1, -1),
        (at(kx_r, -1, 0) * at(ky_b, -1, 0) + at(ky_t, 0, 0) * at(kx_l, -1, 1)) * at(r_bl, -1, 1),
        (at(kx_l, 0, 0) * at(ky_t, 1, -1) + at(ky_b, 0, -1) * at(kx_r, 0, -1)) * at(r_tr, 1, -1),
        (at(kx_r, 0, 0) * at(ky_t, 1, 0) + at(ky_b, 0, 0) * at(kx_l, 0, 1)) * at(r_tl, 1, 1),
    ]
    rows_of = [(table_ref[8 * n : 8 * n + 8, :], 0.0) for n in range(devices // 8)]
    while len(rows_of) > 1:
        rows_of = [add_pair(a, b) for a, b in zip(rows_of[::2], rows_of[1::2])]
    total, rest = fold(rows_of[0], 0)
    m = [
        (total[0:1, i : i + 1], rest[0:1, i : i + 1] + total[0:1, 4 + i : 5 + i]) for i in range(4)
    ]
    mended = sum(extra[corner] * field[12 + corner] for corner in range(4))
    mended = jnp.sum(mended, axis=1, keepdims=True)[0:1, :]
    m[3] = (m[3][0], m[3][1] + mended)
    x1, x2, x3 = (quotient(m[i + 1], m[i]) for i in range(3))
    gap_1 = (x2[0] - x1[0]) + (x2[1] - x1[1])
    gap_2 = (x3[0] - x2[0]) + (x3[1] - x2[1])
    alpha = 1.0 / x1[0]
    ratio = 1.0 + gap_1 / x1[0]
    alpha_1 = gap_1 / (x2[0] * gap_2)
    place = lax.axis_index("row") * lax.axis_size("col") + lax.axis_index("col")
    mine = lane_ids((8, devices)) == place
    values = [alpha + alpha_1 * ratio, alpha_1 * alpha]
    for corner in range(4):
        own = jnp.sum(jnp.where(mine, extra[corner], 0.0), axis=1, keepdims=True)
        values.append(own[0:1, 0:1])
    for i, value in enumerate(values):
        coeff[i] = jnp.broadcast_to(value, (8, LANES))

    one, two = coeff[0][0:1, 0:1], coeff[1][0:1, 0:1]

    def mend(corner, b, i):
        here = (row_ids((8, LANES)) == i % 8) & (
            lane_ids((8, LANES)) == (LANES - 1 if b else 0)
        )
        residual[b, i // 8 * 8 : i // 8 * 8 + 8, :] += jnp.where(
            here, coeff[1] * coeff[2 + corner], 0.0
        )

    copies = []
    for b in range(blocks):

        def step(i, carry, b=b):
            part = pl.ds(pl.multiple_of(8 * i, 8), 8)
            here = at_row(i)
            x, y = r[b, here, :], q[b, here, :]
            height[b, part, :] = prior[part, b * LANES : (b + 1) * LANES] + (one * x - two * y)
            residual[b, part, :] = x - (one * y - two * s[b, part, :])
            return carry

        lax.fori_loop(0, rows // 8, step, 0, unroll=8)
        if b == 0:
            mend(0, b, 0)
            mend(2, b, rows - 1)
        if b == blocks - 1:
            mend(1, b, 0)
            mend(3, b, rows - 1)
        for which, (source, target) in enumerate(((height, height_hbm), (residual, residual_hbm))):
            copy = pltpu.make_async_copy(
                source.at[b], target.at[:, pl.ds(b * LANES, LANES)], sems.at[which, b]
            )
            copy.start()
            copies.append(copy)
    for copy in copies:
        copy.wait()


def finish(table, prior, r, q, s):
    blocks, rows, _ = s.shape
    cells = rows * blocks * LANES
    vmem = pl.BlockSpec(memory_space=pltpu.VMEM)
    return pl.pallas_call(
        finish_kernel,
        out_shape=[jax.ShapeDtypeStruct((rows, blocks * LANES), F32)] * 2,
        in_specs=[vmem] * 5,
        out_specs=[pl.BlockSpec(memory_space=pltpu.HBM)] * 2,
        scratch_shapes=[
            pltpu.VMEM(s.shape, F32),
            pltpu.VMEM(s.shape, F32),
            pltpu.VMEM((8, 8, LANES), F32),
            pltpu.SemaphoreType.DMA((2, blocks)),
        ],
        compiler_params=pltpu.CompilerParams(vmem_limit_bytes=SMALL_VMEM),
        cost_estimate=pl.CostEstimate(flops=8 * cells, bytes_accessed=24 * cells, transcendentals=0),
        name="finish",
    )(table, prior, r, q, s)


def send(strip, axis, by):
    count = lax.axis_size(axis)
    return lax.ppermute(strip, axis, [(i, (i + by) % count) for i in range(count)])


def exchange(up, down, left, right):
    return (
        send(down, "row", 1), send(up, "row", -1), send(right, "col", 1), send(left, "col", -1),
    )


def shards(
    depth_tiles, conf_tiles, tile_owner, tile_offset, tile_count, prior, edge_rows, edge_cols
):
    row_count, col_count = lax.axis_size("row"), lax.axis_size("col")
    own = strips(prior, edge_rows, edge_cols)
    early = exchange(*own)
    payload = pack(tile_owner, tile_offset, tile_count, depth_tiles[0], conf_tiles[0], col_count)
    arranged = arrange(prior, edge_rows)
    payload, early, arranged = lax.optimization_barrier((payload, early, arranged))
    got = lax.all_to_all(payload, "col", split_axis=0, concat_axis=0, tiled=True)
    r, diag, blocked, kx, weights, pulls, *edges = join(got, *arranged, edge_cols, *early)
    late = exchange(*edges)
    r, diag = fill(weights, pulls, blocked, kx, edge_cols, r, diag)
    r, q, s, table = moments(
        row_count * col_count, r, diag, kx, edge_cols, *late, early[2], edges[2], edges[3], own[3]
    )
    table = lax.all_to_all(table, ("row", "col"), split_axis=0, concat_axis=0, tiled=True)
    return tuple(finish(table, prior, r, q, s))


def solution(mesh):
    return jax.shard_map(
        shards,
        mesh=mesh,
        in_specs=(
            P("row", "col", None),
            P("row", "col", None),
            P("row", "col"),
            P("row", "col"),
            P("row", "col"),
            P("row", "col"),
            P("row", "col"),
            P("row", "col"),
        ),
        out_specs=(P("row", "col"), P("row", "col")),
        check_vma=False,
    )
```

```python
import jax
import jax.numpy as jnp
from jax import lax
from jax.experimental import pallas as pl
from jax.experimental.pallas import tpu as pltpu
from jax.sharding import PartitionSpec as P

TS = 32
GROUPS = 8
LAM = 0.05
HUBER = 0.5
META = 16
LANES = 128
PAD = 8
F32 = jnp.float32
SMALL_VMEM = 16 * 1024 * 1024


def is_last(axis):
    return lax.axis_index(axis) == lax.axis_size(axis) - 1


def lane_ids(shape):
    return lax.broadcasted_iota(jnp.int32, shape, len(shape) - 1)


def row_ids(shape):
    return lax.broadcasted_iota(jnp.int32, shape, len(shape) - 2)


def cols_up(parts, after):
    rolled = [pltpu.roll(x, LANES - 1, axis=1) for x in parts] + [after]
    last = lane_ids(parts[0].shape) == LANES - 1
    return [jnp.where(last, rolled[b + 1], rolled[b]) for b in range(len(parts))]


def cols_down(parts, before):
    rolled = [before] + [pltpu.roll(x, 1, axis=1) for x in parts]
    first = lane_ids(parts[0].shape) == 0
    return [jnp.where(first, rolled[b], rolled[b + 1]) for b in range(len(parts))]


def side_columns(first, last):
    shape = (LANES, first.shape[1])
    rows = row_ids(shape)
    return jnp.where(rows == 0, first, jnp.where(rows == LANES - 1, last, 0.0)).T


def right_edges(ky, part, b):
    edges = ky[part, b * LANES : (b + 1) * LANES]
    if (b + 1) * LANES < ky.shape[1]:
        return edges
    return jnp.where(is_last("col") & (lane_ids(edges.shape) == LANES - 1), 0.0, edges)


def at_row(i, shift=0):
    if shift:
        return pl.ds(PAD + 8 * i + shift, 8)
    return pl.ds(pl.multiple_of(PAD + 8 * i, 8), 8)


def swap_blocks(four):
    lane = lane_ids(four[0].shape)
    low_half = lane < 64
    even = (lane & 32) == 0
    half = [None] * 4
    for q in range(2):
        a, b = four[q], four[q + 2]
        half[q] = jnp.where(low_half, a, pltpu.roll(b, 64, axis=1))
        half[q + 2] = jnp.where(low_half, pltpu.roll(a, 64, axis=1), b)
    out = [None] * 4
    for q in (0, 2):
        a, b = half[q], half[q + 1]
        out[q] = jnp.where(even, a, pltpu.roll(b, 32, axis=1))
        out[q + 1] = jnp.where(even, pltpu.roll(a, 96, axis=1), b)
    return out


def pack_kernel(owner_ref, count_ref, offset_ref, depth, conf, out, scratch):
    slots = out.shape[0]
    run = depth.shape[0] // GROUPS
    chunks = depth.shape[1] // LANES
    cells = run * chunks
    blank = jnp.zeros((META, LANES), jnp.bfloat16)
    for s in range(slots):
        out[s, 2 * cells :, :] = blank
    rows = row_ids((META, LANES))
    count = count_ref[0, 0]
    for pair in range(GROUPS // 2):
        offsets = jnp.broadcast_to(offset_ref[:, pair * LANES : (pair + 1) * LANES], (META, LANES))
        high = (offsets >> 4).astype(F32)
        low = (offsets & 15).astype(F32)
        for side in range(2):
            g = 2 * pair + side
            if side:
                high, low = pltpu.roll(high, run, axis=1), pltpu.roll(low, run, axis=1)
            live = jnp.clip(count - g * run, 0, run).astype(F32)
            meta = jnp.where(rows == 0, high, jnp.where(rows == 1, low, jnp.where(rows == 2, live, 0.0)))
            out[owner_ref[0, g * run], 2 * cells :, :] = meta.astype(jnp.bfloat16)

    def one_run(g, carry):
        slot = owner_ref[0, g * run]
        for which, source in enumerate((depth, conf)):
            for m in range(run // 16):
                buffer = scratch.at[which * (run // 16) + m]
                block = source[pl.ds(pl.multiple_of(g * run + 16 * m, 16), 16), :].astype(F32)
                if which:
                    tile = row_ids(block.shape) + (g * run + 16 * m)
                    block = jnp.where(tile < count, block * HUBER, 0.0)
                for c in range(chunks):
                    buffer[pl.ds(c, 16, stride=chunks), :] = block[:, c * LANES : (c + 1) * LANES]
                first = which * cells + m * 16 * chunks
                out[slot, first : first + 16 * chunks, :] = buffer[: 16 * chunks, :].astype(jnp.bfloat16)
        return carry

    lax.fori_loop(0, GROUPS, one_run, 0)


def pack(owners, offsets, count, depth, conf, slots):
    tiles, cells = depth.shape
    run = tiles // GROUPS
    rows = 2 * run * (cells // LANES) + META
    vmem = pl.BlockSpec(memory_space=pltpu.VMEM)
    smem = pl.BlockSpec(memory_space=pltpu.SMEM)
    return pl.pallas_call(
        pack_kernel,
        out_shape=jax.ShapeDtypeStruct((slots, rows, LANES), jnp.bfloat16),
        in_specs=[smem, smem, vmem, vmem, vmem],
        out_specs=vmem,
        scratch_shapes=[pltpu.VMEM((2 * run // 16, 16 * (cells // LANES) + PAD, LANES), F32)],
        compiler_params=pltpu.CompilerParams(vmem_limit_bytes=SMALL_VMEM),
        cost_estimate=pl.CostEstimate(flops=1 << 20, bytes_accessed=4 << 20, transcendentals=0),
        name="pack",
    )(owners, count, offsets, depth, conf)


def strips_kernel(
    top, bottom, kx_bottom, left, right, ky_right, up_out, down_out, left_out, right_out
):
    up_out[...] = top[0:1, :]
    down_out[0:1, :] = bottom[7:8, :]
    down_out[1:2, :] = jnp.where(is_last("row"), 0.0, kx_bottom[7:8, :])
    lane = lane_ids(left.shape)
    both = jnp.where(lane == LANES - 1, right[...], pltpu.roll(ky_right[...], LANES - 1, axis=1))
    turned = jnp.where(lane == 0, left[...], both).T
    left_out[...] = turned[0:1, :]
    right_out[0:1, :] = turned[LANES - 1 : LANES, :]
    right_out[1:2, :] = jnp.where(is_last("col"), 0.0, turned[LANES - 2 : LANES - 1, :])


def strips(prior, kx, ky):
    rows, cols = prior.shape
    last_rows = pl.BlockSpec((8, cols), lambda i: (rows // 8 - 1, 0))
    last_cols = pl.BlockSpec((rows, LANES), lambda i: (0, cols // LANES - 1))
    whole = lambda shape: pl.BlockSpec(shape, lambda i: (0, 0))
    shapes = ((1, cols), (2, cols), (1, rows), (2, rows))
    return pl.pallas_call(
        strips_kernel,
        grid=(1,),
        out_shape=[jax.ShapeDtypeStruct(s, F32) for s in shapes],
        in_specs=[
            whole((8, cols)), last_rows, last_rows, whole((rows, LANES)), last_cols, last_cols,
        ],
        out_specs=[pl.BlockSpec(memory_space=pltpu.VMEM)] * 4,
        name="strips",
    )(prior, prior, kx, prior, prior, ky)


def arrange_kernel(prior_in, kx_in, tiles, prior, kx):
    rows, cols = prior_in.shape
    blocks = cols // LANES

    def one_strip(strip, carry):
        base = pl.multiple_of(TS * strip, TS)
        here = pl.ds(base, TS)
        padded = pl.ds(pl.multiple_of(PAD + base, 8), TS)
        for b in range(blocks):
            lanes = slice(b * LANES, (b + 1) * LANES)
            prior[b, padded, :] = prior_in[here, lanes]
            kx[b, padded, :] = kx_in[here, lanes]
        for b in range(blocks):
            four = swap_blocks([prior[b, grid_rows(PAD, strip, a), :] for a in range(4)])
            for place, part in zip(tiles_of(strip, b, blocks), four):
                tiles[place] = part
        return carry

    lax.fori_loop(0, rows // TS, one_strip, 0, unroll=2)

    @pl.when(is_last("row"))
    def _():
        for b in range(blocks):
            kx[b, PAD + rows - 1 : PAD + rows, :] = jnp.zeros((1, LANES), F32)


def arrange(prior, kx):
    rows, cols = prior.shape
    blocks = cols // LANES
    vmem = pl.BlockSpec(memory_space=pltpu.VMEM)
    padded = (blocks, rows + 2 * PAD, LANES)
    shapes = ((rows * cols // (8 * LANES), 8, LANES), padded, padded)
    return pl.pallas_call(
        arrange_kernel,
        out_shape=[jax.ShapeDtypeStruct(s, F32) for s in shapes],
        in_specs=[vmem] * 2,
        out_specs=[vmem] * 3,
        compiler_params=pltpu.CompilerParams(vmem_limit_bytes=SMALL_VMEM),
        cost_estimate=pl.CostEstimate(flops=1 << 22, bytes_accessed=14 << 20, transcendentals=0),
        name="arrange",
    )(prior, kx)


BATCH = 32
UF = 64
UO = 16
US = 64
UM = 64


def tiles_of(strip, b, blocks):
    first = strip * (blocks * LANES // TS) + 4 * b
    return [first + q for q in range(4)]


def grid_rows(pad, strip, a):
    return pl.ds(pad + TS * strip + a, 8, stride=4)


def to_grid(weights, pulls, diag, r, strip, chosen):
    for b in chosen:
        places = tiles_of(strip, b, diag.shape[0])
        for total, out, pad in ((weights, diag, 0), (pulls, r, PAD)):
            for a, part in enumerate(swap_blocks([total[place] for place in places])):
                out[b, grid_rows(pad, strip, a), :] = part


def add_flows(r, diag, prior, kx, ky, side_p, left_k, i, chosen):
    last = diag.shape[0] - 1
    here, above, below = at_row(i), at_row(i, -1), at_row(i, 1)
    part = pl.ds(pl.multiple_of(8 * i, 8), 8)
    near = sorted({n for b in chosen for n in (b - 1, b, b + 1) if 0 <= n <= last})
    p = {b: prior[b, here, :] for b in near}
    h = {b: right_edges(ky, part, b) for b in near}
    lane = lane_ids((8, LANES))
    up = {b: pltpu.roll(p[b], LANES - 1, axis=1) for b in near}
    down = {b: pltpu.roll(p[b], 1, axis=1) for b in near}
    h_down = {b: pltpu.roll(h[b], 1, axis=1) for b in near}
    for b in chosen:
        p_right = jnp.where(lane == LANES - 1, up[b + 1] if b < last else side_p[part, :], up[b])
        p_left = jnp.where(lane == 0, down[b - 1] if b else side_p[part, :], down[b])
        h_left = jnp.where(lane == 0, h_down[b - 1] if b else left_k[part, :], h_down[b])
        k, k_up = kx[b, here, :], kx[b, above, :]
        down_flow = k * (prior[b, below, :] - p[b])
        up_flow = k_up * (p[b] - prior[b, above, :])
        side_flow = h[b] * (p_right - p[b]) - h_left * (p[b] - p_left)
        r[b, here, :] += (down_flow - up_flow) + side_flow
        diag[b, part, :] += LAM + (k + k_up) + (h[b] + h_left)


def join_kernel(
    got, tiles, prior_in, kx_in, ky, from_up, from_down, from_left, from_right,
    r_out, diag_out, prior, kx, weights, pulls, up_out, down_out, left_out, right_out,
    table_v, table, side_p, left_k, table_sem,
):
    slots, rows_in = got.shape[0], got.shape[1]
    cells = (rows_in - META) // 2
    blocks, rows = diag_out.shape[0], diag_out.shape[1] - PAD
    steps = rows // 8
    for s in range(slots):
        fields = got[s, 2 * cells :, :].astype(F32)
        target = jnp.broadcast_to(fields[0:1, :] * 16.0 + fields[1:2, :], (8, LANES))
        target = target + 1024.0 * pltpu.roll(target, LANES - 1, axis=1)
        table_v[s, 0:1, :] = target[0:1, :].astype(jnp.int32)
        table_v[s, 1:2, :] = fields[2:3, :].astype(jnp.int32)
    table_copy = pltpu.make_async_copy(table_v, table, table_sem)
    table_copy.start()

    zero = jnp.zeros((8, LANES), F32)

    def clear(i, carry):
        weights[i] = zero
        pulls[i] = zero
        return carry

    lax.fori_loop(0, tiles.shape[0], clear, 0, unroll=8)
    side_p[...] = side_columns(from_left[0:1, :], from_right[...])
    left_k[...] = side_columns(from_left[1:2, :], from_left[1:2, :])
    for b in range(blocks):
        lanes = slice(b * LANES, (b + 1) * LANES)
        prior[b, PAD - 1 : PAD, :] = from_up[0:1, lanes]
        kx[b, PAD - 1 : PAD, :] = from_up[1:2, lanes]
        prior[b, PAD + rows : PAD + rows + 1, :] = from_down[0:1, lanes]
        r_out[b, PAD - 1 : PAD, :] = jnp.zeros((1, LANES), F32)
        r_out[b, PAD + rows : PAD + rows + 1, :] = jnp.zeros((1, LANES), F32)
    table_copy.wait()

    def one_slot(slot, carry):
        live = table[slot, 1, 0]

        def batch(step, carry):
            first = step * BATCH
            places, terms = [], []
            for pair in range(BATCH // 2):
                at = pl.multiple_of((first + 2 * pair) * 8, 16)
                depths = got[slot, pl.ds(at, 16), :].astype(F32)
                confs = got[slot, pl.ds(cells + at, 16), :].astype(F32)
                word = table[slot, 0, first + 2 * pair]
                for side in range(2):
                    place = word >> 10 if side else word & 1023
                    error = depths[8 * side : 8 * side + 8] - tiles[place]
                    weight = confs[8 * side : 8 * side + 8] / jnp.maximum(jnp.abs(error), HUBER)
                    places.append(place)
                    terms.append((weight, weight * error))
            for place, (weight, pull) in zip(places, terms):
                weights[place] += weight
                pulls[place] += pull
            return carry

        return lax.fori_loop(0, (live + BATCH - 1) // BATCH, batch, carry)

    lax.fori_loop(0, slots, one_slot, 0)
    last = blocks - 1

    def outer(four, carry):
        for n in range(4):
            to_grid(weights, pulls, diag_out, r_out, 4 * four + n, (0, last))
        return carry

    def ends(n, carry):
        to_grid(weights, pulls, diag_out, r_out, n * (rows // TS - 1), range(1, last))
        return carry

    lax.fori_loop(0, rows // TS // 4, outer, 0)
    lax.fori_loop(0, 2, ends, 0)

    def outer_flows(i, carry):
        add_flows(r_out, diag_out, prior, kx, ky, side_p, left_k, i, (0, last))
        return carry

    def end_flows(n, carry):
        i = n * (steps - 1)
        add_flows(r_out, diag_out, prior, kx, ky, side_p, left_k, i, range(1, last))
        return carry

    lax.fori_loop(0, steps, outer_flows, 0, unroll=UO)
    lax.fori_loop(0, 2, end_flows, 0)

    zeros = jnp.zeros((8, LANES), F32)
    for i, out, row in ((0, up_out, 0), (steps - 1, down_out, 7)):
        image = operate(r_out, diag_out, kx, ky, i, zeros, zeros)
        for b in range(blocks):
            lanes = slice(b * LANES, (b + 1) * LANES)
            out[0:1, lanes] = r_out[b, at_row(i), :][row : row + 1, :]
            out[1:2, lanes] = image[b][row : row + 1, :]
    lane = lane_ids((8, LANES))

    def sides(i, carry):
        here = at_row(i)
        part = pl.ds(pl.multiple_of(8 * i, 8), 8)
        edges = []
        for b, edge, sign in ((0, 0, 1), (blocks - 1, LANES - 1, -1)):
            field = r_out[b, here, :]
            if edge:
                across = pltpu.roll(right_edges(ky, part, b) * field, 1, axis=1)
            else:
                across = right_edges(ky, part, b) * pltpu.roll(field, LANES - 1, axis=1)
            image = diag_out[b, part, :] * field - across - vertical(r_out, kx, b, i)
            edges.append(
                jnp.where(lane == edge, image, pltpu.roll(field, sign % LANES, axis=1))
            )
        side_p[part, :] = jnp.where(lane < LANES // 2, edges[0], edges[1])
        return carry

    lax.fori_loop(0, steps, sides, 0, unroll=US)
    turned = side_p[...].T
    left_out[0:1, :] = turned[1:2, :]
    left_out[1:2, :] = turned[0:1, :]
    right_out[...] = turned[LANES - 2 :, :]


def join(got, tiles, prior, kx, ky, from_up, from_down, from_left, from_right):
    rows, cols = ky.shape
    blocks = cols // LANES
    slots = got.shape[0]
    vmem = pl.BlockSpec(memory_space=pltpu.VMEM)
    strip_shapes = ((2, cols), (2, cols), (2, rows), (2, rows))
    shapes = (prior.shape, (blocks, rows + PAD, LANES), prior.shape, kx.shape, tiles.shape, tiles.shape) + strip_shapes
    cells = rows * cols
    return pl.pallas_call(
        join_kernel,
        out_shape=[jax.ShapeDtypeStruct(s, F32) for s in shapes],
        in_specs=[vmem] * 9,
        out_specs=[vmem] * len(shapes),
        scratch_shapes=[
            pltpu.VMEM((slots, 8, LANES), jnp.int32),
            pltpu.SMEM((slots, 8, LANES), jnp.int32),
            pltpu.VMEM((rows, LANES), F32),
            pltpu.VMEM((rows, LANES), F32),
            pltpu.SemaphoreType.DMA,
        ],
        input_output_aliases={2: 2, 3: 3},
        compiler_params=pltpu.CompilerParams(vmem_limit_bytes=SMALL_VMEM),
        cost_estimate=pl.CostEstimate(flops=30 * cells, bytes_accessed=24 * cells, transcendentals=0),
        name="join",
    )(got, tiles, prior, kx, ky, from_up, from_down, from_left, from_right)


def fill_kernel(weights, pulls, prior, kx, ky, r_in, diag_in, r, diag):
    blocks, rows = diag.shape[0], diag.shape[1] - PAD
    inner = range(1, blocks - 1)

    def grid_step(strip, carry):
        to_grid(weights, pulls, diag, r, strip, inner)
        return carry

    def flow_step(i, carry):
        add_flows(r, diag, prior, kx, ky, None, None, i, inner)
        return carry

    lax.fori_loop(0, rows // TS, grid_step, 0)
    lax.fori_loop(0, rows // 8, flow_step, 0, unroll=UF)


def fill(weights, pulls, prior, kx, ky, r, diag):
    vmem = pl.BlockSpec(memory_space=pltpu.VMEM)
    return pl.pallas_call(
        fill_kernel,
        out_shape=[jax.ShapeDtypeStruct(x.shape, F32) for x in (r, diag)],
        in_specs=[vmem] * 7,
        out_specs=[vmem] * 2,
        input_output_aliases={5: 0, 6: 1},
        compiler_params=pltpu.CompilerParams(vmem_limit_bytes=SMALL_VMEM),
        cost_estimate=pl.CostEstimate(flops=1 << 25, bytes_accessed=16 << 20, transcendentals=0),
        name="fill",
    )(weights, pulls, prior, kx, ky, r, diag)


def vertical(field, kx, b, i):
    here, above, below = at_row(i), at_row(i, -1), at_row(i, 1)
    return kx[b, here, :] * field[b, below, :] + kx[b, above, :] * field[b, above, :]


def operate(field, diag, kx, ky, i, entering, after):
    blocks = diag.shape[0]
    part = pl.ds(8 * i, 8) if isinstance(i, int) else pl.ds(pl.multiple_of(8 * i, 8), 8)
    x = [field[b, at_row(i), :] for b in range(blocks)]
    h = [right_edges(ky, part, b) for b in range(blocks)]
    right = cols_up(x, after)
    left = cols_down([h[b] * x[b] for b in range(blocks)], entering)
    return [
        (diag[b, part, :] * x[b] - vertical(field, kx, b, i)) - (h[b] * right[b] + left[b])
        for b in range(blocks)
    ]


def add_pair(total, other):
    (a, rest_a), (b, rest_b) = total, other
    s = a + b
    back = s - a
    error = (a - (s - back)) + (b - back)
    return s, rest_a + rest_b + error


def fold(pair, axis):
    size = pair[0].shape[axis] // 2
    while size:
        other = tuple(pltpu.roll(part, size, axis=axis) for part in pair)
        pair = add_pair(pair, other)
        size //= 2
    return pair


def moments_kernel(
    r_in, diag, kx, ky, r_up, r_down, r_left, r_right, k_left, own_left, own_right, own_ky,
    r, q, s, table_out, side_r, side_q,
):
    blocks, rows, _ = s.shape
    steps = rows // 8
    last = blocks - 1
    k = k_left[1:2, :]
    side_r[...] = side_columns(k * r_left[0:1, :], r_right[0:1, :])
    side_q[...] = side_columns(
        k * (r_left[1:2, :] - k * own_left[0:1, :]),
        r_right[1:2, :] - own_ky[1:2, :] * own_right[0:1, :],
    )
    top, low = slice(PAD - 1, PAD), slice(PAD + rows, PAD + rows + 1)
    for b in range(blocks):
        lanes = slice(b * LANES, (b + 1) * LANES)
        r[b, top, :] = r_up[0:1, lanes]
        r[b, low, :] = r_down[0:1, lanes]
        q[b, top, :] = r_up[1:2, lanes] - kx[b, top, :] * r[b, PAD : PAD + 1, :]
        final = slice(PAD + rows - 1, PAD + rows)
        q[b, low, :] = r_down[1:2, lanes] - kx[b, final, :] * r[b, final, :]

    def folded(parts):
        while len(parts) > 1:
            parts = [a + b for a, b in zip(parts[::2], parts[1::2])]
        return parts[0]

    def products(left, right):
        return folded([a * b for a, b in zip(left, right)])

    def first(i, carry):
        m0, m1, m2 = carry
        part = pl.ds(pl.multiple_of(8 * i, 8), 8)
        image = operate(r, diag, kx, ky, i, side_r[part, :], side_r[part, :])
        field = [r[b, at_row(i), :] for b in range(blocks)]
        for b in range(blocks):
            q[b, at_row(i), :] = image[b]
        return (
            m0 + products(field, field), m1 + products(field, image), m2 + products(image, image),
        )

    zero = jnp.zeros((8, LANES), F32)
    m0, m1, m2 = lax.fori_loop(0, steps, first, (zero, zero, zero), unroll=UM)

    def second(i, m3):
        part = pl.ds(pl.multiple_of(8 * i, 8), 8)
        image = operate(q, diag, kx, ky, i, side_q[part, :], side_q[part, :])
        for b in range(blocks):
            s[b, part, :] = image[b]
        return m3 + products([q[b, at_row(i), :] for b in range(blocks)], image)

    m3 = lax.fori_loop(0, steps, second, zero, unroll=UM)

    sums = []
    for m in (m0, m1, m2, m3):
        sums.append(fold(fold((m, jnp.zeros_like(m)), 0), 1))
    corners = ((0, 0), (last, 0), (0, rows - 1), (last, rows - 1))

    def cell(ref, corner, pad=PAD):
        b, i = corner
        j = LANES - 1 if b else 0
        first = (pad + i) // 8 * 8
        return ref[b, first : first + 8, :][(pad + i) % 8 : (pad + i) % 8 + 1, j : j + 1]

    values = [value[0:1, 0:1] for value, _ in sums] + [rest[0:1, 0:1] for _, rest in sums]
    values += [cell(r, corner) for corner in corners]
    values += [cell(q, corner) for corner in corners]
    values += [cell(kx, corner) for corner in corners[2:]]
    for _, i in corners[1::2]:
        part = slice(i // 8 * 8, i // 8 * 8 + 8)
        values.append(right_edges(ky, part, last)[i % 8 : i % 8 + 1, LANES - 1 :])
    lane = lane_ids((1, LANES))
    row = jnp.zeros((1, LANES), F32)
    for place, value in enumerate(values):
        row = jnp.where(lane == place, jnp.broadcast_to(value, (1, LANES)), row)
    table_out[...] = jnp.broadcast_to(row, table_out.shape)


def moments(devices, r, diag, *others):
    blocks, rows = diag.shape[0], diag.shape[1] - PAD
    vmem = pl.BlockSpec(memory_space=pltpu.VMEM)
    cells = blocks * rows * LANES
    return pl.pallas_call(
        moments_kernel,
        out_shape=[
            jax.ShapeDtypeStruct(r.shape, F32),
            jax.ShapeDtypeStruct(r.shape, F32),
            jax.ShapeDtypeStruct((blocks, rows, LANES), F32),
            jax.ShapeDtypeStruct((devices, LANES), F32),
        ],
        in_specs=[vmem] * (2 + len(others)),
        out_specs=[vmem] * 4,
        scratch_shapes=[pltpu.VMEM((rows, LANES), F32)] * 2,
        input_output_aliases={0: 0},
        compiler_params=pltpu.CompilerParams(vmem_limit_bytes=SMALL_VMEM),
        cost_estimate=pl.CostEstimate(flops=40 * cells, bytes_accessed=24 * cells, transcendentals=0),
        name="moments",
    )(r, diag, *others)


def split(a):
    high = a * 4097.0
    high = high - (high - a)
    return high, a - high


def product(a, b):
    p = a * b
    a1, a2 = split(a)
    b1, b2 = split(b)
    return p, ((a1 * b1 - p) + a1 * b2 + a2 * b1) + a2 * b2


def quotient(top, bottom):
    q = top[0] / bottom[0]
    p, error = product(q, bottom[0])
    rest = ((top[0] - p) - error + top[1] - q * bottom[1]) / bottom[0]
    return q, rest


def finish_kernel(
    table_ref, prior, r, q, s, height_hbm, residual_hbm,
    height, residual, coeff, sems,
):
    blocks, rows = s.shape[0], s.shape[1]
    turned = table_ref[...].T
    devices = turned.shape[1]
    field = [turned[i : i + 1, :] for i in range(20)]

    def at(index, down, right):
        shift = -(down * lax.axis_size("col") + right)
        return pltpu.roll(jnp.broadcast_to(field[index], (8, devices)), shift % devices, axis=1)

    r_tl, r_tr, r_bl, r_br = 8, 9, 10, 11
    kx_l, kx_r, ky_t, ky_b = 16, 17, 18, 19
    extra = [
        (at(kx_l, -1, 0) * at(ky_b, -1, -1) + at(ky_t, 0, -1) * at(kx_r, -1, -1)) * at(r_br, -1, -1),
        (at(kx_r, -1, 0) * at(ky_b, -1, 0) + at(ky_t, 0, 0) * at(kx_l, -1, 1)) * at(r_bl, -1, 1),
        (at(kx_l, 0, 0) * at(ky_t, 1, -1) + at(ky_b, 0, -1) * at(kx_r, 0, -1)) * at(r_tr, 1, -1),
        (at(kx_r, 0, 0) * at(ky_t, 1, 0) + at(ky_b, 0, 0) * at(kx_l, 0, 1)) * at(r_tl, 1, 1),
    ]
    rows_of = [(table_ref[8 * n : 8 * n + 8, :], 0.0) for n in range(devices // 8)]
    while len(rows_of) > 1:
        rows_of = [add_pair(a, b) for a, b in zip(rows_of[::2], rows_of[1::2])]
    total, rest = fold(rows_of[0], 0)
    m = [
        (total[0:1, i : i + 1], rest[0:1, i : i + 1] + total[0:1, 4 + i : 5 + i]) for i in range(4)
    ]
    mended = sum(extra[corner] * field[12 + corner] for corner in range(4))
    mended = jnp.sum(mended, axis=1, keepdims=True)[0:1, :]
    m[3] = (m[3][0], m[3][1] + mended)
    x1, x2, x3 = (quotient(m[i + 1], m[i]) for i in range(3))
    gap_1 = (x2[0] - x1[0]) + (x2[1] - x1[1])
    gap_2 = (x3[0] - x2[0]) + (x3[1] - x2[1])
    alpha = 1.0 / x1[0]
    ratio = 1.0 + gap_1 / x1[0]
    alpha_1 = gap_1 / (x2[0] * gap_2)
    place = lax.axis_index("row") * lax.axis_size("col") + lax.axis_index("col")
    mine = lane_ids((8, devices)) == place
    values = [alpha + alpha_1 * ratio, alpha_1 * alpha]
    for corner in range(4):
        own = jnp.sum(jnp.where(mine, extra[corner], 0.0), axis=1, keepdims=True)
        values.append(own[0:1, 0:1])
    for i, value in enumerate(values):
        coeff[i] = jnp.broadcast_to(value, (8, LANES))

    one, two = coeff[0][0:1, 0:1], coeff[1][0:1, 0:1]

    def mend(corner, b, i):
        here = (row_ids((8, LANES)) == i % 8) & (
            lane_ids((8, LANES)) == (LANES - 1 if b else 0)
        )
        residual[b, i // 8 * 8 : i // 8 * 8 + 8, :] += jnp.where(
            here, coeff[1] * coeff[2 + corner], 0.0
        )

    copies = []
    for b in range(blocks):

        def step(i, carry, b=b):
            part = pl.ds(pl.multiple_of(8 * i, 8), 8)
            here = at_row(i)
            x, y = r[b, here, :], q[b, here, :]
            height[b, part, :] = prior[part, b * LANES : (b + 1) * LANES] + (one * x - two * y)
            residual[b, part, :] = x - (one * y - two * s[b, part, :])
            return carry

        lax.fori_loop(0, rows // 8, step, 0, unroll=8)
        if b == 0:
            mend(0, b, 0)
            mend(2, b, rows - 1)
        if b == blocks - 1:
            mend(1, b, 0)
            mend(3, b, rows - 1)
        for which, (source, target) in enumerate(((height, height_hbm), (residual, residual_hbm))):
            copy = pltpu.make_async_copy(
                source.at[b], target.at[:, pl.ds(b * LANES, LANES)], sems.at[which, b]
            )
            copy.start()
            copies.append(copy)
    for copy in copies:
        copy.wait()


def finish(table, prior, r, q, s):
    blocks, rows, _ = s.shape
    cells = rows * blocks * LANES
    vmem = pl.BlockSpec(memory_space=pltpu.VMEM)
    return pl.pallas_call(
        finish_kernel,
        out_shape=[jax.ShapeDtypeStruct((rows, blocks * LANES), F32)] * 2,
        in_specs=[vmem] * 5,
        out_specs=[pl.BlockSpec(memory_space=pltpu.HBM)] * 2,
        scratch_shapes=[
            pltpu.VMEM(s.shape, F32),
            pltpu.VMEM(s.shape, F32),
            pltpu.VMEM((8, 8, LANES), F32),
            pltpu.SemaphoreType.DMA((2, blocks)),
        ],
        compiler_params=pltpu.CompilerParams(vmem_limit_bytes=SMALL_VMEM),
        cost_estimate=pl.CostEstimate(flops=8 * cells, bytes_accessed=24 * cells, transcendentals=0),
        name="finish",
    )(table, prior, r, q, s)


def send(strip, axis, by):
    count = lax.axis_size(axis)
    return lax.ppermute(strip, axis, [(i, (i + by) % count) for i in range(count)])


def exchange(up, down, left, right):
    return (
        send(down, "row", 1), send(up, "row", -1), send(right, "col", 1), send(left, "col", -1),
    )


def shards(
    depth_tiles, conf_tiles, tile_owner, tile_offset, tile_count, prior, edge_rows, edge_cols
):
    row_count, col_count = lax.axis_size("row"), lax.axis_size("col")
    own = strips(prior, edge_rows, edge_cols)
    early = exchange(*own)
    payload = pack(tile_owner, tile_offset, tile_count, depth_tiles[0], conf_tiles[0], col_count)
    arranged = arrange(prior, edge_rows)
    payload, early, arranged = lax.optimization_barrier((payload, early, arranged))
    got = lax.all_to_all(payload, "col", split_axis=0, concat_axis=0, tiled=True)
    r, diag, blocked, kx, weights, pulls, *edges = join(got, *arranged, edge_cols, *early)
    late = exchange(*edges)
    r, diag = fill(weights, pulls, blocked, kx, edge_cols, r, diag)
    r, q, s, table = moments(
        row_count * col_count, r, diag, kx, edge_cols, *late, early[2], edges[2], edges[3], own[3]
    )
    table = lax.all_to_all(table, ("row", "col"), split_axis=0, concat_axis=0, tiled=True)
    return tuple(finish(table, prior, r, q, s))


def solution(mesh):
    return jax.shard_map(
        shards,
        mesh=mesh,
        in_specs=(
            P("row", "col", None),
            P("row", "col", None),
            P("row", "col"),
            P("row", "col"),
            P("row", "col"),
            P("row", "col"),
            P("row", "col"),
            P("row", "col"),
        ),
        out_specs=(P("row", "col"), P("row", "col")),
        check_vma=False,
    )
```

```python
import jax
import jax.numpy as jnp
from jax import lax
from jax.experimental import pallas as pl
from jax.experimental.pallas import tpu as pltpu
from jax.sharding import PartitionSpec as P

TS = 32
GROUPS = 8
LAM = 0.05
HUBER = 0.5
META = 16
LANES = 128
PAD = 8
F32 = jnp.float32
SMALL_VMEM = 16 * 1024 * 1024


def is_last(axis):
    return lax.axis_index(axis) == lax.axis_size(axis) - 1


def lane_ids(shape):
    return lax.broadcasted_iota(jnp.int32, shape, len(shape) - 1)


def row_ids(shape):
    return lax.broadcasted_iota(jnp.int32, shape, len(shape) - 2)


def cols_up(parts, after):
    rolled = [pltpu.roll(x, LANES - 1, axis=1) for x in parts] + [after]
    last = lane_ids(parts[0].shape) == LANES - 1
    return [jnp.where(last, rolled[b + 1], rolled[b]) for b in range(len(parts))]


def cols_down(parts, before):
    rolled = [before] + [pltpu.roll(x, 1, axis=1) for x in parts]
    first = lane_ids(parts[0].shape) == 0
    return [jnp.where(first, rolled[b], rolled[b + 1]) for b in range(len(parts))]


def side_columns(first, last):
    shape = (LANES, first.shape[1])
    rows = row_ids(shape)
    return jnp.where(rows == 0, first, jnp.where(rows == LANES - 1, last, 0.0)).T


def right_edges(ky, part, b):
    edges = ky[part, b * LANES : (b + 1) * LANES]
    if (b + 1) * LANES < ky.shape[1]:
        return edges
    return jnp.where(is_last("col") & (lane_ids(edges.shape) == LANES - 1), 0.0, edges)


def at_row(i, shift=0):
    if shift:
        return pl.ds(PAD + 8 * i + shift, 8)
    return pl.ds(pl.multiple_of(PAD + 8 * i, 8), 8)


def swap_blocks(four):
    lane = lane_ids(four[0].shape)
    low_half = lane < 64
    even = (lane & 32) == 0
    half = [None] * 4
    for q in range(2):
        a, b = four[q], four[q + 2]
        half[q] = jnp.where(low_half, a, pltpu.roll(b, 64, axis=1))
        half[q + 2] = jnp.where(low_half, pltpu.roll(a, 64, axis=1), b)
    out = [None] * 4
    for q in (0, 2):
        a, b = half[q], half[q + 1]
        out[q] = jnp.where(even, a, pltpu.roll(b, 32, axis=1))
        out[q + 1] = jnp.where(even, pltpu.roll(a, 96, axis=1), b)
    return out


def pack_kernel(owner_ref, count_ref, offset_ref, depth, conf, out, scratch):
    slots = out.shape[0]
    run = depth.shape[0] // GROUPS
    chunks = depth.shape[1] // LANES
    cells = run * chunks
    blank = jnp.zeros((META, LANES), jnp.bfloat16)
    for s in range(slots):
        out[s, 2 * cells :, :] = blank
    rows = row_ids((META, LANES))
    count = count_ref[0, 0]
    for pair in range(GROUPS // 2):
        offsets = jnp.broadcast_to(offset_ref[:, pair * LANES : (pair + 1) * LANES], (META, LANES))
        high = (offsets >> 4).astype(F32)
        low = (offsets & 15).astype(F32)
        for side in range(2):
            g = 2 * pair + side
            if side:
                high, low = pltpu.roll(high, run, axis=1), pltpu.roll(low, run, axis=1)
            live = jnp.clip(count - g * run, 0, run).astype(F32)
            meta = jnp.where(rows == 0, high, jnp.where(rows == 1, low, jnp.where(rows == 2, live, 0.0)))
            out[owner_ref[0, g * run], 2 * cells :, :] = meta.astype(jnp.bfloat16)

    def one_run(g, carry):
        slot = owner_ref[0, g * run]
        for which, source in enumerate((depth, conf)):
            for m in range(run // 16):
                buffer = scratch.at[which * (run // 16) + m]
                block = source[pl.ds(pl.multiple_of(g * run + 16 * m, 16), 16), :].astype(F32)
                if which:
                    tile = row_ids(block.shape) + (g * run + 16 * m)
                    block = jnp.where(tile < count, block * HUBER, 0.0)
                for c in range(chunks):
                    buffer[pl.ds(c, 16, stride=chunks), :] = block[:, c * LANES : (c + 1) * LANES]
                first = which * cells + m * 16 * chunks
                out[slot, first : first + 16 * chunks, :] = buffer[: 16 * chunks, :].astype(jnp.bfloat16)
        return carry

    lax.fori_loop(0, GROUPS, one_run, 0, unroll=2)


def pack(owners, offsets, count, depth, conf, slots):
    tiles, cells = depth.shape
    run = tiles // GROUPS
    rows = 2 * run * (cells // LANES) + META
    vmem = pl.BlockSpec(memory_space=pltpu.VMEM)
    smem = pl.BlockSpec(memory_space=pltpu.SMEM)
    return pl.pallas_call(
        pack_kernel,
        out_shape=jax.ShapeDtypeStruct((slots, rows, LANES), jnp.bfloat16),
        in_specs=[smem, smem, vmem, vmem, vmem],
        out_specs=vmem,
        scratch_shapes=[pltpu.VMEM((2 * run // 16, 16 * (cells // LANES) + PAD, LANES), F32)],
        compiler_params=pltpu.CompilerParams(vmem_limit_bytes=SMALL_VMEM),
        cost_estimate=pl.CostEstimate(flops=1 << 20, bytes_accessed=4 << 20, transcendentals=0),
        name="pack",
    )(owners, count, offsets, depth, conf)


def strips_kernel(
    top, bottom, kx_bottom, left, right, ky_right, up_out, down_out, left_out, right_out
):
    up_out[...] = top[0:1, :]
    down_out[0:1, :] = bottom[7:8, :]
    down_out[1:2, :] = jnp.where(is_last("row"), 0.0, kx_bottom[7:8, :])
    lane = lane_ids(left.shape)
    both = jnp.where(lane == LANES - 1, right[...], pltpu.roll(ky_right[...], LANES - 1, axis=1))
    turned = jnp.where(lane == 0, left[...], both).T
    left_out[...] = turned[0:1, :]
    right_out[0:1, :] = turned[LANES - 1 : LANES, :]
    right_out[1:2, :] = jnp.where(is_last("col"), 0.0, turned[LANES - 2 : LANES - 1, :])


def strips(prior, kx, ky):
    rows, cols = prior.shape
    last_rows = pl.BlockSpec((8, cols), lambda i: (rows // 8 - 1, 0))
    last_cols = pl.BlockSpec((rows, LANES), lambda i: (0, cols // LANES - 1))
    whole = lambda shape: pl.BlockSpec(shape, lambda i: (0, 0))
    shapes = ((1, cols), (2, cols), (1, rows), (2, rows))
    return pl.pallas_call(
        strips_kernel,
        grid=(1,),
        out_shape=[jax.ShapeDtypeStruct(s, F32) for s in shapes],
        in_specs=[
            whole((8, cols)), last_rows, last_rows, whole((rows, LANES)), last_cols, last_cols,
        ],
        out_specs=[pl.BlockSpec(memory_space=pltpu.VMEM)] * 4,
        name="strips",
    )(prior, prior, kx, prior, prior, ky)


def arrange_kernel(prior_in, kx_in, tiles, prior, kx):
    rows, cols = prior_in.shape
    blocks = cols // LANES

    def one_strip(strip, carry):
        base = pl.multiple_of(TS * strip, TS)
        here = pl.ds(base, TS)
        padded = pl.ds(pl.multiple_of(PAD + base, 8), TS)
        for b in range(blocks):
            lanes = slice(b * LANES, (b + 1) * LANES)
            prior[b, padded, :] = prior_in[here, lanes]
            kx[b, padded, :] = kx_in[here, lanes]
        for b in range(blocks):
            four = swap_blocks([prior[b, grid_rows(PAD, strip, a), :] for a in range(4)])
            for place, part in zip(tiles_of(strip, b, blocks), four):
                tiles[place] = part
        return carry

    lax.fori_loop(0, rows // TS, one_strip, 0, unroll=2)

    @pl.when(is_last("row"))
    def _():
        for b in range(blocks):
            kx[b, PAD + rows - 1 : PAD + rows, :] = jnp.zeros((1, LANES), F32)


def arrange(prior, kx):
    rows, cols = prior.shape
    blocks = cols // LANES
    vmem = pl.BlockSpec(memory_space=pltpu.VMEM)
    padded = (blocks, rows + 2 * PAD, LANES)
    shapes = ((rows * cols // (8 * LANES), 8, LANES), padded, padded)
    return pl.pallas_call(
        arrange_kernel,
        out_shape=[jax.ShapeDtypeStruct(s, F32) for s in shapes],
        in_specs=[vmem] * 2,
        out_specs=[vmem] * 3,
        compiler_params=pltpu.CompilerParams(vmem_limit_bytes=SMALL_VMEM),
        cost_estimate=pl.CostEstimate(flops=1 << 22, bytes_accessed=14 << 20, transcendentals=0),
        name="arrange",
    )(prior, kx)


BATCH = 32
UF = 64
UO = 32
US = 64
UM = 64


def tiles_of(strip, b, blocks):
    first = strip * (blocks * LANES // TS) + 4 * b
    return [first + q for q in range(4)]


def grid_rows(pad, strip, a):
    return pl.ds(pad + TS * strip + a, 8, stride=4)


def to_grid(weights, pulls, diag, r, strip, chosen):
    for b in chosen:
        places = tiles_of(strip, b, diag.shape[0])
        for total, out, pad in ((weights, diag, 0), (pulls, r, PAD)):
            for a, part in enumerate(swap_blocks([total[place] for place in places])):
                out[b, grid_rows(pad, strip, a), :] = part


def add_flows(r, diag, prior, kx, ky, side_p, left_k, i, chosen):
    last = diag.shape[0] - 1
    here, above, below = at_row(i), at_row(i, -1), at_row(i, 1)
    part = pl.ds(pl.multiple_of(8 * i, 8), 8)
    near = sorted({n for b in chosen for n in (b - 1, b, b + 1) if 0 <= n <= last})
    p = {b: prior[b, here, :] for b in near}
    h = {b: right_edges(ky, part, b) for b in near}
    lane = lane_ids((8, LANES))
    up = {b: pltpu.roll(p[b], LANES - 1, axis=1) for b in near}
    down = {b: pltpu.roll(p[b], 1, axis=1) for b in near}
    h_down = {b: pltpu.roll(h[b], 1, axis=1) for b in near}
    for b in chosen:
        p_right = jnp.where(lane == LANES - 1, up[b + 1] if b < last else side_p[part, :], up[b])
        p_left = jnp.where(lane == 0, down[b - 1] if b else side_p[part, :], down[b])
        h_left = jnp.where(lane == 0, h_down[b - 1] if b else left_k[part, :], h_down[b])
        k, k_up = kx[b, here, :], kx[b, above, :]
        down_flow = k * (prior[b, below, :] - p[b])
        up_flow = k_up * (p[b] - prior[b, above, :])
        side_flow = h[b] * (p_right - p[b]) - h_left * (p[b] - p_left)
        r[b, here, :] += (down_flow - up_flow) + side_flow
        diag[b, part, :] += LAM + (k + k_up) + (h[b] + h_left)


def join_kernel(
    got, tiles, prior_in, kx_in, ky, from_up, from_down, from_left, from_right,
    r_out, diag_out, prior, kx, weights, pulls, up_out, down_out, left_out, right_out,
    table_v, table, side_p, left_k, table_sem,
):
    slots, rows_in = got.shape[0], got.shape[1]
    cells = (rows_in - META) // 2
    blocks, rows = diag_out.shape[0], diag_out.shape[1] - PAD
    steps = rows // 8
    for s in range(slots):
        fields = got[s, 2 * cells :, :].astype(F32)
        target = jnp.broadcast_to(fields[0:1, :] * 16.0 + fields[1:2, :], (8, LANES))
        target = target + 1024.0 * pltpu.roll(target, LANES - 1, axis=1)
        table_v[s, 0:1, :] = target[0:1, :].astype(jnp.int32)
        table_v[s, 1:2, :] = fields[2:3, :].astype(jnp.int32)
    table_copy = pltpu.make_async_copy(table_v, table, table_sem)
    table_copy.start()

    zero = jnp.zeros((8, LANES), F32)

    def clear(i, carry):
        weights[i] = zero
        pulls[i] = zero
        return carry

    lax.fori_loop(0, tiles.shape[0], clear, 0, unroll=8)
    side_p[...] = side_columns(from_left[0:1, :], from_right[...])
    left_k[...] = side_columns(from_left[1:2, :], from_left[1:2, :])
    for b in range(blocks):
        lanes = slice(b * LANES, (b + 1) * LANES)
        prior[b, PAD - 1 : PAD, :] = from_up[0:1, lanes]
        kx[b, PAD - 1 : PAD, :] = from_up[1:2, lanes]
        prior[b, PAD + rows : PAD + rows + 1, :] = from_down[0:1, lanes]
        r_out[b, PAD - 1 : PAD, :] = jnp.zeros((1, LANES), F32)
        r_out[b, PAD + rows : PAD + rows + 1, :] = jnp.zeros((1, LANES), F32)
    table_copy.wait()

    def one_slot(slot, carry):
        live = table[slot, 1, 0]

        def batch(step, carry):
            first = step * BATCH
            places, terms = [], []
            for pair in range(BATCH // 2):
                at = pl.multiple_of((first + 2 * pair) * 8, 16)
                depths = got[slot, pl.ds(at, 16), :].astype(F32)
                confs = got[slot, pl.ds(cells + at, 16), :].astype(F32)
                word = table[slot, 0, first + 2 * pair]
                for side in range(2):
                    place = word >> 10 if side else word & 1023
                    error = depths[8 * side : 8 * side + 8] - tiles[place]
                    weight = confs[8 * side : 8 * side + 8] / jnp.maximum(jnp.abs(error), HUBER)
                    places.append(place)
                    terms.append((weight, weight * error))
            for place, (weight, pull) in zip(places, terms):
                weights[place] += weight
                pulls[place] += pull
            return carry

        return lax.fori_loop(0, (live + BATCH - 1) // BATCH, batch, carry)

    lax.fori_loop(0, slots, one_slot, 0)
    last = blocks - 1

    def outer(four, carry):
        for n in range(4):
            to_grid(weights, pulls, diag_out, r_out, 4 * four + n, (0, last))
        return carry

    def ends(n, carry):
        to_grid(weights, pulls, diag_out, r_out, n * (rows // TS - 1), range(1, last))
        return carry

    lax.fori_loop(0, rows // TS // 4, outer, 0)
    lax.fori_loop(0, 2, ends, 0)

    def outer_flows(i, carry):
        add_flows(r_out, diag_out, prior, kx, ky, side_p, left_k, i, (0, last))
        return carry

    def end_flows(n, carry):
        i = n * (steps - 1)
        add_flows(r_out, diag_out, prior, kx, ky, side_p, left_k, i, range(1, last))
        return carry

    lax.fori_loop(0, steps, outer_flows, 0, unroll=UO)
    lax.fori_loop(0, 2, end_flows, 0)

    zeros = jnp.zeros((8, LANES), F32)
    for i, out, row in ((0, up_out, 0), (steps - 1, down_out, 7)):
        image = operate(r_out, diag_out, kx, ky, i, zeros, zeros)
        for b in range(blocks):
            lanes = slice(b * LANES, (b + 1) * LANES)
            out[0:1, lanes] = r_out[b, at_row(i), :][row : row + 1, :]
            out[1:2, lanes] = image[b][row : row + 1, :]
    lane = lane_ids((8, LANES))

    def sides(i, carry):
        here = at_row(i)
        part = pl.ds(pl.multiple_of(8 * i, 8), 8)
        edges = []
        for b, edge, sign in ((0, 0, 1), (blocks - 1, LANES - 1, -1)):
            field = r_out[b, here, :]
            if edge:
                across = pltpu.roll(right_edges(ky, part, b) * field, 1, axis=1)
            else:
                across = right_edges(ky, part, b) * pltpu.roll(field, LANES - 1, axis=1)
            image = diag_out[b, part, :] * field - across - vertical(r_out, kx, b, i)
            edges.append(
                jnp.where(lane == edge, image, pltpu.roll(field, sign % LANES, axis=1))
            )
        side_p[part, :] = jnp.where(lane < LANES // 2, edges[0], edges[1])
        return carry

    lax.fori_loop(0, steps, sides, 0, unroll=US)
    turned = side_p[...].T
    left_out[0:1, :] = turned[1:2, :]
    left_out[1:2, :] = turned[0:1, :]
    right_out[...] = turned[LANES - 2 :, :]


def join(got, tiles, prior, kx, ky, from_up, from_down, from_left, from_right):
    rows, cols = ky.shape
    blocks = cols // LANES
    slots = got.shape[0]
    vmem = pl.BlockSpec(memory_space=pltpu.VMEM)
    strip_shapes = ((2, cols), (2, cols), (2, rows), (2, rows))
    shapes = (prior.shape, (blocks, rows + PAD, LANES), prior.shape, kx.shape, tiles.shape, tiles.shape) + strip_shapes
    cells = rows * cols
    return pl.pallas_call(
        join_kernel,
        out_shape=[jax.ShapeDtypeStruct(s, F32) for s in shapes],
        in_specs=[vmem] * 9,
        out_specs=[vmem] * len(shapes),
        scratch_shapes=[
            pltpu.VMEM((slots, 8, LANES), jnp.int32),
            pltpu.SMEM((slots, 8, LANES), jnp.int32),
            pltpu.VMEM((rows, LANES), F32),
            pltpu.VMEM((rows, LANES), F32),
            pltpu.SemaphoreType.DMA,
        ],
        input_output_aliases={2: 2, 3: 3},
        compiler_params=pltpu.CompilerParams(vmem_limit_bytes=SMALL_VMEM),
        cost_estimate=pl.CostEstimate(flops=30 * cells, bytes_accessed=24 * cells, transcendentals=0),
        name="join",
    )(got, tiles, prior, kx, ky, from_up, from_down, from_left, from_right)


def fill_kernel(weights, pulls, prior, kx, ky, r_in, diag_in, r, diag):
    blocks, rows = diag.shape[0], diag.shape[1] - PAD
    inner = range(1, blocks - 1)

    def grid_step(strip, carry):
        to_grid(weights, pulls, diag, r, strip, inner)
        return carry

    def flow_step(i, carry):
        add_flows(r, diag, prior, kx, ky, None, None, i, inner)
        return carry

    lax.fori_loop(0, rows // TS, grid_step, 0)
    lax.fori_loop(0, rows // 8, flow_step, 0, unroll=UF)


def fill(weights, pulls, prior, kx, ky, r, diag):
    vmem = pl.BlockSpec(memory_space=pltpu.VMEM)
    return pl.pallas_call(
        fill_kernel,
        out_shape=[jax.ShapeDtypeStruct(x.shape, F32) for x in (r, diag)],
        in_specs=[vmem] * 7,
        out_specs=[vmem] * 2,
        input_output_aliases={5: 0, 6: 1},
        compiler_params=pltpu.CompilerParams(vmem_limit_bytes=SMALL_VMEM),
        cost_estimate=pl.CostEstimate(flops=1 << 25, bytes_accessed=16 << 20, transcendentals=0),
        name="fill",
    )(weights, pulls, prior, kx, ky, r, diag)


def vertical(field, kx, b, i):
    here, above, below = at_row(i), at_row(i, -1), at_row(i, 1)
    return kx[b, here, :] * field[b, below, :] + kx[b, above, :] * field[b, above, :]


def operate(field, diag, kx, ky, i, entering, after):
    blocks = diag.shape[0]
    part = pl.ds(8 * i, 8) if isinstance(i, int) else pl.ds(pl.multiple_of(8 * i, 8), 8)
    x = [field[b, at_row(i), :] for b in range(blocks)]
    h = [right_edges(ky, part, b) for b in range(blocks)]
    right = cols_up(x, after)
    left = cols_down([h[b] * x[b] for b in range(blocks)], entering)
    return [
        (diag[b, part, :] * x[b] - vertical(field, kx, b, i)) - (h[b] * right[b] + left[b])
        for b in range(blocks)
    ]


def add_pair(total, other):
    (a, rest_a), (b, rest_b) = total, other
    s = a + b
    back = s - a
    error = (a - (s - back)) + (b - back)
    return s, rest_a + rest_b + error


def fold(pair, axis):
    size = pair[0].shape[axis] // 2
    while size:
        other = tuple(pltpu.roll(part, size, axis=axis) for part in pair)
        pair = add_pair(pair, other)
        size //= 2
    return pair


def moments_kernel(
    r_in, diag, kx, ky, r_up, r_down, r_left, r_right, k_left, own_left, own_right, own_ky,
    r, q, s, table_out, side_r, side_q,
):
    blocks, rows, _ = s.shape
    steps = rows // 8
    last = blocks - 1
    k = k_left[1:2, :]
    side_r[...] = side_columns(k * r_left[0:1, :], r_right[0:1, :])
    side_q[...] = side_columns(
        k * (r_left[1:2, :] - k * own_left[0:1, :]),
        r_right[1:2, :] - own_ky[1:2, :] * own_right[0:1, :],
    )
    top, low = slice(PAD - 1, PAD), slice(PAD + rows, PAD + rows + 1)
    for b in range(blocks):
        lanes = slice(b * LANES, (b + 1) * LANES)
        r[b, top, :] = r_up[0:1, lanes]
        r[b, low, :] = r_down[0:1, lanes]
        q[b, top, :] = r_up[1:2, lanes] - kx[b, top, :] * r[b, PAD : PAD + 1, :]
        final = slice(PAD + rows - 1, PAD + rows)
        q[b, low, :] = r_down[1:2, lanes] - kx[b, final, :] * r[b, final, :]

    def folded(parts):
        while len(parts) > 1:
            parts = [a + b for a, b in zip(parts[::2], parts[1::2])]
        return parts[0]

    def products(left, right):
        return folded([a * b for a, b in zip(left, right)])

    def first(i, carry):
        m0, m1, m2 = carry
        part = pl.ds(pl.multiple_of(8 * i, 8), 8)
        image = operate(r, diag, kx, ky, i, side_r[part, :], side_r[part, :])
        field = [r[b, at_row(i), :] for b in range(blocks)]
        for b in range(blocks):
            q[b, at_row(i), :] = image[b]
        return (
            m0 + products(field, field), m1 + products(field, image), m2 + products(image, image),
        )

    zero = jnp.zeros((8, LANES), F32)
    m0, m1, m2 = lax.fori_loop(0, steps, first, (zero, zero, zero), unroll=UM)

    def second(i, m3):
        part = pl.ds(pl.multiple_of(8 * i, 8), 8)
        image = operate(q, diag, kx, ky, i, side_q[part, :], side_q[part, :])
        for b in range(blocks):
            s[b, part, :] = image[b]
        return m3 + products([q[b, at_row(i), :] for b in range(blocks)], image)

    m3 = lax.fori_loop(0, steps, second, zero, unroll=UM)

    sums = []
    for m in (m0, m1, m2, m3):
        sums.append(fold(fold((m, jnp.zeros_like(m)), 0), 1))
    corners = ((0, 0), (last, 0), (0, rows - 1), (last, rows - 1))

    def cell(ref, corner, pad=PAD):
        b, i = corner
        j = LANES - 1 if b else 0
        first = (pad + i) // 8 * 8
        return ref[b, first : first + 8, :][(pad + i) % 8 : (pad + i) % 8 + 1, j : j + 1]

    values = [value[0:1, 0:1] for value, _ in sums] + [rest[0:1, 0:1] for _, rest in sums]
    values += [cell(r, corner) for corner in corners]
    values += [cell(q, corner) for corner in corners]
    values += [cell(kx, corner) for corner in corners[2:]]
    for _, i in corners[1::2]:
        part = slice(i // 8 * 8, i // 8 * 8 + 8)
        values.append(right_edges(ky, part, last)[i % 8 : i % 8 + 1, LANES - 1 :])
    lane = lane_ids((1, LANES))
    row = jnp.zeros((1, LANES), F32)
    for place, value in enumerate(values):
        row = jnp.where(lane == place, jnp.broadcast_to(value, (1, LANES)), row)
    table_out[...] = jnp.broadcast_to(row, table_out.shape)


def moments(devices, r, diag, *others):
    blocks, rows = diag.shape[0], diag.shape[1] - PAD
    vmem = pl.BlockSpec(memory_space=pltpu.VMEM)
    cells = blocks * rows * LANES
    return pl.pallas_call(
        moments_kernel,
        out_shape=[
            jax.ShapeDtypeStruct(r.shape, F32),
            jax.ShapeDtypeStruct(r.shape, F32),
            jax.ShapeDtypeStruct((blocks, rows, LANES), F32),
            jax.ShapeDtypeStruct((devices, LANES), F32),
        ],
        in_specs=[vmem] * (2 + len(others)),
        out_specs=[vmem] * 4,
        scratch_shapes=[pltpu.VMEM((rows, LANES), F32)] * 2,
        input_output_aliases={0: 0},
        compiler_params=pltpu.CompilerParams(vmem_limit_bytes=SMALL_VMEM),
        cost_estimate=pl.CostEstimate(flops=40 * cells, bytes_accessed=24 * cells, transcendentals=0),
        name="moments",
    )(r, diag, *others)


def split(a):
    high = a * 4097.0
    high = high - (high - a)
    return high, a - high


def product(a, b):
    p = a * b
    a1, a2 = split(a)
    b1, b2 = split(b)
    return p, ((a1 * b1 - p) + a1 * b2 + a2 * b1) + a2 * b2


def quotient(top, bottom):
    q = top[0] / bottom[0]
    p, error = product(q, bottom[0])
    rest = ((top[0] - p) - error + top[1] - q * bottom[1]) / bottom[0]
    return q, rest


def finish_kernel(
    table_ref, prior, r, q, s, height_hbm, residual_hbm,
    height, residual, coeff, sems,
):
    blocks, rows = s.shape[0], s.shape[1]
    turned = table_ref[...].T
    devices = turned.shape[1]
    field = [turned[i : i + 1, :] for i in range(20)]

    def at(index, down, right):
        shift = -(down * lax.axis_size("col") + right)
        return pltpu.roll(jnp.broadcast_to(field[index], (8, devices)), shift % devices, axis=1)

    r_tl, r_tr, r_bl, r_br = 8, 9, 10, 11
    kx_l, kx_r, ky_t, ky_b = 16, 17, 18, 19
    extra = [
        (at(kx_l, -1, 0) * at(ky_b, -1, -1) + at(ky_t, 0, -1) * at(kx_r, -1, -1)) * at(r_br, -1, -1),
        (at(kx_r, -1, 0) * at(ky_b, -1, 0) + at(ky_t, 0, 0) * at(kx_l, -1, 1)) * at(r_bl, -1, 1),
        (at(kx_l, 0, 0) * at(ky_t, 1, -1) + at(ky_b, 0, -1) * at(kx_r, 0, -1)) * at(r_tr, 1, -1),
        (at(kx_r, 0, 0) * at(ky_t, 1, 0) + at(ky_b, 0, 0) * at(kx_l, 0, 1)) * at(r_tl, 1, 1),
    ]
    rows_of = [(table_ref[8 * n : 8 * n + 8, :], 0.0) for n in range(devices // 8)]
    while len(rows_of) > 1:
        rows_of = [add_pair(a, b) for a, b in zip(rows_of[::2], rows_of[1::2])]
    total, rest = fold(rows_of[0], 0)
    m = [
        (total[0:1, i : i + 1], rest[0:1, i : i + 1] + total[0:1, 4 + i : 5 + i]) for i in range(4)
    ]
    mended = sum(extra[corner] * field[12 + corner] for corner in range(4))
    mended = jnp.sum(mended, axis=1, keepdims=True)[0:1, :]
    m[3] = (m[3][0], m[3][1] + mended)
    x1, x2, x3 = (quotient(m[i + 1], m[i]) for i in range(3))
    gap_1 = (x2[0] - x1[0]) + (x2[1] - x1[1])
    gap_2 = (x3[0] - x2[0]) + (x3[1] - x2[1])
    alpha = 1.0 / x1[0]
    ratio = 1.0 + gap_1 / x1[0]
    alpha_1 = gap_1 / (x2[0] * gap_2)
    place = lax.axis_index("row") * lax.axis_size("col") + lax.axis_index("col")
    mine = lane_ids((8, devices)) == place
    values = [alpha + alpha_1 * ratio, alpha_1 * alpha]
    for corner in range(4):
        own = jnp.sum(jnp.where(mine, extra[corner], 0.0), axis=1, keepdims=True)
        values.append(own[0:1, 0:1])
    for i, value in enumerate(values):
        coeff[i] = jnp.broadcast_to(value, (8, LANES))

    one, two = coeff[0][0:1, 0:1], coeff[1][0:1, 0:1]

    def mend(corner, b, i):
        here = (row_ids((8, LANES)) == i % 8) & (
            lane_ids((8, LANES)) == (LANES - 1 if b else 0)
        )
        residual[b, i // 8 * 8 : i // 8 * 8 + 8, :] += jnp.where(
            here, coeff[1] * coeff[2 + corner], 0.0
        )

    copies = []
    for b in range(blocks):

        def step(i, carry, b=b):
            part = pl.ds(pl.multiple_of(8 * i, 8), 8)
            here = at_row(i)
            x, y = r[b, here, :], q[b, here, :]
            height[b, part, :] = prior[part, b * LANES : (b + 1) * LANES] + (one * x - two * y)
            residual[b, part, :] = x - (one * y - two * s[b, part, :])
            return carry

        lax.fori_loop(0, rows // 8, step, 0, unroll=16)
        if b == 0:
            mend(0, b, 0)
            mend(2, b, rows - 1)
        if b == blocks - 1:
            mend(1, b, 0)
            mend(3, b, rows - 1)
        for which, (source, target) in enumerate(((height, height_hbm), (residual, residual_hbm))):
            copy = pltpu.make_async_copy(
                source.at[b], target.at[:, pl.ds(b * LANES, LANES)], sems.at[which, b]
            )
            copy.start()
            copies.append(copy)
    for copy in copies:
        copy.wait()


def finish(table, prior, r, q, s):
    blocks, rows, _ = s.shape
    cells = rows * blocks * LANES
    vmem = pl.BlockSpec(memory_space=pltpu.VMEM)
    return pl.pallas_call(
        finish_kernel,
        out_shape=[jax.ShapeDtypeStruct((rows, blocks * LANES), F32)] * 2,
        in_specs=[vmem] * 5,
        out_specs=[pl.BlockSpec(memory_space=pltpu.HBM)] * 2,
        scratch_shapes=[
            pltpu.VMEM(s.shape, F32),
            pltpu.VMEM(s.shape, F32),
            pltpu.VMEM((8, 8, LANES), F32),
            pltpu.SemaphoreType.DMA((2, blocks)),
        ],
        compiler_params=pltpu.CompilerParams(vmem_limit_bytes=SMALL_VMEM),
        cost_estimate=pl.CostEstimate(flops=8 * cells, bytes_accessed=24 * cells, transcendentals=0),
        name="finish",
    )(table, prior, r, q, s)


def send(strip, axis, by):
    count = lax.axis_size(axis)
    return lax.ppermute(strip, axis, [(i, (i + by) % count) for i in range(count)])


def exchange(up, down, left, right):
    return (
        send(down, "row", 1), send(up, "row", -1), send(right, "col", 1), send(left, "col", -1),
    )


def shards(
    depth_tiles, conf_tiles, tile_owner, tile_offset, tile_count, prior, edge_rows, edge_cols
):
    row_count, col_count = lax.axis_size("row"), lax.axis_size("col")
    own = strips(prior, edge_rows, edge_cols)
    early = exchange(*own)
    payload = pack(tile_owner, tile_offset, tile_count, depth_tiles[0], conf_tiles[0], col_count)
    arranged = arrange(prior, edge_rows)
    payload, early, arranged = lax.optimization_barrier((payload, early, arranged))
    got = lax.all_to_all(payload, "col", split_axis=0, concat_axis=0, tiled=True)
    r, diag, blocked, kx, weights, pulls, *edges = join(got, *arranged, edge_cols, *early)
    late = exchange(*edges)
    r, diag = fill(weights, pulls, blocked, kx, edge_cols, r, diag)
    r, q, s, table = moments(
        row_count * col_count, r, diag, kx, edge_cols, *late, early[2], edges[2], edges[3], own[3]
    )
    table = lax.all_to_all(table, ("row", "col"), split_axis=0, concat_axis=0, tiled=True)
    return tuple(finish(table, prior, r, q, s))


def solution(mesh):
    return jax.shard_map(
        shards,
        mesh=mesh,
        in_specs=(
            P("row", "col", None),
            P("row", "col", None),
            P("row", "col"),
            P("row", "col"),
            P("row", "col"),
            P("row", "col"),
            P("row", "col"),
            P("row", "col"),
        ),
        out_specs=(P("row", "col"), P("row", "col")),
        check_vma=False,
    )
```
